32 devices in a mesh: dp: 2 (over core), expert: 16 (over z, y, x).
Axes of the slice: x: 2, y: 2, z: 4, core: 2. Of those that a mesh axis runs over, the one named last changes fastest.
Arguments:
- tokens: bfloat16 [32, 256, 2048], P(('dp', 'expert')), may hold values from -6 to 6
- w_qkv: bfloat16 [2048, 6144], P(('dp', 'expert')), may hold values from -0.125 to 0.125
- w_out: bfloat16 [2048, 2048], P(('dp', 'expert')), may hold values from -0.75 to 0.75
- w_router: bfloat16 [2048, 16], P(('dp', 'expert')), may hold values from -0.0625 to 0.0625
- gains: bfloat16 [4, 2048], P(None, ('dp', 'expert')), may hold values from 0.099609375 to 1.8984375
- w_gate: bfloat16 [16, 2048, 1024], P('expert', None, 'dp'), may hold values from -0.125 to 0.125
- w_up: bfloat16 [16, 2048, 1024], P('expert', None, 'dp'), may hold values from -0.125 to 0.125
- w_down: bfloat16 [16, 1024, 2048], P('expert', 'dp'), may hold values from -4 to 4
- lengths: int32 [32], P(('dp', 'expert')), may hold values from 64 to 256, as said below
- routes: int32 [32, 256, 8], P(('dp', 'expert')), may hold values from 0 to 15, as said below
- send_counts: int32 [32, 16], P(('dp', 'expert')), may hold values from 0 to 128, as said below
- cotangent: bfloat16 [32, 256, 2048], P(('dp', 'expert')), may hold values from -6 to 6
Outputs:
- result: bfloat16 [32, 256, 2048], P(('dp', 'expert'))
- grad_tokens: float32 [32, 256, 2048], P(('dp', 'expert'))
- grad_qkv: float32 [2048, 6144], P(('dp', 'expert'))
- grad_out: float32 [2048, 2048], P(('dp', 'expert'))
- grad_router: float32 [2048, 16], P(('dp', 'expert'))
- grad_gains: float32 [4, 2048], P(None, ('dp', 'expert'))
- grad_gate: float32 [16, 2048, 1024], P('expert', None, 'dp')
- grad_up: float32 [16, 2048, 1024], P('expert', None, 'dp')
- grad_down: float32 [16, 1024, 2048], P('expert', 'dp')
- balance: float32 [], replicated
The draws below stay inside these ranges and needn't reach their ends.
Inputs may be any that keep to these rules, and one draw needn't show every extreme that they name: Row r holds one sequence in its first lengths[r] slots; the rest are padding; at least one row is full. Each slot names 8 different experts; the routes of padded slots are not used. send_counts[r, e] is the number of live slots of row r that name expert e; one expert is named by exactly min(128, lengths[r]) live slots of every row r.
All inputs are finite; a program needn't handle non-finite values.
Results may differ from the reference program's by a relative error of at most 0.02.
Values may be sent and summed in bfloat16 or wider, within the bound.
A program may use at most 384 MiB of HBM per device.

```python
import math
import jax
import jax.numpy as jnp
from jax import lax

D = 2048
HEADS = 16
HEAD = 128
FF = 1024
TOP = 8
EXPERTS = 16
ROW = 256
ROWS = 32
SLOTS = 8192
CAP = 128


def row_plan(row_key, length, hot_expert):
    perm_key, delta_key, order_key = jax.random.split(row_key, 3)
    others_count = EXPERTS - 1
    heaviest = jnp.minimum(CAP, length)
    rest = length * TOP - heaviest
    base_load = rest // others_count
    extra = rest % others_count
    other_slots = jnp.arange(others_count, dtype=jnp.int32)
    loads = base_load + (other_slots < extra).astype(jnp.int32)
    spread_max = jnp.maximum(0, jnp.minimum(base_load, heaviest - base_load - 1))
    shifts = jax.random.randint(delta_key, (others_count,), 0, 1 << 16) % (spread_max + 1)
    leader = other_slots // 2 * 2
    pair_shift = shifts[leader]
    has_partner = leader + 1 < others_count
    signed_shift = jnp.where(other_slots % 2 == 0, pair_shift, -pair_shift)
    loads = loads + jnp.where(has_partner, signed_shift, 0)
    others = (hot_expert + 1 + jax.random.permutation(perm_key, others_count).astype(jnp.int32)) % EXPERTS
    sequence_ids = jnp.concatenate([hot_expert[None], others]).astype(jnp.int32)
    sequence_loads = jnp.concatenate([heaviest[None], loads]).astype(jnp.int32)
    run_ends = jnp.cumsum(sequence_loads)
    layout_rows = jnp.arange(ROW, dtype=jnp.int32)
    pick_cols = jnp.arange(TOP, dtype=jnp.int32)
    flat_pos = pick_cols[None, :] * length + layout_rows[:, None]
    run_index = jnp.sum((run_ends[None, None, :] <= flat_pos[:, :, None]).astype(jnp.int32), axis=-1)
    live_routes = sequence_ids[jnp.minimum(run_index, EXPERTS - 1)]
    padded_routes = (layout_rows[:, None] + pick_cols[None, :]) % EXPERTS
    is_live = layout_rows < length
    layout_routes = jnp.where(is_live[:, None], live_routes, padded_routes)
    order_scores = jax.random.randint(order_key, (ROW,), 0, 1 << 16) * ROW + layout_rows
    order_scores = jnp.where(is_live, order_scores, (1 << 28) + layout_rows)
    slot_order = jnp.argsort(order_scores)
    routes_row = jnp.zeros((ROW, TOP), jnp.int32).at[slot_order].set(layout_routes.astype(jnp.int32))
    counts_row = jnp.zeros((EXPERTS,), jnp.int32).at[sequence_ids].set(sequence_loads)
    return (routes_row, counts_row)


def sequence_plan(key):
    low_length = ROW // 4
    length_key = jax.random.fold_in(key, 11)
    hot_key = jax.random.fold_in(key, 12)
    row_ids = jnp.arange(ROWS, dtype=jnp.int32)
    rising = low_length + (ROW - low_length) * row_ids // (ROWS - 1)
    jitter = jax.random.randint(length_key, (ROWS,), -(ROW // 8), ROW // 8 + 1)
    lengths = jnp.clip(rising + jitter, low_length, ROW).astype(jnp.int32)
    lengths = lengths.at[0].set(low_length).at[ROWS - 1].set(ROW)
    hot_expert = jax.random.randint(hot_key, (), 0, EXPERTS).astype(jnp.int32)
    row_keys = jax.vmap(partial_key, in_axes=(None, 0))(key, row_ids)
    routes, counts = jax.vmap(row_plan, in_axes=(0, 0, None))(row_keys, lengths, hot_expert)
    return (lengths, routes, counts)


def partial_key(key, row_id):
    return jax.random.fold_in(key, 1000 + row_id)


def draw_lengths(key, part):
    return sequence_plan(key)[0]


def draw_routes(key, part):
    return sequence_plan(key)[1]


def draw_send_counts(key, part):
    return sequence_plan(key)[2]


def block_levels(own_key, shape, pieces, smallest, largest):
    factor_of = 1.0
    for dim, blocks in pieces:
        steps = jax.random.uniform(jax.random.fold_in(jax.random.fold_in(own_key, 6), dim), (blocks,), jnp.float32, smallest / len(pieces), largest / len(pieces))
        factor_of = factor_of * jnp.repeat(jnp.exp(steps), shape[dim] // blocks).reshape((-1,) + (1,) * (len(shape) - 1 - dim))
    return factor_of


def gaussian(key, shape, spread, bound, cuts=(), kind=jnp.bfloat16):
    array = jax.random.normal(key, shape, jnp.float32) * spread
    if len(cuts) > 0:
        array = block_levels(key, shape, cuts, -0.22, 0.18) * array
    return jnp.clip(array, min=-bound, max=bound).astype(kind)


def setup_inputs(seed: int = 0) -> dict:
    seeds = jax.random.split(jax.random.key(seed), 13)
    return {
        "tokens": gaussian(seeds[0], (ROWS, ROW, D), 1.0, 6.0, ((0, 32),)),
        "w_qkv": gaussian(seeds[1], (D, 3 * D), D ** -0.5, 0.125, ((0, 32),)),
        "w_out": gaussian(seeds[2], (D, D), (D // 32) ** -0.5, 0.75, ((0, 32),)),
        "w_router": gaussian(seeds[3], (D, EXPERTS), (4 * D) ** -0.5, 0.0625, ((0, 32),)),
        "gains": jnp.clip(1.0 + 0.18 * jax.random.normal(seeds[4], (4, D), jnp.float32), 0.099609375, 1.8984375).astype(jnp.bfloat16),
        "w_gate": gaussian(seeds[5], (EXPERTS, D, FF), D ** -0.5, 0.125, ((0, 16), (2, 2))),
        "w_up": gaussian(seeds[6], (EXPERTS, D, FF), (max(D * 256 // (EXPERTS * EXPERTS), 1)) ** -0.5, 0.125, ((0, 16), (2, 2))),
        "w_down": gaussian(seeds[7], (EXPERTS, FF, D), (max(FF // 512, 1)) ** -0.5, 4.0, ((0, 16), (1, 2))),
        "lengths": draw_lengths(jax.random.fold_in(seeds[12], 71), 0),
        "routes": draw_routes(jax.random.fold_in(seeds[12], 71), 0),
        "send_counts": draw_send_counts(jax.random.fold_in(seeds[12], 71), 0),
        "cotangent": gaussian(seeds[11], (ROWS, ROW, D), 1.0, 6.0, ((0, 32),)),
    }


NORM_EPS = 1e-05
BALANCE_WEIGHT = 0.01
HIGHEST = lax.Precision.HIGHEST

@jax.custom_vjp
def low(v):
    return lax.optimization_barrier(v.astype(jnp.bfloat16)).astype(jnp.float32)

@jax.custom_vjp
def low_back(v):
    return v

def low_keep(v):
    return (low(v), None)

def low_pass(kept, grad):
    return (grad,)

def back_keep(v):
    return (v, None)

def back_low(kept, grad):
    return (low(grad),)
low.defvjp(low_keep, low_pass)
low_back.defvjp(back_keep, back_low)

def norm_scale(values, gain_row):
    return values * lax.rsqrt(lax.optimization_barrier(jnp.mean(values * values, axis=-1, keepdims=True)) + NORM_EPS) * gain_row

def rope_tables(positions_count, head_width):
    half_width = head_width // 2
    frequency = jnp.exp(jnp.arange(half_width, dtype=jnp.float32) * (-2.0 * math.log(10000.0) / head_width))
    angles = jnp.arange(positions_count, dtype=jnp.float32)[:, None] * frequency[None, :]
    angles = jnp.concatenate([angles, angles], axis=1)
    return (jnp.cos(angles)[:, None, :], jnp.sin(angles)[:, None, :])

def rotate(values, cosine, sine_part):
    half_width = values.shape[-1] // 2
    turned = jnp.concatenate([-values[..., half_width:], values[..., :half_width]], axis=-1)
    return values * cosine + turned * sine_part

def query_key(query_part, key_part, query_gain, key_gain):
    positions_count = query_part.shape[0]
    cosine, sine_part = rope_tables(positions_count, HEAD)
    queries = norm_scale(query_part, query_gain).reshape(positions_count, HEADS, HEAD)
    key_heads = norm_scale(key_part, key_gain).reshape(positions_count, HEADS, HEAD)
    return (rotate(queries, cosine, sine_part), rotate(key_heads, cosine, sine_part))

def expert_apply(parts):
    gate_w, up_w, down_w, rows_in = parts
    gate_pre = low_back(jnp.dot(rows_in, gate_w, precision=HIGHEST))
    up_pre = low_back(jnp.dot(rows_in, up_w, precision=HIGHEST))
    hidden_low = low(jax.nn.silu(gate_pre) * up_pre)
    return low_back(low(jnp.dot(hidden_low, down_w, precision=HIGHEST)))

def reference(tokens, w_qkv, w_out, w_router, gains, w_gate, w_up, w_down, lengths, routes, send_counts, cotangent):
    positions = jnp.arange(ROW, dtype=jnp.int32)
    live_slots = positions[None, :] < lengths[:, None]
    expert_ids = jnp.arange(EXPERTS, dtype=jnp.int32)
    route_hot = (routes[..., None] == expert_ids) & live_slots[:, :, None, None]
    route_int = route_hot.astype(jnp.int32)
    per_token = lax.optimization_barrier(jnp.sum(route_int, axis=2))
    earlier = jnp.cumsum(per_token, axis=1) - per_token
    route_rank = lax.optimization_barrier(jnp.sum(earlier[:, :, None, :] * route_int, axis=-1))
    limits = lax.optimization_barrier(jnp.sum(jnp.minimum(send_counts, CAP)[:, None, None, :] * route_int, axis=-1))
    kept_route = route_rank < limits
    slot_index = (jnp.arange(ROWS, dtype=jnp.int32)[:, None, None] * CAP + route_rank).astype(jnp.int32)
    target_expert = jnp.where(kept_route, routes, EXPERTS).astype(jnp.int32)
    target_slot = jnp.where(kept_route, slot_index, 0).astype(jnp.int32)
    token_ids = (jnp.arange(ROWS, dtype=jnp.int32)[:, None] * ROW + positions[None, :]).astype(jnp.int32)
    token_ids = jnp.broadcast_to(token_ids[:, :, None], routes.shape)
    source = jnp.full((EXPERTS, ROWS * CAP), SLOTS, jnp.int32).at[target_expert, target_slot].set(token_ids, mode='drop')
    filled = (source < SLOTS).astype(jnp.float32)[:, :, None]
    source = jnp.minimum(source, SLOTS - 1).astype(jnp.int32)
    flat_index = jnp.where(kept_route, routes * (ROWS * CAP) + slot_index, 0).astype(jnp.int32)
    live_float = live_slots.astype(jnp.float32)[:, :, None]
    count_total = lax.optimization_barrier(jnp.sum(send_counts, axis=0)).astype(jnp.float32)
    balance_factor = float(EXPERTS) / (float(TOP) * float(SLOTS) * float(SLOTS))

    def forward(inputs, qkv_w, out_w, router_w, gain_rows, gate_w, up_w, down_w):

        def attend(row_pair):
            row_in, row_live = row_pair
            normed = low(norm_scale(row_in, gain_rows[0]))
            projected = low_back(jnp.dot(normed, qkv_w, precision=HIGHEST))
            rot_query, rot_keys = query_key(projected[:, :D], projected[:, D:2 * D], gain_rows[1], gain_rows[2])
            queries = low(rot_query)
            keys_low = low(rot_keys)
            values_low = low(projected[:, 2 * D:]).reshape(ROW, HEADS, HEAD)
            scores = low_back(jnp.einsum('qhd,khd->hqk', queries, keys_low, precision=HIGHEST) * HEAD ** (-0.5))
            allowed = (positions[None, :] <= positions[:, None]) & row_live[None, :]
            scores = jnp.where(allowed[None], scores, -1e+30)
            attn_probs = low(jax.nn.softmax(scores, axis=-1))
            mixed_heads = jnp.einsum('hqk,khd->qhd', attn_probs, values_low, precision=HIGHEST).reshape(ROW, D)
            mixed_heads = low_back(low(mixed_heads))
            return row_in + low_back(jnp.dot(mixed_heads, out_w, precision=HIGHEST))
        hidden_state = lax.map(jax.checkpoint(attend), (inputs, live_slots))
        ffn_in = low(norm_scale(hidden_state, gain_rows[3]))
        logits = low_back(jnp.einsum('rtd,de->rte', ffn_in, router_w, precision=HIGHEST))
        router_probs = jax.nn.softmax(logits, axis=-1)
        prob_total = lax.optimization_barrier(jnp.sum(router_probs * live_float, axis=(0, 1)))
        balance = jnp.sum(count_total * prob_total) * balance_factor
        rows_in = low_back(ffn_in.reshape(SLOTS, D)[source] * filled)
        expert_out = lax.map(jax.checkpoint(expert_apply), (gate_w, up_w, down_w, rows_in))
        flat_out = expert_out.reshape(EXPERTS * ROWS * CAP, D)
        route_prob = jnp.take_along_axis(router_probs, routes, axis=-1)
        combine_weight = jnp.where(kept_route, route_prob, 0.0)
        mixture = jnp.zeros_like(hidden_state)
        for pick_index in range(TOP):
            mixture = mixture + combine_weight[:, :, pick_index, None] * flat_out[flat_index[:, :, pick_index]]
        return (live_float * (hidden_state + mixture), balance)
    floats = (tokens.astype(jnp.float32), w_qkv.astype(jnp.float32), w_out.astype(jnp.float32), w_router.astype(jnp.float32), gains.astype(jnp.float32), w_gate.astype(jnp.float32), w_up.astype(jnp.float32), w_down.astype(jnp.float32))
    (layer, balance), pull_back = jax.vjp(forward, floats[0], floats[1], floats[2], floats[3], floats[4], floats[5], floats[6], floats[7])
    gradients = pull_back((cotangent.astype(jnp.float32), jnp.asarray(BALANCE_WEIGHT, jnp.float32)))
    return (layer.astype(jnp.bfloat16), gradients[0], gradients[1], gradients[2], gradients[3], gradients[4], gradients[5], gradients[6], gradients[7], balance)
```

```python
import functools
import itertools
import math

import jax
import jax.numpy as jnp
from jax import lax
from jax.experimental import pallas as pl
from jax.experimental.pallas import tpu as pltpu
from jax.sharding import PartitionSpec as P

D = 2048
HEADS = 16
HEAD = 128


NORM_EPS = 1e-05
BALANCE_WEIGHT = 0.01


def norm_scale(values, gain_row):
    return (
        values * lax.rsqrt(jnp.mean(values * values, axis=-1, keepdims=True) + NORM_EPS) * gain_row
    )


def rope_tables(positions_count, head_width):
    half_width = head_width // 2
    frequency = jnp.exp(
        jnp.arange(half_width, dtype=jnp.float32) * (-2.0 * math.log(10000.0) / head_width)
    )
    angles = jnp.arange(positions_count, dtype=jnp.float32)[:, None] * frequency[None, :]
    angles = jnp.concatenate([angles, angles], axis=1)
    return (jnp.cos(angles)[:, None, :], jnp.sin(angles)[:, None, :])


def rotate(values, cosine, sine_part):
    half_width = values.shape[-1] // 2
    turned = jnp.concatenate([-values[..., half_width:], values[..., :half_width]], axis=-1)
    return values * cosine + turned * sine_part


def query_key(query_part, key_part, query_gain, key_gain):
    positions_count = query_part.shape[0]
    cosine, sine_part = rope_tables(positions_count, HEAD)
    queries = norm_scale(query_part, query_gain).reshape(positions_count, HEADS, HEAD)
    key_heads = norm_scale(key_part, key_gain).reshape(positions_count, HEADS, HEAD)
    return (rotate(queries, cosine, sine_part), rotate(key_heads, cosine, sine_part))


def expert_forward(rows_in, gate_weight, up_weight, down_weight):
    gate_pre = jnp.einsum(
        "nkcd,kdf->nkcf", rows_in, gate_weight, preferred_element_type=jnp.float32
    )
    up_pre = jnp.einsum("nkcd,kdf->nkcf", rows_in, up_weight, preferred_element_type=jnp.float32)
    hidden_low = (jax.nn.silu(gate_pre) * up_pre).astype(jnp.bfloat16)
    output = jnp.einsum(
        "nkcf,kfd->nkcd", hidden_low, down_weight, preferred_element_type=jnp.float32
    )
    return (gate_pre, up_pre, hidden_low, output)


def routed_body(
    tokens,
    w_qkv,
    w_out,
    w_router,
    gains,
    w_gate,
    w_up,
    w_down,
    lengths,
    routes,
    send_counts,
    cotangent,
):
    row_count = tokens.shape[1]
    top_count = routes.shape[2]
    expert_count = w_router.shape[1]
    owners = lax.axis_size("expert")
    local_experts = expert_count // owners
    capacity = row_count * top_count // expert_count
    slots_all = row_count * lax.axis_size("dp") * owners
    balance_factor = float(expert_count) / (float(top_count) * float(slots_all) * float(slots_all))
    score_scale = HEAD ** (-0.5)
    inputs = tokens[0].astype(jnp.float32)
    positions = jnp.arange(row_count, dtype=jnp.int32)
    live_slots = positions < lengths[0]
    live_float = live_slots.astype(jnp.float32)[:, None]
    mixer_parts = (
        lax.all_gather(w_qkv, ("dp", "expert"), axis=0, tiled=True),
        lax.all_gather(w_out, ("dp", "expert"), axis=0, tiled=True),
        lax.all_gather(w_router, ("dp", "expert"), axis=0, tiled=True),
        lax.all_gather(gains, ("dp", "expert"), axis=1, tiled=True),
    )
    qkv_weight, out_weight, router_weight, gain_rows = mixer_parts
    gain_float = gain_rows.astype(jnp.float32)
    attn_in, attn_norm_back = jax.vjp(norm_scale, inputs, gain_float[0])
    normed = attn_in.astype(jnp.bfloat16)
    projected = jnp.dot(normed, qkv_weight, preferred_element_type=jnp.float32)
    (rot_query, rot_keys), query_key_back = jax.vjp(
        query_key, projected[:, :D], projected[:, D : 2 * D], gain_float[1], gain_float[2]
    )
    queries = rot_query.astype(jnp.bfloat16)
    keys_low = rot_keys.astype(jnp.bfloat16)
    values_low = projected[:, 2 * D :].astype(jnp.bfloat16).reshape(row_count, HEADS, HEAD)
    allowed = (positions[None, :] <= positions[:, None]) & live_slots[None, :]
    scores = (
        jnp.einsum("qhd,khd->hqk", queries, keys_low, preferred_element_type=jnp.float32)
        * score_scale
    )
    scores = jnp.where(allowed[None], scores, -1e30)
    highest = jnp.max(scores, axis=-1, keepdims=True)
    expo_scores = jnp.exp(scores - highest)
    totals = jnp.sum(expo_scores, axis=-1, keepdims=True)
    attn_probs = expo_scores / totals
    log_total = highest + jnp.log(totals)
    mixed_heads = jnp.einsum(
        "hqk,khd->qhd",
        attn_probs.astype(jnp.bfloat16),
        values_low,
        preferred_element_type=jnp.float32,
    )
    mixed_low = mixed_heads.reshape(row_count, D).astype(jnp.bfloat16)
    hidden_state = inputs + jnp.dot(mixed_low, out_weight, preferred_element_type=jnp.float32)
    ffn_in, ffn_norm_back = jax.vjp(norm_scale, hidden_state, gain_float[3])
    ffn_low = ffn_in.astype(jnp.bfloat16)
    logits = jnp.dot(ffn_low, router_weight, preferred_element_type=jnp.float32)
    router_probs = jax.nn.softmax(logits, axis=-1)
    count_float = send_counts[0].astype(jnp.float32)
    prob_local = jnp.sum(router_probs * live_float, axis=0)
    count_total, prob_total = lax.psum((count_float, prob_local), ("dp", "expert"))
    balance = jnp.sum(count_total * prob_total) * balance_factor
    route_rows = routes[0]
    expert_ids = jnp.arange(expert_count, dtype=jnp.int32)
    route_hot = (route_rows[:, :, None] == expert_ids) & live_slots[:, None, None]
    route_int = route_hot.astype(jnp.int32)
    per_token = jnp.sum(route_int, axis=1)
    earlier = jnp.cumsum(per_token, axis=0) - per_token
    route_rank = jnp.sum(earlier[:, None, :] * route_int, axis=-1)
    limits = jnp.sum(jnp.minimum(send_counts[0], capacity)[None, None, :] * route_int, axis=-1)
    kept_route = route_rank < limits
    target_expert = jnp.where(kept_route, route_rows, expert_count)
    target_slot = jnp.where(kept_route, route_rank, 0)
    token_ids = jnp.broadcast_to(positions[:, None], route_rows.shape)
    source = (
        jnp.full((expert_count, capacity), row_count, jnp.int32)
        .at[target_expert, target_slot]
        .set(token_ids, mode="drop")
    )
    padded_in = jnp.concatenate([ffn_low, jnp.zeros((1, D), jnp.bfloat16)], axis=0)
    send_rows = padded_in[source].reshape(owners, local_experts, capacity, D)
    expert_weights = (w_gate, w_up, w_down)
    gathered = lax.all_gather(
        lax.all_to_all(send_rows, "expert", split_axis=0, concat_axis=0, tiled=True),
        "dp",
        axis=0,
        tiled=True,
    )
    gate_pre, up_pre, hidden_low, partial_out = expert_forward(gathered, w_gate, w_up, w_down)
    summed = lax.psum_scatter(
        partial_out.astype(jnp.bfloat16), "dp", scatter_dimension=0, tiled=True
    )
    expert_out, expert_rows, gate_pre, up_pre, hidden_low = (
        summed,
        gathered,
        gate_pre,
        up_pre,
        hidden_low,
    )
    returned = lax.all_to_all(
        expert_out, "expert", split_axis=0, concat_axis=0, tiled=True
    ).reshape(expert_count * capacity, D)
    flat_index = jnp.where(kept_route, route_rows * capacity + route_rank, 0)
    picked = returned[flat_index]
    route_prob = jnp.sum(router_probs[:, None, :] * route_hot.astype(jnp.float32), axis=-1)
    combine_weight = jnp.where(kept_route, route_prob, 0.0)
    mixture = jnp.sum(combine_weight[:, :, None] * picked, axis=1)
    layer = live_float * (hidden_state + mixture)
    result = layer.astype(jnp.bfloat16)[None]
    qkv_back, out_back, router_back = (
        lax.all_gather(w_qkv, ("dp", "expert"), axis=0, tiled=True),
        lax.all_gather(w_out, ("dp", "expert"), axis=0, tiled=True),
        lax.all_gather(w_router, ("dp", "expert"), axis=0, tiled=True),
    )
    grad_layer = cotangent[0].astype(jnp.float32) * live_float
    dot_route = jnp.sum(grad_layer[:, None, :] * picked, axis=-1)
    balance_coef = BALANCE_WEIGHT * balance_factor
    grad_probs = jnp.sum(
        jnp.where(kept_route, dot_route, 0.0)[:, :, None] * route_hot.astype(jnp.float32), axis=1
    )
    grad_probs = grad_probs + balance_coef * count_total[None, :] * live_float
    grad_logits = router_probs * (
        grad_probs - jnp.sum(router_probs * grad_probs, axis=-1, keepdims=True)
    )
    grad_logits_low = grad_logits.astype(jnp.bfloat16)
    route_scale = (
        jnp.zeros((expert_count, capacity), jnp.float32)
        .at[target_expert, target_slot]
        .set(combine_weight, mode="drop")
    )
    padded_grad = jnp.concatenate([grad_layer, jnp.zeros((1, D), jnp.float32)], axis=0)
    grad_send = (
        (padded_grad[source] * route_scale[:, :, None])
        .astype(jnp.bfloat16)
        .reshape(owners, local_experts, capacity, D)
    )
    arrived = lax.all_to_all(grad_send, "expert", split_axis=0, concat_axis=0, tiled=True)
    grad_rows_all = lax.all_gather(arrived, "dp", axis=0, tiled=True)
    gate_weight, up_weight, down_weight = expert_weights
    grad_down_w = jnp.einsum(
        "nkcf,nkcd->kfd", hidden_low, grad_rows_all, preferred_element_type=jnp.float32
    )
    grad_units = jnp.einsum(
        "nkcd,kfd->nkcf", grad_rows_all, down_weight, preferred_element_type=jnp.float32
    )
    gate_sigmoid = jax.nn.sigmoid(gate_pre)
    grad_gate_low = (
        grad_units * up_pre * gate_sigmoid * (1.0 + gate_pre * (1.0 - gate_sigmoid))
    ).astype(jnp.bfloat16)
    grad_up_low = (grad_units * gate_pre * gate_sigmoid).astype(jnp.bfloat16)
    grad_gate_w = jnp.einsum(
        "nkcd,nkcf->kdf", expert_rows, grad_gate_low, preferred_element_type=jnp.float32
    )
    grad_up_w = jnp.einsum(
        "nkcd,nkcf->kdf", expert_rows, grad_up_low, preferred_element_type=jnp.float32
    )
    back_part = jnp.einsum(
        "nkcf,kdf->nkcd", grad_gate_low, gate_weight, preferred_element_type=jnp.float32
    )
    back_part = back_part + jnp.einsum(
        "nkcf,kdf->nkcd", grad_up_low, up_weight, preferred_element_type=jnp.float32
    )
    back_rows = lax.psum_scatter(
        back_part.astype(jnp.bfloat16), "dp", scatter_dimension=0, tiled=True
    )
    expert_grads = (grad_gate_w, grad_up_w, grad_down_w)
    sent_back = lax.all_to_all(
        back_rows, "expert", split_axis=0, concat_axis=0, tiled=True
    ).reshape(expert_count * capacity, D)
    grad_ffn = jnp.einsum(
        "tj,tjd->td",
        kept_route.astype(jnp.bfloat16),
        sent_back[flat_index],
        preferred_element_type=jnp.float32,
    )
    grad_ffn = grad_ffn + jnp.einsum(
        "te,de->td", grad_logits_low, router_back, preferred_element_type=jnp.float32
    )
    grad_router_w = jnp.einsum(
        "td,te->de", ffn_low, grad_logits_low, preferred_element_type=jnp.float32
    )
    grad_hidden_part, grad_gain_ffn = ffn_norm_back(grad_ffn)
    grad_hidden_state = grad_layer + grad_hidden_part
    grad_attn_low = grad_hidden_state.astype(jnp.bfloat16)
    grad_out_w = jnp.einsum(
        "td,te->de", mixed_low, grad_attn_low, preferred_element_type=jnp.float32
    )
    grad_mixed = jnp.einsum(
        "te,de->td", grad_attn_low, out_back, preferred_element_type=jnp.float32
    )
    grad_mixed = grad_mixed.astype(jnp.bfloat16).reshape(row_count, HEADS, HEAD)
    scores_again = (
        jnp.einsum("qhd,khd->hqk", queries, keys_low, preferred_element_type=jnp.float32)
        * score_scale
    )
    probs_again = jnp.where(allowed[None], jnp.exp(scores_again - log_total), 0.0)
    grad_values = jnp.einsum(
        "hqk,qhd->khd",
        probs_again.astype(jnp.bfloat16),
        grad_mixed,
        preferred_element_type=jnp.float32,
    )
    grad_attn_probs = jnp.einsum(
        "qhd,khd->hqk", grad_mixed, values_low, preferred_element_type=jnp.float32
    )
    grad_scores = probs_again * (
        grad_attn_probs - jnp.sum(probs_again * grad_attn_probs, axis=-1, keepdims=True)
    )
    grad_scores_low = grad_scores.astype(jnp.bfloat16)
    grad_queries = (
        jnp.einsum("hqk,khd->qhd", grad_scores_low, keys_low, preferred_element_type=jnp.float32)
        * score_scale
    )
    grad_keys = (
        jnp.einsum("hqk,qhd->khd", grad_scores_low, queries, preferred_element_type=jnp.float32)
        * score_scale
    )
    grad_query_part, grad_key_part, grad_gain_query, grad_gain_key = query_key_back(
        (grad_queries, grad_keys)
    )
    grad_projected = jnp.concatenate(
        [grad_query_part, grad_key_part, grad_values.reshape(row_count, D)], axis=1
    ).astype(jnp.bfloat16)
    grad_qkv_w = jnp.einsum("td,te->de", normed, grad_projected, preferred_element_type=jnp.float32)
    grad_normed = jnp.einsum(
        "te,de->td", grad_projected, qkv_back, preferred_element_type=jnp.float32
    )
    grad_input_part, grad_gain_attn = attn_norm_back(grad_normed)
    grad_inputs = grad_hidden_state + grad_input_part
    grad_gain_rows = jnp.stack([grad_gain_attn, grad_gain_query, grad_gain_key, grad_gain_ffn])
    mixer_grads = (
        lax.psum_scatter(grad_qkv_w, ("dp", "expert"), scatter_dimension=0, tiled=True),
        lax.psum_scatter(grad_out_w, ("dp", "expert"), scatter_dimension=0, tiled=True),
        lax.psum_scatter(grad_router_w, ("dp", "expert"), scatter_dimension=0, tiled=True),
        lax.psum_scatter(grad_gain_rows, ("dp", "expert"), scatter_dimension=1, tiled=True),
    )
    return (
        result,
        grad_inputs[None],
        mixer_grads[0],
        mixer_grads[1],
        mixer_grads[2],
        mixer_grads[3],
        expert_grads[0],
        expert_grads[1],
        expert_grads[2],
        balance,
    )


MESH = pl.DeviceIdType.MESH


class Grid:
    def __init__(self, dims, cores=False):
        self.cores = cores
        self.dims = ((2,) if cores else ()) + tuple(dims)
        self.size = math.prod(self.dims)
        self.strides = [math.prod(self.dims[d + 1 :]) for d in range(len(self.dims))]
        self.lanes = {}
        for d in range(len(self.dims)):
            for side in self.sides(d):
                self.lanes[(d, side)] = len(self.lanes)

    def coords(self):
        expert = lax.axis_index("expert")
        c = [lax.axis_index("dp")] if self.cores else []
        first = len(c)
        for d in range(first, len(self.dims)):
            c.append(lax.rem(expert // self.strides[d], self.dims[d]))
        return c

    def rels(self, d):
        n = self.dims[d]
        if n == 1:
            return []
        if n == 2:
            return [(1, 0)]
        return [(k, side) for k in range(1, n) for side in (-1, 1)]

    def sides(self, d):
        n = self.dims[d]
        return [] if n == 1 else [0] if n == 2 else [-1, 1]

    def at(self, c, d, rel):
        k, side = rel
        return 1 - c[d] if side == 0 else c[d] + side * k

    def valid(self, c, d, rel):
        k, side = rel
        if side == 0:
            return None
        return c[d] - k >= 0 if side < 0 else c[d] + k < self.dims[d]

    def index(self, coords):
        return sum(x * s for x, s in zip(coords, self.strides))

    def neighbor(self, c, d, side):
        other = list(c)
        other[d] = self.at(c, d, (1, side))
        ok = self.valid(c, d, (1, side))
        if self.cores and d == 0:
            return {"dp": other[0]}, ok
        first = 1 if self.cores else 0
        expert = sum(x * s for x, s in zip(other[first:], self.strides[first:]))
        return {"expert": expert}, ok

    def events(self, order):
        return [
            dict(zip(order, combo))
            for combo in itertools.product(*[[None] + self.rels(d) for d in order])
        ]

    def place(self, c, order, event):
        pred, o, last = None, list(c), -1
        for i, d in enumerate(order):
            if event[d]:
                pred = both(pred, self.valid(c, d, event[d]))
                o[d] = self.at(c, d, event[d])
                last = i
        return o, pred, last


def both(a, b):
    if a is None:
        return b
    if b is None:
        return a
    return jnp.logical_and(a, b)


def when(pred, f):
    if pred is None:
        f()
    else:
        pl.when(pred)(f)


def greet(grid, c):
    barrier = pltpu.get_barrier_semaphore()
    total = jnp.int32(0)
    for d, side in grid.lanes:
        device, ok = grid.neighbor(c, d, side)
        when(
            ok,
            lambda device=device: pl.semaphore_signal(
                barrier, inc=1, device_id=device, device_id_type=MESH
            ),
        )
        total = total + (1 if ok is None else ok.astype(jnp.int32))
    pl.semaphore_wait(barrier, total)


def hops(event):
    return sum(r[0] for r in event.values() if r)


def gather_kernel(grid, parts, count, *refs):
    srcs, outs = refs[:count], refs[count : 2 * count]
    send_sem, recv_sem, own_sem = refs[2 * count :]
    c = grid.coords()
    me = grid.index(c)
    own = [pltpu.make_async_copy(s, o.at[me], own_sem.at[i]) for i, (s, o) in enumerate(zip(srcs, outs))]
    for copy in own:
        copy.start()
    greet(grid, c)
    sent = []

    def piece(p, ref):
        _, row0, rows, _ = parts[p]
        return ref.at[pl.ds(row0, rows)]

    def push(p, origin, source, d, side, pred):
        device, ok = grid.neighbor(c, d, side)
        pred = both(pred, ok)
        copy = pltpu.make_async_remote_copy(
            src_ref=source,
            dst_ref=piece(p, outs[parts[p][0]].at[origin]),
            send_sem=send_sem.at[p, origin, grid.lanes[(d, side)]],
            recv_sem=recv_sem.at[p, origin],
            device_id=device,
            device_id_type=MESH,
        )
        when(pred, copy.start)
        sent.append((pred, copy))

    todo = []
    for p, (_, _, _, order) in enumerate(parts):
        for n, event in enumerate(grid.events(order)):
            todo.append((hops(event), p if len(parts) > 8 else 0, n, p, event))
    todo.sort(key=lambda t: t[:4])
    for _, _, _, p, event in todo:
        a, _, _, order = parts[p]
        o, pred, last = grid.place(c, order, event)
        origin = grid.index(o)
        if last < 0:
            source = piece(p, srcs[a])
        else:
            source = piece(p, outs[a].at[origin])
            arrival = pltpu.make_async_remote_copy(
                src_ref=source,
                dst_ref=source,
                send_sem=send_sem.at[p, origin, 0],
                recv_sem=recv_sem.at[p, origin],
                device_id={"expert": lax.axis_index("expert")},
                device_id_type=MESH,
            )
            when(pred, arrival.wait_recv)
            side = event[order[last]][1]
            if side:
                push(p, origin, source, order[last], -side, pred)
        for d in order[last + 1 :]:
            for side in grid.sides(d):
                push(p, origin, source, d, side, pred)
    for pred, copy in sent:
        when(pred, copy.wait_send)
    for copy in own:
        copy.wait()


def gather(arrays, grid, parts, cid):
    n, count = grid.size, len(arrays)
    return pl.pallas_call(
        functools.partial(gather_kernel, grid, parts, count),
        out_shape=[jax.ShapeDtypeStruct((n,) + x.shape, x.dtype) for x in arrays],
        in_specs=[pl.BlockSpec(memory_space=pl.ANY)] * count,
        out_specs=[pl.BlockSpec(memory_space=pl.ANY)] * count,
        scratch_shapes=[
            pltpu.SemaphoreType.DMA((len(parts), n, len(grid.lanes))),
            pltpu.SemaphoreType.DMA((len(parts), n)),
            pltpu.SemaphoreType.DMA((count,)),
        ],
        compiler_params=pltpu.CompilerParams(collective_id=cid, has_side_effects=True),
    )(*arrays)


def landing_slots(grid, order):
    base, total, earlier = {}, 0, 1
    for d in order:
        base[d] = total
        total += len(grid.rels(d)) * earlier
        earlier *= grid.dims[d]
    return base, total


def scatter_kernel(grid, parts, count, *refs):
    k = len(parts)
    srcs, outs = refs[:count], refs[count : 2 * count]
    held, mine, totals = refs[2 * count : 2 * count + k], refs[2 * count + k : 2 * count + 2 * k], refs[2 * count + 2 * k : 3 * count + 2 * k]
    send_sem, recv_sem, mine_sem, out_sem = refs[3 * count + 2 * k :]
    c = grid.coords()

    def piece(p, ref):
        _, row0, rows, _ = parts[p]
        return ref.at[pl.ds(row0, rows)]

    def own_slot(order, o):
        slot = 0
        for d in order[:-1]:
            slot = slot * grid.dims[d] + o[d]
        return slot

    def landing(order, d, rel, o):
        base, _ = landing_slots(grid, order)
        slot = grid.rels(d).index(rel)
        for q in order[: order.index(d)]:
            slot = slot * grid.dims[q] + o[q]
        return base[d] + slot

    def own_copy(p, o):
        a, _, _, order = parts[p]
        slot = own_slot(order, o)
        return pltpu.make_async_copy(
            piece(p, srcs[a].at[grid.index(o)]), mine[p].at[slot], mine_sem.at[p, slot]
        )

    for p, (_, _, _, order) in enumerate(parts):
        for position in itertools.product(*[range(grid.dims[d]) for d in order[:-1]]):
            o = list(c)
            for d, v in zip(order[:-1], position):
                o[d] = v
            own_copy(p, o).start()
    greet(grid, c)
    todo = []
    for p, (_, _, _, order) in enumerate(parts):
        for event in grid.events(order):
            todo.append((tuple(-(event[d][0] if event[d] else 0) for d in reversed(order)), p, event))
    todo.sort(key=lambda t: t[:2])
    sent = []
    for _, p, event in todo:
        a, row0, rows, order = parts[p]
        o, pred, last = grid.place(c, order, event)
        always, sometimes = [], []
        if last >= 0:
            far, side = event[order[last]]
            if side and far + 1 < grid.dims[order[last]]:
                _, ok = grid.neighbor(c, order[last], -side)
                sometimes.append((landing(order, order[last], (far + 1, side), o), ok))
        for d in order[last + 1 :]:
            for side in grid.sides(d):
                _, ok = grid.neighbor(c, d, side)
                slot = landing(order, d, (1, -side), o)
                if ok is None:
                    always.append(slot)
                else:
                    sometimes.append((slot, ok))
        final = last < 0
        if not always and not sometimes and not final:
            source = piece(p, srcs[a].at[grid.index(o)])
        else:
            source = mine[p].at[own_slot(order, o)]
            when(pred, own_copy(p, o).wait)
            steps = [(slot, ok) for slot, ok in sometimes]
            if always or final:
                steps.insert(0, (always, None))

            def add(slots, opening, final=final, source=source, p=p, row0=row0, rows=rows, a=a):
                for slot in slots:
                    landed = held[p].at[slot]
                    pltpu.make_async_remote_copy(
                        src_ref=landed,
                        dst_ref=landed,
                        send_sem=send_sem.at[p, 0],
                        recv_sem=recv_sem.at[p, slot],
                        device_id={"expert": lax.axis_index("expert")},
                        device_id_type=MESH,
                    ).wait_recv()
                tile = min(16, rows)

                @pl.loop(0, rows // tile)
                def _(t):
                    here = pl.ds(pl.multiple_of(t * tile, tile), tile)
                    there = pl.ds(pl.multiple_of(row0 + t * tile, tile), tile)
                    if final and not opening:
                        value = totals[a][there, :]
                    else:
                        value = source[here, :].astype(jnp.float32)
                    for slot in slots:
                        value = value + held[p][slot, here, :].astype(jnp.float32)
                    if final:
                        totals[a][there, :] = value
                    else:
                        source[here, :] = value.astype(source.dtype)

            for n, (slots, ok) in enumerate(steps):
                slots = slots if isinstance(slots, list) else [slots]
                when(both(pred, ok), functools.partial(add, slots, n == 0))
        if last >= 0:
            d = order[last]
            device, _ = grid.neighbor(c, d, event[d][1])
            slot = landing(order, d, event[d], o)
            copy = pltpu.make_async_remote_copy(
                src_ref=source,
                dst_ref=held[p].at[slot],
                send_sem=send_sem.at[p, slot],
                recv_sem=recv_sem.at[p, slot],
                device_id=device,
                device_id_type=MESH,
            )
            when(pred, copy.start)
            sent.append((pred, copy))
    done = [pltpu.make_async_copy(t, o, out_sem.at[i]) for i, (t, o) in enumerate(zip(totals, outs))]
    for copy in done:
        copy.start()
    for pred, copy in sent:
        when(pred, copy.wait_send)
    for copy in done:
        copy.wait()


def scatter(arrays, grid, parts, cid):
    count = len(arrays)
    slots = [landing_slots(grid, order)[1] for _, _, _, order in parts]
    mine = [grid.size // grid.dims[order[-1]] for _, _, _, order in parts]
    blocks = [((rows, arrays[a].shape[2]), arrays[a].dtype) for a, _, rows, _ in parts]
    flat = [jax.ShapeDtypeStruct(x.shape[1:], jnp.float32) for x in arrays]
    return pl.pallas_call(
        functools.partial(scatter_kernel, grid, parts, count),
        out_shape=flat,
        in_specs=[pl.BlockSpec(memory_space=pl.ANY)] * count,
        out_specs=[pl.BlockSpec(memory_space=pl.ANY)] * count,
        scratch_shapes=[pltpu.VMEM((s,) + b, t) for s, (b, t) in zip(slots, blocks)]
        + [pltpu.VMEM((s,) + b, t) for s, (b, t) in zip(mine, blocks)]
        + [pltpu.VMEM(x.shape, x.dtype) for x in flat]
        + [
            pltpu.SemaphoreType.DMA((len(parts), max(slots))),
            pltpu.SemaphoreType.DMA((len(parts), max(slots))),
            pltpu.SemaphoreType.DMA((len(parts), max(mine))),
            pltpu.SemaphoreType.DMA((count,)),
        ],
        compiler_params=pltpu.CompilerParams(
            collective_id=cid, has_side_effects=True, vmem_limit_bytes=60 << 20
        ),
    )(*arrays)


def cut(array, rows, orders):
    share = rows // len(orders)
    return tuple((array, i * share, share, order) for i, order in enumerate(orders))


def gathered_body(
    dims,
    tokens,
    w_qkv,
    w_out,
    w_router,
    gains,
    w_gate,
    w_up,
    w_down,
    lengths,
    routes,
    send_counts,
    cotangent,
):
    row_count = tokens.shape[1]
    top_count = routes.shape[2]
    expert_count = w_router.shape[1]
    owners = math.prod(dims)
    weight_rows = w_qkv.shape[0]
    capacity = row_count * top_count // expert_count
    slots_all = row_count * 2 * owners
    balance_factor = float(expert_count) / (float(top_count) * float(slots_all) * float(slots_all))
    score_scale = HEAD ** (-0.5)
    low = jnp.bfloat16
    full = jnp.float32
    chips = Grid(dims)
    devices = Grid(dims, cores=True)
    z, y, x = 0, 1, 2
    row_orders = [(x, z, y), (y, z, x), (z, x, y), (z, y, x)]
    wide_orders = [tuple(d + 1 for d in order) + (0,) for order in row_orders]
    expert = lax.axis_index("expert")
    core = lax.axis_index("dp")
    swap = [(0, 1), (1, 0)]

    small = jnp.concatenate(
        [w_router, gains.T, jnp.zeros((weight_rows, 128 - expert_count - 4), low)], axis=1
    )
    qkv_all, out_all, small_all = gather(
        [w_qkv, w_out, small],
        devices,
        cut(0, weight_rows, wide_orders) + cut(1, weight_rows, wide_orders[:2]) + cut(2, weight_rows, wide_orders[2:3]),
        1,
    )
    qkv_weight = qkv_all.reshape(D, 3 * D)
    out_weight = out_all.reshape(D, D)
    small_all = small_all.reshape(D, 128)
    router_weight = small_all[:, :expert_count]
    gain_float = small_all[:, expert_count : expert_count + 4].T.astype(full)
    gate_own, up_own, down_own = w_gate[0], w_up[0], w_down[0]
    gate_far, up_far, down_far = (lax.ppermute(w, "dp", swap) for w in (gate_own, up_own, down_own))

    positions = jnp.arange(row_count, dtype=jnp.int32)
    live_slots = positions < lengths[0]
    live_float = live_slots.astype(full)[:, None]
    expert_ids = jnp.arange(expert_count, dtype=jnp.int32)
    named = jnp.any(routes[0][:, :, None] == expert_ids, axis=1) & live_slots[:, None]
    before = (positions[None, :] < positions[:, None]).astype(low)
    rank = jnp.dot(before, named.astype(low), preferred_element_type=full)
    limit = jnp.minimum(send_counts[0], capacity).astype(full)
    kept = named & (rank < limit[None, :])
    kept_rank = jnp.where(kept, rank, -1.0)

    inputs = tokens[0].astype(full)
    attn_in, attn_norm_back = jax.vjp(norm_scale, inputs, gain_float[0])
    normed = attn_in.astype(low)
    projected = jnp.dot(normed, qkv_weight, preferred_element_type=full)
    (rot_query, rot_keys), query_key_back = jax.vjp(
        query_key, projected[:, :D], projected[:, D : 2 * D], gain_float[1], gain_float[2]
    )
    queries = rot_query.astype(low)
    keys_low = rot_keys.astype(low)
    values_low = projected[:, 2 * D :].astype(low).reshape(row_count, HEADS, HEAD)
    allowed = (positions[None, :] <= positions[:, None]) & live_slots[None, :]
    scores = jnp.einsum("qhd,khd->hqk", queries, keys_low, preferred_element_type=full) * score_scale
    scores = jnp.where(allowed[None], scores, -1e30)
    highest = jnp.max(scores, axis=-1, keepdims=True)
    expo_scores = jnp.exp(scores - highest)
    totals = jnp.sum(expo_scores, axis=-1, keepdims=True)
    attn_probs = expo_scores / totals
    log_total = highest + jnp.log(totals)
    mixed_heads = jnp.einsum("hqk,khd->qhd", attn_probs.astype(low), values_low, preferred_element_type=full)
    mixed_low = mixed_heads.reshape(row_count, D).astype(low)
    hidden_state = inputs + jnp.dot(mixed_low, out_weight, preferred_element_type=full)
    ffn_in, ffn_norm_back = jax.vjp(norm_scale, hidden_state, gain_float[3])
    ffn_low = ffn_in.astype(low)
    logits = jnp.dot(ffn_low, router_weight, preferred_element_type=full)
    router_probs = jax.nn.softmax(logits, axis=-1)
    prob_local = jnp.sum(router_probs * live_float, axis=0)
    sums = jnp.concatenate([send_counts[0].astype(full), prob_local])
    aside = jnp.concatenate(
        [
            jnp.where(kept, router_probs, 0.0).T,
            kept_rank.T,
            jnp.pad(sums[None, :], ((0, 7), (0, row_count - 2 * expert_count))),
        ],
        axis=0,
    )

    (cot_rows,) = gather([cotangent[0]], chips, cut(0, row_count, row_orders), 2)
    ffn_rows, aside_rows = gather(
        [ffn_low, aside],
        chips,
        cut(0, row_count, row_orders) + cut(1, aside.shape[0], row_orders[2:3]),
        3,
    )
    sums_core = jnp.sum(aside_rows[:, 2 * expert_count, : 2 * expert_count], axis=0)
    sums_all = sums_core + lax.ppermute(sums_core, "dp", swap)
    count_total, prob_total = sums_all[:expert_count], sums_all[expert_count:]
    balance = jnp.sum(count_total * prob_total) * balance_factor
    weight_of = lax.dynamic_index_in_dim(aside_rows, expert, 1, keepdims=False)
    rank_of = lax.dynamic_index_in_dim(aside_rows, expert_count + expert, 1, keepdims=False)
    pick = rank_of[:, None, :] == jnp.arange(capacity, dtype=jnp.int32).astype(full)[None, :, None]
    pick_low = pick.astype(low)
    all_slots = owners * capacity
    rows_in = jnp.einsum("rkt,rtd->rkd", pick_low, ffn_rows, preferred_element_type=full)
    rows_in = rows_in.astype(low).reshape(all_slots, D)
    cot_in = jnp.einsum("rkt,rtd->rkd", pick_low, cot_rows, preferred_element_type=full)
    cot_in = cot_in.astype(low).reshape(all_slots, D)
    slot_weight = jnp.sum(jnp.where(pick, weight_of[:, None, :], 0.0), axis=-1).reshape(all_slots, 1)
    grad_rows = (cot_in.astype(full) * slot_weight).astype(low)

    def forward(gate_weight, up_weight):
        gate_pre = jnp.dot(rows_in, gate_weight, preferred_element_type=full)
        up_pre = jnp.dot(rows_in, up_weight, preferred_element_type=full)
        return gate_pre, up_pre, (jax.nn.silu(gate_pre) * up_pre).astype(low)

    own, far = forward(gate_own, up_own), forward(gate_far, up_far)
    expert_out = jnp.dot(own[2], down_own, preferred_element_type=full)
    expert_out = (expert_out + jnp.dot(far[2], down_far, preferred_element_type=full)).astype(low)
    dot_slot = jnp.sum(cot_in.astype(full) * expert_out.astype(full), axis=-1).reshape(owners, 1, capacity)
    dot_route = jnp.sum(jnp.where(pick, dot_slot.reshape(owners, capacity, 1), 0.0), axis=1)
    mixture_part = jnp.einsum(
        "rkt,rkd->rtd", pick_low, expert_out.reshape(owners, capacity, D), preferred_element_type=full
    )
    mixture_part = (mixture_part * weight_of[:, :, None]).astype(low)

    def backward(parts, down_weight):
        gate_pre, up_pre, _ = parts
        grad_units = jnp.einsum("sd,fd->sf", grad_rows, down_weight, preferred_element_type=full)
        gate_sigmoid = jax.nn.sigmoid(gate_pre)
        grad_gate = grad_units * up_pre * gate_sigmoid * (1.0 + gate_pre * (1.0 - gate_sigmoid))
        return grad_gate.astype(low), (grad_units * gate_pre * gate_sigmoid).astype(low)

    grad_own, grad_far = backward(own, down_own), backward(far, down_far)
    back = jnp.einsum("sf,df->sd", grad_own[0], gate_own, preferred_element_type=full)
    back = back + jnp.einsum("sf,df->sd", grad_own[1], up_own, preferred_element_type=full)
    back = back + jnp.einsum("sf,df->sd", grad_far[0], gate_far, preferred_element_type=full)
    back = back + jnp.einsum("sf,df->sd", grad_far[1], up_far, preferred_element_type=full)
    back_part = jnp.einsum(
        "rkt,rkd->rtd", pick_low, back.astype(low).reshape(owners, capacity, D), preferred_element_type=full
    ).astype(low)
    route_part = jnp.where(
        (expert_ids == expert)[None, :, None], dot_route[:, None, :], 0.0
    )

    def outer(left, right):
        return jnp.einsum("sa,sb->ab", left, right, preferred_element_type=full)

    def weight_grads(units, grads):
        return outer(rows_in, grads[0]), outer(rows_in, grads[1]), outer(units, grad_rows)

    sent_grads = [
        lax.ppermute(g.astype(low), "dp", swap) for g in weight_grads(far[2], grad_far)
    ]
    expert_grads = [
        (a + b.astype(full))[None] for a, b in zip(weight_grads(own[2], grad_own), sent_grads)
    ]
    grad_ffn, grad_route = scatter(
        [back_part, route_part],
        chips,
        cut(0, row_count, row_orders) + cut(1, expert_count, row_orders[2:3]),
        4,
    )
    (mixture,) = scatter([mixture_part], chips, cut(0, row_count, row_orders), 5)
    result = (live_float * (hidden_state + mixture)).astype(low)[None]

    balance_coef = BALANCE_WEIGHT * balance_factor
    grad_probs = grad_route.T + balance_coef * count_total[None, :] * live_float
    grad_logits = router_probs * (
        grad_probs - jnp.sum(router_probs * grad_probs, axis=-1, keepdims=True)
    )
    grad_logits_low = grad_logits.astype(low)
    grad_ffn = grad_ffn + jnp.einsum("te,de->td", grad_logits_low, router_weight, preferred_element_type=full)
    grad_router_w = jnp.einsum("td,te->de", ffn_low, grad_logits_low, preferred_element_type=full)

    grad_layer = cotangent[0].astype(full) * live_float
    grad_hidden_part, grad_gain_ffn = ffn_norm_back(grad_ffn)
    grad_hidden_state = grad_layer + grad_hidden_part
    grad_attn_low = grad_hidden_state.astype(low)
    grad_mixed = jnp.einsum("te,de->td", grad_attn_low, out_weight, preferred_element_type=full)
    grad_mixed = grad_mixed.astype(low).reshape(row_count, HEADS, HEAD)
    scores_again = jnp.einsum("qhd,khd->hqk", queries, keys_low, preferred_element_type=full) * score_scale
    probs_again = jnp.where(allowed[None], jnp.exp(scores_again - log_total), 0.0)
    grad_values = jnp.einsum("hqk,qhd->khd", probs_again.astype(low), grad_mixed, preferred_element_type=full)
    grad_attn_probs = jnp.einsum("qhd,khd->hqk", grad_mixed, values_low, preferred_element_type=full)
    grad_scores = probs_again * (
        grad_attn_probs - jnp.sum(probs_again * grad_attn_probs, axis=-1, keepdims=True)
    )
    grad_scores_low = grad_scores.astype(low)
    grad_queries = jnp.einsum("hqk,khd->qhd", grad_scores_low, keys_low, preferred_element_type=full) * score_scale
    grad_keys = jnp.einsum("hqk,qhd->khd", grad_scores_low, queries, preferred_element_type=full) * score_scale
    grad_query_part, grad_key_part, grad_gain_query, grad_gain_key = query_key_back(
        (grad_queries, grad_keys)
    )
    grad_projected = jnp.concatenate(
        [grad_query_part, grad_key_part, grad_values.reshape(row_count, D)], axis=1
    ).astype(low)
    grad_normed = jnp.einsum("te,de->td", grad_projected, qkv_weight, preferred_element_type=full)
    grad_input_part, grad_gain_attn = attn_norm_back(grad_normed)
    grad_inputs = grad_hidden_state + grad_input_part
    grad_gain_rows = jnp.stack([grad_gain_attn, grad_gain_query, grad_gain_key, grad_gain_ffn])

    half = D // 2

    def core_half(value, side):
        return lax.dynamic_slice_in_dim(value, side * half, half, 1)

    small_grads = jnp.concatenate(
        [grad_router_w, grad_gain_rows.T, jnp.zeros((D, 128 - expert_count - 4), full)], axis=1
    )

    def mixer_grads(side):
        return (
            outer(core_half(normed, side), grad_projected),
            outer(core_half(mixed_low, side), grad_attn_low),
            lax.dynamic_slice_in_dim(small_grads, side * half, half, 0),
        )

    far_qkv, far_out, far_small = mixer_grads(1 - core)
    far_parts = [
        lax.ppermute(g, "dp", swap) for g in (far_qkv.astype(low), far_out.astype(low), far_small)
    ]
    shares = [
        (a + b.astype(full)).astype(b.dtype).reshape(owners, weight_rows, a.shape[1])
        for a, b in zip(mixer_grads(core), far_parts)
    ]
    grad_qkv, grad_out, grad_small = scatter(
        shares,
        chips,
        cut(0, weight_rows, row_orders) + cut(1, weight_rows, row_orders) + cut(2, weight_rows, row_orders[2:3]),
        6,
    )
    return (
        result,
        grad_inputs[None],
        grad_qkv,
        grad_out,
        grad_small[:, :expert_count],
        grad_small[:, expert_count : expert_count + 4].T,
        *expert_grads,
        balance,
    )


def solution(mesh):
    dims = {4: (1, 2, 2), 8: (2, 2, 2), 16: (4, 2, 2)}.get(mesh.shape["expert"])
    plan = routed_body if dims is None or mesh.shape["dp"] != 2 else functools.partial(gathered_body, dims)
    placed = (
        P(("dp", "expert"), None, None),
        P(("dp", "expert"), None),
        P(("dp", "expert"), None),
        P(("dp", "expert"), None),
        P(None, ("dp", "expert")),
        P("expert", None, "dp"),
        P("expert", None, "dp"),
        P("expert", "dp", None),
        P(("dp", "expert")),
        P(("dp", "expert"), None, None),
        P(("dp", "expert"), None),
        P(("dp", "expert"), None, None),
    )
    return jax.shard_map(
        plan,
        mesh=mesh,
        in_specs=placed,
        out_specs=(
            P(("dp", "expert"), None, None),
            P(("dp", "expert"), None, None),
            P(("dp", "expert"), None),
            P(("dp", "expert"), None),
            P(("dp", "expert"), None),
            P(None, ("dp", "expert")),
            P("expert", None, "dp"),
            P("expert", None, "dp"),
            P("expert", "dp", None),
            P(),
        ),
        check_vma=False,
    )
```

```python
import functools
import itertools
import math

import jax
import jax.numpy as jnp
from jax import lax
from jax.experimental import pallas as pl
from jax.experimental.pallas import tpu as pltpu
from jax.sharding import PartitionSpec as P

D = 2048
HEADS = 16
HEAD = 128


NORM_EPS = 1e-05
BALANCE_WEIGHT = 0.01


def norm_scale(values, gain_row):
    return (
        values * lax.rsqrt(jnp.mean(values * values, axis=-1, keepdims=True) + NORM_EPS) * gain_row
    )


def rope_tables(positions_count, head_width):
    half_width = head_width // 2
    frequency = jnp.exp(
        jnp.arange(half_width, dtype=jnp.float32) * (-2.0 * math.log(10000.0) / head_width)
    )
    angles = jnp.arange(positions_count, dtype=jnp.float32)[:, None] * frequency[None, :]
    angles = jnp.concatenate([angles, angles], axis=1)
    return (jnp.cos(angles)[:, None, :], jnp.sin(angles)[:, None, :])


def rotate(values, cosine, sine_part):
    half_width = values.shape[-1] // 2
    turned = jnp.concatenate([-values[..., half_width:], values[..., :half_width]], axis=-1)
    return values * cosine + turned * sine_part


def query_key(query_part, key_part, query_gain, key_gain):
    positions_count = query_part.shape[0]
    cosine, sine_part = rope_tables(positions_count, HEAD)
    queries = norm_scale(query_part, query_gain).reshape(positions_count, HEADS, HEAD)
    key_heads = norm_scale(key_part, key_gain).reshape(positions_count, HEADS, HEAD)
    return (rotate(queries, cosine, sine_part), rotate(key_heads, cosine, sine_part))


def expert_forward(rows_in, gate_weight, up_weight, down_weight):
    gate_pre = jnp.einsum(
        "nkcd,kdf->nkcf", rows_in, gate_weight, preferred_element_type=jnp.float32
    )
    up_pre = jnp.einsum("nkcd,kdf->nkcf", rows_in, up_weight, preferred_element_type=jnp.float32)
    hidden_low = (jax.nn.silu(gate_pre) * up_pre).astype(jnp.bfloat16)
    output = jnp.einsum(
        "nkcf,kfd->nkcd", hidden_low, down_weight, preferred_element_type=jnp.float32
    )
    return (gate_pre, up_pre, hidden_low, output)


def routed_body(
    tokens,
    w_qkv,
    w_out,
    w_router,
    gains,
    w_gate,
    w_up,
    w_down,
    lengths,
    routes,
    send_counts,
    cotangent,
):
    row_count = tokens.shape[1]
    top_count = routes.shape[2]
    expert_count = w_router.shape[1]
    owners = lax.axis_size("expert")
    local_experts = expert_count // owners
    capacity = row_count * top_count // expert_count
    slots_all = row_count * lax.axis_size("dp") * owners
    balance_factor = float(expert_count) / (float(top_count) * float(slots_all) * float(slots_all))
    score_scale = HEAD ** (-0.5)
    inputs = tokens[0].astype(jnp.float32)
    positions = jnp.arange(row_count, dtype=jnp.int32)
    live_slots = positions < lengths[0]
    live_float = live_slots.astype(jnp.float32)[:, None]
    mixer_parts = (
        lax.all_gather(w_qkv, ("dp", "expert"), axis=0, tiled=True),
        lax.all_gather(w_out, ("dp", "expert"), axis=0, tiled=True),
        lax.all_gather(w_router, ("dp", "expert"), axis=0, tiled=True),
        lax.all_gather(gains, ("dp", "expert"), axis=1, tiled=True),
    )
    qkv_weight, out_weight, router_weight, gain_rows = mixer_parts
    gain_float = gain_rows.astype(jnp.float32)
    attn_in, attn_norm_back = jax.vjp(norm_scale, inputs, gain_float[0])
    normed = attn_in.astype(jnp.bfloat16)
    projected = jnp.dot(normed, qkv_weight, preferred_element_type=jnp.float32)
    (rot_query, rot_keys), query_key_back = jax.vjp(
        query_key, projected[:, :D], projected[:, D : 2 * D], gain_float[1], gain_float[2]
    )
    queries = rot_query.astype(jnp.bfloat16)
    keys_low = rot_keys.astype(jnp.bfloat16)
    values_low = projected[:, 2 * D :].astype(jnp.bfloat16).reshape(row_count, HEADS, HEAD)
    allowed = (positions[None, :] <= positions[:, None]) & live_slots[None, :]
    scores = (
        jnp.einsum("qhd,khd->hqk", queries, keys_low, preferred_element_type=jnp.float32)
        * score_scale
    )
    scores = jnp.where(allowed[None], scores, -1e30)
    highest = jnp.max(scores, axis=-1, keepdims=True)
    expo_scores = jnp.exp(scores - highest)
    totals = jnp.sum(expo_scores, axis=-1, keepdims=True)
    attn_probs = expo_scores / totals
    log_total = highest + jnp.log(totals)
    mixed_heads = jnp.einsum(
        "hqk,khd->qhd",
        attn_probs.astype(jnp.bfloat16),
        values_low,
        preferred_element_type=jnp.float32,
    )
    mixed_low = mixed_heads.reshape(row_count, D).astype(jnp.bfloat16)
    hidden_state = inputs + jnp.dot(mixed_low, out_weight, preferred_element_type=jnp.float32)
    ffn_in, ffn_norm_back = jax.vjp(norm_scale, hidden_state, gain_float[3])
    ffn_low = ffn_in.astype(jnp.bfloat16)
    logits = jnp.dot(ffn_low, router_weight, preferred_element_type=jnp.float32)
    router_probs = jax.nn.softmax(logits, axis=-1)
    count_float = send_counts[0].astype(jnp.float32)
    prob_local = jnp.sum(router_probs * live_float, axis=0)
    count_total, prob_total = lax.psum((count_float, prob_local), ("dp", "expert"))
    balance = jnp.sum(count_total * prob_total) * balance_factor
    route_rows = routes[0]
    expert_ids = jnp.arange(expert_count, dtype=jnp.int32)
    route_hot = (route_rows[:, :, None] == expert_ids) & live_slots[:, None, None]
    route_int = route_hot.astype(jnp.int32)
    per_token = jnp.sum(route_int, axis=1)
    earlier = jnp.cumsum(per_token, axis=0) - per_token
    route_rank = jnp.sum(earlier[:, None, :] * route_int, axis=-1)
    limits = jnp.sum(jnp.minimum(send_counts[0], capacity)[None, None, :] * route_int, axis=-1)
    kept_route = route_rank < limits
    target_expert = jnp.where(kept_route, route_rows, expert_count)
    target_slot = jnp.where(kept_route, route_rank, 0)
    token_ids = jnp.broadcast_to(positions[:, None], route_rows.shape)
    source = (
        jnp.full((expert_count, capacity), row_count, jnp.int32)
        .at[target_expert, target_slot]
        .set(token_ids, mode="drop")
    )
    padded_in = jnp.concatenate([ffn_low, jnp.zeros((1, D), jnp.bfloat16)], axis=0)
    send_rows = padded_in[source].reshape(owners, local_experts, capacity, D)
    expert_weights = (w_gate, w_up, w_down)
    gathered = lax.all_gather(
        lax.all_to_all(send_rows, "expert", split_axis=0, concat_axis=0, tiled=True),
        "dp",
        axis=0,
        tiled=True,
    )
    gate_pre, up_pre, hidden_low, partial_out = expert_forward(gathered, w_gate, w_up, w_down)
    summed = lax.psum_scatter(
        partial_out.astype(jnp.bfloat16), "dp", scatter_dimension=0, tiled=True
    )
    expert_out, expert_rows, gate_pre, up_pre, hidden_low = (
        summed,
        gathered,
        gate_pre,
        up_pre,
        hidden_low,
    )
    returned = lax.all_to_all(
        expert_out, "expert", split_axis=0, concat_axis=0, tiled=True
    ).reshape(expert_count * capacity, D)
    flat_index = jnp.where(kept_route, route_rows * capacity + route_rank, 0)
    picked = returned[flat_index]
    route_prob = jnp.sum(router_probs[:, None, :] * route_hot.astype(jnp.float32), axis=-1)
    combine_weight = jnp.where(kept_route, route_prob, 0.0)
    mixture = jnp.sum(combine_weight[:, :, None] * picked, axis=1)
    layer = live_float * (hidden_state + mixture)
    result = layer.astype(jnp.bfloat16)[None]
    qkv_back, out_back, router_back = (
        lax.all_gather(w_qkv, ("dp", "expert"), axis=0, tiled=True),
        lax.all_gather(w_out, ("dp", "expert"), axis=0, tiled=True),
        lax.all_gather(w_router, ("dp", "expert"), axis=0, tiled=True),
    )
    grad_layer = cotangent[0].astype(jnp.float32) * live_float
    dot_route = jnp.sum(grad_layer[:, None, :] * picked, axis=-1)
    balance_coef = BALANCE_WEIGHT * balance_factor
    grad_probs = jnp.sum(
        jnp.where(kept_route, dot_route, 0.0)[:, :, None] * route_hot.astype(jnp.float32), axis=1
    )
    grad_probs = grad_probs + balance_coef * count_total[None, :] * live_float
    grad_logits = router_probs * (
        grad_probs - jnp.sum(router_probs * grad_probs, axis=-1, keepdims=True)
    )
    grad_logits_low = grad_logits.astype(jnp.bfloat16)
    route_scale = (
        jnp.zeros((expert_count, capacity), jnp.float32)
        .at[target_expert, target_slot]
        .set(combine_weight, mode="drop")
    )
    padded_grad = jnp.concatenate([grad_layer, jnp.zeros((1, D), jnp.float32)], axis=0)
    grad_send = (
        (padded_grad[source] * route_scale[:, :, None])
        .astype(jnp.bfloat16)
        .reshape(owners, local_experts, capacity, D)
    )
    arrived = lax.all_to_all(grad_send, "expert", split_axis=0, concat_axis=0, tiled=True)
    grad_rows_all = lax.all_gather(arrived, "dp", axis=0, tiled=True)
    gate_weight, up_weight, down_weight = expert_weights
    grad_down_w = jnp.einsum(
        "nkcf,nkcd->kfd", hidden_low, grad_rows_all, preferred_element_type=jnp.float32
    )
    grad_units = jnp.einsum(
        "nkcd,kfd->nkcf", grad_rows_all, down_weight, preferred_element_type=jnp.float32
    )
    gate_sigmoid = jax.nn.sigmoid(gate_pre)
    grad_gate_low = (
        grad_units * up_pre * gate_sigmoid * (1.0 + gate_pre * (1.0 - gate_sigmoid))
    ).astype(jnp.bfloat16)
    grad_up_low = (grad_units * gate_pre * gate_sigmoid).astype(jnp.bfloat16)
    grad_gate_w = jnp.einsum(
        "nkcd,nkcf->kdf", expert_rows, grad_gate_low, preferred_element_type=jnp.float32
    )
    grad_up_w = jnp.einsum(
        "nkcd,nkcf->kdf", expert_rows, grad_up_low, preferred_element_type=jnp.float32
    )
    back_part = jnp.einsum(
        "nkcf,kdf->nkcd", grad_gate_low, gate_weight, preferred_element_type=jnp.float32
    )
    back_part = back_part + jnp.einsum(
        "nkcf,kdf->nkcd", grad_up_low, up_weight, preferred_element_type=jnp.float32
    )
    back_rows = lax.psum_scatter(
        back_part.astype(jnp.bfloat16), "dp", scatter_dimension=0, tiled=True
    )
    expert_grads = (grad_gate_w, grad_up_w, grad_down_w)
    sent_back = lax.all_to_all(
        back_rows, "expert", split_axis=0, concat_axis=0, tiled=True
    ).reshape(expert_count * capacity, D)
    grad_ffn = jnp.einsum(
        "tj,tjd->td",
        kept_route.astype(jnp.bfloat16),
        sent_back[flat_index],
        preferred_element_type=jnp.float32,
    )
    grad_ffn = grad_ffn + jnp.einsum(
        "te,de->td", grad_logits_low, router_back, preferred_element_type=jnp.float32
    )
    grad_router_w = jnp.einsum(
        "td,te->de", ffn_low, grad_logits_low, preferred_element_type=jnp.float32
    )
    grad_hidden_part, grad_gain_ffn = ffn_norm_back(grad_ffn)
    grad_hidden_state = grad_layer + grad_hidden_part
    grad_attn_low = grad_hidden_state.astype(jnp.bfloat16)
    grad_out_w = jnp.einsum(
        "td,te->de", mixed_low, grad_attn_low, preferred_element_type=jnp.float32
    )
    grad_mixed = jnp.einsum(
        "te,de->td", grad_attn_low, out_back, preferred_element_type=jnp.float32
    )
    grad_mixed = grad_mixed.astype(jnp.bfloat16).reshape(row_count, HEADS, HEAD)
    scores_again = (
        jnp.einsum("qhd,khd->hqk", queries, keys_low, preferred_element_type=jnp.float32)
        * score_scale
    )
    probs_again = jnp.where(allowed[None], jnp.exp(scores_again - log_total), 0.0)
    grad_values = jnp.einsum(
        "hqk,qhd->khd",
        probs_again.astype(jnp.bfloat16),
        grad_mixed,
        preferred_element_type=jnp.float32,
    )
    grad_attn_probs = jnp.einsum(
        "qhd,khd->hqk", grad_mixed, values_low, preferred_element_type=jnp.float32
    )
    grad_scores = probs_again * (
        grad_attn_probs - jnp.sum(probs_again * grad_attn_probs, axis=-1, keepdims=True)
    )
    grad_scores_low = grad_scores.astype(jnp.bfloat16)
    grad_queries = (
        jnp.einsum("hqk,khd->qhd", grad_scores_low, keys_low, preferred_element_type=jnp.float32)
        * score_scale
    )
    grad_keys = (
        jnp.einsum("hqk,qhd->khd", grad_scores_low, queries, preferred_element_type=jnp.float32)
        * score_scale
    )
    grad_query_part, grad_key_part, grad_gain_query, grad_gain_key = query_key_back(
        (grad_queries, grad_keys)
    )
    grad_projected = jnp.concatenate(
        [grad_query_part, grad_key_part, grad_values.reshape(row_count, D)], axis=1
    ).astype(jnp.bfloat16)
    grad_qkv_w = jnp.einsum("td,te->de", normed, grad_projected, preferred_element_type=jnp.float32)
    grad_normed = jnp.einsum(
        "te,de->td", grad_projected, qkv_back, preferred_element_type=jnp.float32
    )
    grad_input_part, grad_gain_attn = attn_norm_back(grad_normed)
    grad_inputs = grad_hidden_state + grad_input_part
    grad_gain_rows = jnp.stack([grad_gain_attn, grad_gain_query, grad_gain_key, grad_gain_ffn])
    mixer_grads = (
        lax.psum_scatter(grad_qkv_w, ("dp", "expert"), scatter_dimension=0, tiled=True),
        lax.psum_scatter(grad_out_w, ("dp", "expert"), scatter_dimension=0, tiled=True),
        lax.psum_scatter(grad_router_w, ("dp", "expert"), scatter_dimension=0, tiled=True),
        lax.psum_scatter(grad_gain_rows, ("dp", "expert"), scatter_dimension=1, tiled=True),
    )
    return (
        result,
        grad_inputs[None],
        mixer_grads[0],
        mixer_grads[1],
        mixer_grads[2],
        mixer_grads[3],
        expert_grads[0],
        expert_grads[1],
        expert_grads[2],
        balance,
    )


MESH = pl.DeviceIdType.MESH


class Grid:
    def __init__(self, dims, cores=False):
        self.cores = cores
        self.dims = ((2,) if cores else ()) + tuple(dims)
        self.size = math.prod(self.dims)
        self.strides = [math.prod(self.dims[d + 1 :]) for d in range(len(self.dims))]
        self.lanes = {}
        for d in range(len(self.dims)):
            for side in self.sides(d):
                self.lanes[(d, side)] = len(self.lanes)

    def coords(self):
        expert = lax.axis_index("expert")
        c = [lax.axis_index("dp")] if self.cores else []
        first = len(c)
        for d in range(first, len(self.dims)):
            c.append(lax.rem(expert // self.strides[d], self.dims[d]))
        return c

    def rels(self, d):
        n = self.dims[d]
        if n == 1:
            return []
        if n == 2:
            return [(1, 0)]
        return [(k, side) for k in range(1, n) for side in (-1, 1)]

    def sides(self, d):
        n = self.dims[d]
        return [] if n == 1 else [0] if n == 2 else [-1, 1]

    def at(self, c, d, rel):
        k, side = rel
        return 1 - c[d] if side == 0 else c[d] + side * k

    def valid(self, c, d, rel):
        k, side = rel
        if side == 0:
            return None
        return c[d] - k >= 0 if side < 0 else c[d] + k < self.dims[d]

    def index(self, coords):
        return sum(x * s for x, s in zip(coords, self.strides))

    def neighbor(self, c, d, side):
        other = list(c)
        other[d] = self.at(c, d, (1, side))
        ok = self.valid(c, d, (1, side))
        if self.cores and d == 0:
            return {"dp": other[0]}, ok
        first = 1 if self.cores else 0
        expert = sum(x * s for x, s in zip(other[first:], self.strides[first:]))
        return {"expert": expert}, ok

    def events(self, order):
        return [
            dict(zip(order, combo))
            for combo in itertools.product(*[[None] + self.rels(d) for d in order])
        ]

    def place(self, c, order, event):
        pred, o, last = None, list(c), -1
        for i, d in enumerate(order):
            if event[d]:
                pred = both(pred, self.valid(c, d, event[d]))
                o[d] = self.at(c, d, event[d])
                last = i
        return o, pred, last


def both(a, b):
    if a is None:
        return b
    if b is None:
        return a
    return jnp.logical_and(a, b)


def when(pred, f):
    if pred is None:
        f()
    else:
        pl.when(pred)(f)


def greet(grid, c):
    barrier = pltpu.get_barrier_semaphore()
    total = jnp.int32(0)
    for d, side in grid.lanes:
        device, ok = grid.neighbor(c, d, side)
        when(
            ok,
            lambda device=device: pl.semaphore_signal(
                barrier, inc=1, device_id=device, device_id_type=MESH
            ),
        )
        total = total + (1 if ok is None else ok.astype(jnp.int32))
    pl.semaphore_wait(barrier, total)


def farthest(order, event):
    return tuple(event[d][0] if event[d] else 0 for d in reversed(order))


class Beside:
    def __init__(self, ins=(), in_specs=(), outs=(), scratch=(), steps=None, lead=0.0, span=1.0):
        self.lead, self.span = lead, span
        self.ins, self.in_specs, self.outs, self.scratch = ins, in_specs, outs, scratch
        self.steps = steps

    def share(self, refs, count, own_scratch):
        cuts = [count, len(self.ins), count, len(self.outs), own_scratch, len(self.scratch)]
        groups, at = [], 0
        for n in cuts:
            groups.append(refs[at : at + n])
            at += n
        steps = self.steps(groups[1], groups[3], groups[5]) if self.steps else []
        return groups[0], groups[2], groups[4], steps


def mingle(events, steps, free, lead, span):
    for event in events[:free]:
        event()
    first = round(lead * len(steps))
    for step in steps[:first]:
        step()
    rest, left = events[free:], steps[first:]
    done = 0
    for n, event in enumerate(rest):
        event()
        while done < len(left) and done * len(rest) * span < (n + 1) * len(left):
            left[done]()
            done += 1
    for step in left[done:]:
        step()


def gather_kernel(grid, parts, count, beside, *refs):
    srcs, outs, (send_sem, recv_sem, own_sem), steps = beside.share(refs, count, 3)
    c = grid.coords()
    me = grid.index(c)
    own = [pltpu.make_async_copy(s, o.at[me], own_sem.at[i]) for i, (s, o) in enumerate(zip(srcs, outs))]
    for copy in own:
        copy.start()
    greet(grid, c)
    sent = []

    def piece(p, ref):
        _, row0, rows, _ = parts[p]
        return ref.at[pl.ds(row0, rows)]

    def push(p, origin, source, d, side, pred):
        device, ok = grid.neighbor(c, d, side)
        pred = both(pred, ok)
        copy = pltpu.make_async_remote_copy(
            src_ref=source,
            dst_ref=piece(p, outs[parts[p][0]].at[origin]),
            send_sem=send_sem.at[p, origin, grid.lanes[(d, side)]],
            recv_sem=recv_sem.at[p, origin],
            device_id=device,
            device_id_type=MESH,
        )
        when(pred, copy.start)
        sent.append((pred, copy))

    todo = []
    for p, (_, _, _, order) in enumerate(parts):
        for event in grid.events(order):
            todo.append((farthest(order, event), p, event))
    todo.sort(key=lambda t: t[:2])

    def handle(p, event):
        a, _, _, order = parts[p]
        o, pred, last = grid.place(c, order, event)
        origin = grid.index(o)
        if last < 0:
            source = piece(p, srcs[a])
        else:
            source = piece(p, outs[a].at[origin])
            arrival = pltpu.make_async_remote_copy(
                src_ref=source,
                dst_ref=source,
                send_sem=send_sem.at[p, origin, 0],
                recv_sem=recv_sem.at[p, origin],
                device_id={"expert": lax.axis_index("expert")},
                device_id_type=MESH,
            )
            when(pred, arrival.wait_recv)
            side = event[order[last]][1]
            if side:
                push(p, origin, source, order[last], -side, pred)
        for d in order[last + 1 :]:
            for side in grid.sides(d):
                push(p, origin, source, d, side, pred)

    mingle(
        [functools.partial(handle, p, event) for _, p, event in todo],
        steps,
        sum(not any(event.values()) for _, _, event in todo),
        beside.lead,
        beside.span,
    )
    for pred, copy in sent:
        when(pred, copy.wait_send)
    for copy in own:
        copy.wait()


def gather(arrays, grid, parts, cid, beside=Beside(), vmem=16 << 20):
    n, count = grid.size, len(arrays)
    return pl.pallas_call(
        functools.partial(gather_kernel, grid, parts, count, beside),
        out_shape=[jax.ShapeDtypeStruct((n,) + x.shape, x.dtype) for x in arrays] + list(beside.outs),
        in_specs=[pl.BlockSpec(memory_space=pl.ANY)] * count + list(beside.in_specs),
        out_specs=[pl.BlockSpec(memory_space=pl.ANY)] * (count + len(beside.outs)),
        scratch_shapes=[
            pltpu.SemaphoreType.DMA((len(parts), n, len(grid.lanes))),
            pltpu.SemaphoreType.DMA((len(parts), n)),
            pltpu.SemaphoreType.DMA((count,)),
        ]
        + list(beside.scratch),
        compiler_params=pltpu.CompilerParams(
            collective_id=cid, has_side_effects=True, vmem_limit_bytes=vmem
        ),
    )(*arrays, *beside.ins)


def landing_slots(grid, order):
    base, total, earlier = {}, 0, 1
    for d in order:
        base[d] = total
        total += len(grid.rels(d)) * earlier
        earlier *= grid.dims[d]
    return base, total


def scatter_kernel(grid, parts, count, beside, *refs):
    k = len(parts)
    srcs, outs, scratch, steps = beside.share(refs, count, 2 * k + count + 4)
    held, mine, totals = scratch[:k], scratch[k : 2 * k], scratch[2 * k : 2 * k + count]
    send_sem, recv_sem, mine_sem, out_sem = scratch[2 * k + count :]
    c = grid.coords()

    def piece(p, ref):
        _, row0, rows, _ = parts[p]
        return ref.at[pl.ds(row0, rows)]

    def own_slot(order, o):
        slot = 0
        for d in order[:-1]:
            slot = slot * grid.dims[d] + o[d]
        return slot

    def landing(order, d, rel, o):
        base, _ = landing_slots(grid, order)
        slot = grid.rels(d).index(rel)
        for q in order[: order.index(d)]:
            slot = slot * grid.dims[q] + o[q]
        return base[d] + slot

    def own_copy(p, o):
        a, _, _, order = parts[p]
        slot = own_slot(order, o)
        return pltpu.make_async_copy(
            piece(p, srcs[a].at[grid.index(o)]), mine[p].at[slot], mine_sem.at[p, slot]
        )

    for p, (_, _, _, order) in enumerate(parts):
        for position in itertools.product(*[range(grid.dims[d]) for d in order[:-1]]):
            o = list(c)
            for d, v in zip(order[:-1], position):
                o[d] = v
            own_copy(p, o).start()
    greet(grid, c)
    todo = []
    for p, (_, _, _, order) in enumerate(parts):
        for event in grid.events(order):
            todo.append((tuple(-far for far in farthest(order, event)), p, event))
    todo.sort(key=lambda t: t[:2])
    sent = []

    def handle(p, event):
        a, row0, rows, order = parts[p]
        o, pred, last = grid.place(c, order, event)
        always, sometimes = [], []
        if last >= 0:
            far, side = event[order[last]]
            if side and far + 1 < grid.dims[order[last]]:
                _, ok = grid.neighbor(c, order[last], -side)
                sometimes.append((landing(order, order[last], (far + 1, side), o), ok))
        for d in order[last + 1 :]:
            for side in grid.sides(d):
                _, ok = grid.neighbor(c, d, side)
                slot = landing(order, d, (1, -side), o)
                if ok is None:
                    always.append(slot)
                else:
                    sometimes.append((slot, ok))
        final = last < 0
        if not always and not sometimes and not final:
            source = piece(p, srcs[a].at[grid.index(o)])
        else:
            source = mine[p].at[own_slot(order, o)]
            when(pred, own_copy(p, o).wait)
            steps = [(slot, ok) for slot, ok in sometimes]
            if always or final:
                steps.insert(0, (always, None))

            def add(slots, opening, final=final, source=source, p=p, row0=row0, rows=rows, a=a):
                for slot in slots:
                    landed = held[p].at[slot]
                    pltpu.make_async_remote_copy(
                        src_ref=landed,
                        dst_ref=landed,
                        send_sem=send_sem.at[p, 0],
                        recv_sem=recv_sem.at[p, slot],
                        device_id={"expert": lax.axis_index("expert")},
                        device_id_type=MESH,
                    ).wait_recv()
                tile = min(16, rows)

                @pl.loop(0, rows // tile)
                def _(t):
                    here = pl.ds(pl.multiple_of(t * tile, tile), tile)
                    there = pl.ds(pl.multiple_of(row0 + t * tile, tile), tile)
                    if final and not opening:
                        value = totals[a][there, :]
                    else:
                        value = source[here, :].astype(jnp.float32)
                    for slot in slots:
                        value = value + held[p][slot, here, :].astype(jnp.float32)
                    if final:
                        totals[a][there, :] = value
                    else:
                        source[here, :] = value.astype(source.dtype)

            for n, (slots, ok) in enumerate(steps):
                slots = slots if isinstance(slots, list) else [slots]
                when(both(pred, ok), functools.partial(add, slots, n == 0))
        if last >= 0:
            d = order[last]
            device, _ = grid.neighbor(c, d, event[d][1])
            slot = landing(order, d, event[d], o)
            copy = pltpu.make_async_remote_copy(
                src_ref=source,
                dst_ref=held[p].at[slot],
                send_sem=send_sem.at[p, slot],
                recv_sem=recv_sem.at[p, slot],
                device_id=device,
                device_id_type=MESH,
            )
            when(pred, copy.start)
            sent.append((pred, copy))

    mingle(
        [functools.partial(handle, p, event) for _, p, event in todo],
        steps,
        sum(event[parts[p][3][-1]] is not None for _, p, event in todo),
        beside.lead,
        beside.span,
    )
    done = [pltpu.make_async_copy(t, o, out_sem.at[i]) for i, (t, o) in enumerate(zip(totals, outs))]
    for copy in done:
        copy.start()
    for pred, copy in sent:
        when(pred, copy.wait_send)
    for copy in done:
        copy.wait()


def scatter(arrays, grid, parts, cid, beside=Beside()):
    count = len(arrays)
    slots = [landing_slots(grid, order)[1] for _, _, _, order in parts]
    mine = [grid.size // grid.dims[order[-1]] for _, _, _, order in parts]
    blocks = [((rows, arrays[a].shape[2]), arrays[a].dtype) for a, _, rows, _ in parts]
    flat = [jax.ShapeDtypeStruct(x.shape[1:], jnp.float32) for x in arrays]
    return pl.pallas_call(
        functools.partial(scatter_kernel, grid, parts, count, beside),
        out_shape=flat + list(beside.outs),
        in_specs=[pl.BlockSpec(memory_space=pl.ANY)] * count + list(beside.in_specs),
        out_specs=[pl.BlockSpec(memory_space=pl.ANY)] * (count + len(beside.outs)),
        scratch_shapes=[pltpu.VMEM((s,) + b, t) for s, (b, t) in zip(slots, blocks)]
        + [pltpu.VMEM((s,) + b, t) for s, (b, t) in zip(mine, blocks)]
        + [pltpu.VMEM(x.shape, x.dtype) for x in flat]
        + [
            pltpu.SemaphoreType.DMA((len(parts), max(slots))),
            pltpu.SemaphoreType.DMA((len(parts), max(slots))),
            pltpu.SemaphoreType.DMA((len(parts), max(mine))),
            pltpu.SemaphoreType.DMA((count,)),
        ]
        + list(beside.scratch),
        compiler_params=pltpu.CompilerParams(
            collective_id=cid, has_side_effects=True, vmem_limit_bytes=60 << 20
        ),
    )(*arrays, *beside.ins)


def cut(array, shares, orders):
    starts = [sum(shares[:i]) for i in range(len(shares))]
    return tuple((array, start, share, order) for start, share, order in zip(starts, shares, orders))


def each_tile(total, width, f):
    @pl.loop(0, total // width)
    def _(t):
        f(pl.ds(pl.multiple_of(t * width, width), width))


def dot(left, right):
    return jnp.dot(left, right, preferred_element_type=jnp.float32)


def dot_across(left, right):
    return lax.dot_general(left, right, (((1,), (1,)), ((), ())), preferred_element_type=jnp.float32)


class Move:
    def __init__(self, *refs):
        self.refs = refs

    def start(self):
        pltpu.make_async_copy(*self.refs).start()

    def wait(self):
        pltpu.make_async_copy(*self.refs).wait()


ANYWHERE = pl.BlockSpec(memory_space=pl.ANY)
ON_CORE = pl.BlockSpec(memory_space=pltpu.VMEM)


def weight_copies(halves, held, sem):
    gate_own, gate_far, up_own, up_far, down_own, down_far = halves
    gate, up, down = held
    half = gate.shape[1] // 2
    own, far = pl.ds(0, half), pl.ds(half, half)
    pairs = [
        (gate_own, gate.at[:, own]),
        (gate_far, gate.at[:, far]),
        (up_own, up.at[:, own]),
        (up_far, up.at[:, far]),
        (down_own, down.at[own, :]),
        (down_far, down.at[far, :]),
    ]
    return [Move(a, b, sem.at[i]) for i, (a, b) in enumerate(pairs)]


def pick_of(ranks, row, capacity):
    line = ranks[row : row + 1, :]
    slot = lax.broadcasted_iota(jnp.int32, (capacity, line.shape[1]), 0).astype(jnp.float32)
    return line == slot


def put_of(ranks, row, capacity):
    line = ranks[:, row : row + 1]
    slot = lax.broadcasted_iota(jnp.int32, (line.shape[0], capacity), 1).astype(jnp.float32)
    return (line == slot).astype(jnp.float32).astype(jnp.bfloat16)


def forward_beside(ffn_rows, rank_rows, rank_cols, weight_cols, halves, capacity):
    row_count, tokens, width = ffn_rows.shape
    hidden = 2 * halves[0].shape[1]
    pairs, pair = row_count // 2, 2 * capacity
    slots = row_count * capacity
    low, full = jnp.bfloat16, jnp.float32

    def steps(ins, outs, scratch):
        ffn_in, ranks, ranks_t, weights_t = ins[:4]
        weights, (ffn, xs, pre, units, out, mix), sems = scratch[:3], scratch[3:9], scratch[9:]
        load_sem, row_sem, out_sem = sems
        heavy = weight_copies(ins[4:], weights, load_sem)
        gate_w, up_w, down_w = weights

        def load(q):
            return Move(ffn_in.at[pl.ds(2 * q, 2)], ffn.at[q % 2], row_sem.at[q % 2])

        def leave(q):
            here = pl.ds(q * pair, pair)
            moves = [
                (xs, outs[0].at[here]),
                (pre.at[0], outs[1].at[here]),
                (pre.at[1], outs[2].at[here]),
                (units, outs[3].at[here]),
                (out, outs[4].at[here]),
                (mix, outs[5].at[pl.ds(2 * q, 2)]),
            ]
            return [Move(a, b, out_sem.at[i]) for i, (a, b) in enumerate(moves)]

        def opening():
            for copy in heavy:
                copy.start()
            load(0).start()

        def choose(q):
            load(q).wait()
            if q + 1 < pairs:
                load(q + 1).start()
            if q:
                leave(q - 1)[0].wait()
            for i in range(2):
                pick = pick_of(ranks, 2 * q + i, capacity).astype(full).astype(low)
                rows = pl.ds(i * capacity, capacity)

                def tile(cols, i=i, pick=pick, rows=rows):
                    xs[rows, cols] = dot(pick, ffn[q % 2, i, :, cols]).astype(low)

                each_tile(width, 512, tile)
            leave(q)[0].start()

        def widen(q):
            if q == 0:
                for copy in heavy[:4]:
                    copy.wait()
            else:
                for copy in leave(q - 1)[1:4]:
                    copy.wait()

            def tile(cols):
                gate = dot(xs[...], gate_w[:, cols])
                up = dot(xs[...], up_w[:, cols])
                pre[0, :, cols] = gate
                pre[1, :, cols] = up
                units[:, cols] = (gate * jax.nn.sigmoid(gate) * up).astype(low)

            each_tile(hidden, 256, tile)
            for copy in leave(q)[1:4]:
                copy.start()

        def narrow(q):
            if q == 0:
                for copy in heavy[4:]:
                    copy.wait()
            else:
                for copy in leave(q - 1)[4:]:
                    copy.wait()
            puts = [put_of(ranks_t, 2 * q + i, capacity) for i in range(2)]
            scales = [weights_t[:, 2 * q + i : 2 * q + i + 1] for i in range(2)]

            def tile(cols):
                value = dot(units[...], down_w[:, cols]).astype(low)
                out[:, cols] = value
                for i in range(2):
                    part = dot(puts[i], value[i * capacity : (i + 1) * capacity]) * scales[i]
                    mix[i, :, cols] = part.astype(low)

            each_tile(width, 256, tile)
            for copy in leave(q)[4:]:
                copy.start()

        def closing():
            for copy in leave(pairs - 1):
                copy.wait()

        listed = [opening]
        for q in range(pairs):
            listed += [functools.partial(f, q) for f in (choose, widen, narrow)]
        return listed + [closing]

    return Beside(
        ins=(ffn_rows, rank_rows, rank_cols, weight_cols) + tuple(halves),
        in_specs=(ANYWHERE, ON_CORE, ON_CORE, ON_CORE) + (ANYWHERE,) * 6,
        outs=[
            jax.ShapeDtypeStruct((slots, width), low),
            jax.ShapeDtypeStruct((slots, hidden), full),
            jax.ShapeDtypeStruct((slots, hidden), full),
            jax.ShapeDtypeStruct((slots, hidden), low),
            jax.ShapeDtypeStruct((slots, width), low),
            jax.ShapeDtypeStruct((row_count, tokens, width), low),
        ],
        scratch=[
            pltpu.VMEM((width, hidden), low),
            pltpu.VMEM((width, hidden), low),
            pltpu.VMEM((hidden, width), low),
            pltpu.VMEM((2, 2, tokens, width), low),
            pltpu.VMEM((pair, width), low),
            pltpu.VMEM((2, pair, hidden), full),
            pltpu.VMEM((pair, hidden), low),
            pltpu.VMEM((pair, width), low),
            pltpu.VMEM((2, tokens, width), low),
            pltpu.SemaphoreType.DMA((6,)),
            pltpu.SemaphoreType.DMA((2,)),
            pltpu.SemaphoreType.DMA((6,)),
        ],
        steps=steps,
        lead=0.2,
        span=0.5,
    )


def backward_beside(cot_rows, rank_rows, rank_cols, weight_rows, gate_pre, up_pre, expert_out, halves, capacity):
    row_count, tokens, width = cot_rows.shape
    hidden = 2 * halves[0].shape[1]
    pairs, pair = row_count // 2, 2 * capacity
    slots = row_count * capacity
    low, full = jnp.bfloat16, jnp.float32

    def steps(ins, outs, scratch):
        cot_in, ranks, ranks_t, weights, gate_in, up_in, out_in = ins[:7]
        heavy_refs, (cot, ge, pre, out, gg, gu, gx, dots, sums), sems = scratch[:3], scratch[3:12], scratch[12:]
        load_sem, row_sem, out_sem = sems
        heavy = weight_copies(ins[7:], heavy_refs, load_sem)
        gate_w, up_w, down_w = heavy_refs

        def load(q):
            return Move(cot_in.at[pl.ds(2 * q, 2)], cot.at[q % 2], row_sem.at[q % 2])

        def fetch(q):
            here = pl.ds(q * pair, pair)
            moves = [(out_in, out), (gate_in, pre.at[0]), (up_in, pre.at[1])]
            return [Move(a.at[here], b, row_sem.at[2 + i]) for i, (a, b) in enumerate(moves)]

        def leave(q):
            here = pl.ds(q * pair, pair)
            moves = [(ge, outs[0].at[here]), (gg, outs[1].at[here]), (gu, outs[2].at[here])]
            moves.append((gx, outs[3].at[pl.ds(2 * q, 2)]))
            return [Move(a, b, out_sem.at[i]) for i, (a, b) in enumerate(moves)]

        last = Move(dots, outs[4], out_sem.at[4])

        def opening():
            load(0).start()
            for copy in fetch(0):
                copy.start()
            for copy in heavy:
                copy.start()

        def choose(q):
            load(q).wait()
            fetch(q)[0].wait()
            if q + 1 < pairs:
                load(q + 1).start()
            if q:
                leave(q - 1)[0].wait()
            for i in range(2):
                row = 2 * q + i
                pick = pick_of(ranks, row, capacity)
                pick_low = pick.astype(full).astype(low)
                scale = jnp.sum(jnp.where(pick, weights[row : row + 1, :], 0.0), axis=1, keepdims=True)
                rows = pl.ds(i * capacity, capacity)
                sums[...] = jnp.zeros_like(sums)

                def tile(cols, i=i, pick_low=pick_low, scale=scale, rows=rows):
                    value = dot(pick_low, cot[q % 2, i, :, cols])
                    ge[rows, cols] = (value * scale).astype(low)
                    product = value * out[rows, cols].astype(full)
                    total = product[:, :128]
                    for lane in range(128, product.shape[1], 128):
                        total = total + product[:, lane : lane + 128]
                    sums[...] += total

                each_tile(width, 512, tile)
                slot_dot = jnp.sum(sums[...], axis=1, keepdims=True)
                dots[row : row + 1, :] = jnp.sum(jnp.where(pick, slot_dot, 0.0), axis=0, keepdims=True)
            leave(q)[0].start()
            if q + 1 < pairs:
                fetch(q + 1)[0].start()

        def narrow(q):
            for copy in fetch(q)[1:]:
                copy.wait()
            if q == 0:
                for copy in heavy:
                    copy.wait()
            else:
                for copy in leave(q - 1)[1:3]:
                    copy.wait()

            def tile(cols):
                grad = dot_across(ge[...], down_w[cols, :])
                gate, up = pre[0, :, cols], pre[1, :, cols]
                sigmoid = jax.nn.sigmoid(gate)
                gg[:, cols] = (grad * up * sigmoid * (1.0 + gate * (1.0 - sigmoid))).astype(low)
                gu[:, cols] = (grad * gate * sigmoid).astype(low)

            each_tile(hidden, 256, tile)
            for copy in leave(q)[1:3]:
                copy.start()
            if q + 1 < pairs:
                for copy in fetch(q + 1)[1:]:
                    copy.start()

        def widen(q):
            if q:
                leave(q - 1)[3].wait()
            puts = [put_of(ranks_t, 2 * q + i, capacity) for i in range(2)]

            def tile(cols):
                value = dot_across(gg[...], gate_w[cols, :]) + dot_across(gu[...], up_w[cols, :])
                value = value.astype(low)
                for i in range(2):
                    part = dot(puts[i], value[i * capacity : (i + 1) * capacity])
                    gx[i, :, cols] = part.astype(low)

            each_tile(width, 256, tile)
            leave(q)[3].start()

        def closing():
            last.start()
            for copy in leave(pairs - 1):
                copy.wait()
            last.wait()

        listed = [opening]
        for q in range(pairs):
            listed += [functools.partial(f, q) for f in (choose, narrow, widen)]
        return listed + [closing]

    return Beside(
        ins=(cot_rows, rank_rows, rank_cols, weight_rows, gate_pre, up_pre, expert_out) + tuple(halves),
        in_specs=(ANYWHERE, ON_CORE, ON_CORE, ON_CORE) + (ANYWHERE,) * 9,
        outs=[
            jax.ShapeDtypeStruct((slots, width), low),
            jax.ShapeDtypeStruct((slots, hidden), low),
            jax.ShapeDtypeStruct((slots, hidden), low),
            jax.ShapeDtypeStruct((row_count, tokens, width), low),
            jax.ShapeDtypeStruct((row_count, tokens), full),
        ],
        scratch=[
            pltpu.VMEM((width, hidden), low),
            pltpu.VMEM((width, hidden), low),
            pltpu.VMEM((hidden, width), low),
            pltpu.VMEM((2, 2, tokens, width), low),
            pltpu.VMEM((pair, width), low),
            pltpu.VMEM((2, pair, hidden), full),
            pltpu.VMEM((pair, width), low),
            pltpu.VMEM((pair, hidden), low),
            pltpu.VMEM((pair, hidden), low),
            pltpu.VMEM((2, tokens, width), low),
            pltpu.VMEM((row_count, tokens), full),
            pltpu.VMEM((capacity, 128), full),
            pltpu.SemaphoreType.DMA((6,)),
            pltpu.SemaphoreType.DMA((5,)),
            pltpu.SemaphoreType.DMA((5,)),
        ],
        steps=steps,
        span=0.8,
    )


def outer_beside(rows_in, grad_rows, grad_gate, grad_up, units):
    slots, width = rows_in.shape
    hidden = units.shape[1]
    half = hidden // 2
    block = 256
    low, full = jnp.bfloat16, jnp.float32

    def steps(ins, outs, scratch):
        rows_ref, grads_ref, gate_ref, up_ref, units_ref = ins
        left, turned, gate, up, grads, wide_own, wide_far, tall_own, tall_far, load_sem, left_sem, out_sem = scratch
        heavy = [
            Move(a, b, load_sem.at[i])
            for i, (a, b) in enumerate([(gate_ref, gate), (up_ref, up), (grads_ref, grads)])
        ]
        jobs = [(rows_ref, t) for t in range(width // block)] + [
            (units_ref, t) for t in range(hidden // block)
        ]

        def load(n):
            ref, t = jobs[n]
            return Move(
                ref.at[:, pl.ds(t * block, block)], left.at[n % 2], left_sem.at[n % 2]
            )

        def turn(n):
            load(n).wait()
            if n + 1 < len(jobs):
                load(n + 1).start()

            @pl.loop(0, slots // block)
            def _(k):
                here = pl.ds(pl.multiple_of(k * block, block), block)
                turned[:, here] = left[n % 2, here, :].astype(full).T.astype(low)

        def leave_wide(which, t):
            here = pl.ds(t * block, block)
            return [
                Move(wide_own.at[which], outs[2 * which].at[here], out_sem.at[2 * which]),
                Move(wide_far.at[which], outs[2 * which + 1].at[here], out_sem.at[2 * which + 1]),
            ]

        def leave_tall(t):
            far = t * block >= half
            here = pl.ds(t * block - (half if far else 0), block)
            return Move(
                tall_far if far else tall_own, outs[5 if far else 4].at[here], out_sem.at[5 if far else 4]
            )

        def wide(which, t):
            right = (gate, up)[which]
            if t == 0:
                heavy[which].wait()
            else:
                for copy in leave_wide(which, t - 1):
                    copy.wait()

            def own(cols):
                wide_own[which, :, cols] = dot(turned[...], right[:, cols])

            each_tile(half, 256, own)

            @pl.loop(0, half // 256)
            def _(k):
                cols = pl.ds(pl.multiple_of(k * 256, 256), 256)
                there = pl.ds(pl.multiple_of(half + k * 256, 256), 256)
                wide_far[which, :, cols] = dot(turned[...], right[:, there]).astype(low)

            for copy in leave_wide(which, t):
                copy.start()

        def tall(t):
            far = t * block >= half
            if t == 0:
                heavy[2].wait()
            if t * block not in (0, half):
                leave_tall(t - 1).wait()

            def tile(cols):
                value = dot(turned[...], grads[:, cols])
                if far:
                    tall_far[:, cols] = value.astype(low)
                else:
                    tall_own[:, cols] = value

            each_tile(width, 256, tile)
            leave_tall(t).start()

        def opening():
            load(0).start()
            for copy in heavy:
                copy.start()

        def closing():
            for which in range(2):
                for copy in leave_wide(which, width // block - 1):
                    copy.wait()
            leave_tall(half // block - 1).wait()
            leave_tall(hidden // block - 1).wait()

        listed = [opening]
        for n, (ref, t) in enumerate(jobs):
            listed.append(functools.partial(turn, n))
            if n < width // block:
                listed += [functools.partial(wide, which, t) for which in range(2)]
            else:
                listed.append(functools.partial(tall, t))
        return listed + [closing]

    return Beside(
        ins=(rows_in, grad_rows, grad_gate, grad_up, units),
        in_specs=(ANYWHERE,) * 5,
        outs=[
            jax.ShapeDtypeStruct((width, half), full),
            jax.ShapeDtypeStruct((width, half), low),
            jax.ShapeDtypeStruct((width, half), full),
            jax.ShapeDtypeStruct((width, half), low),
            jax.ShapeDtypeStruct((half, width), full),
            jax.ShapeDtypeStruct((half, width), low),
        ],
        scratch=[
            pltpu.VMEM((2, slots, block), low),
            pltpu.VMEM((block, slots), low),
            pltpu.VMEM((slots, hidden), low),
            pltpu.VMEM((slots, hidden), low),
            pltpu.VMEM((slots, width), low),
            pltpu.VMEM((2, block, half), full),
            pltpu.VMEM((2, block, half), low),
            pltpu.VMEM((block, width), full),
            pltpu.VMEM((block, width), low),
            pltpu.SemaphoreType.DMA((3,)),
            pltpu.SemaphoreType.DMA((2,)),
            pltpu.SemaphoreType.DMA((6,)),
        ],
        steps=steps,
        span=0.6,
    )


def gathered_body(
    dims,
    tokens,
    w_qkv,
    w_out,
    w_router,
    gains,
    w_gate,
    w_up,
    w_down,
    lengths,
    routes,
    send_counts,
    cotangent,
):
    row_count = tokens.shape[1]
    top_count = routes.shape[2]
    expert_count = w_router.shape[1]
    owners = math.prod(dims)
    weight_rows = w_qkv.shape[0]
    capacity = row_count * top_count // expert_count
    slots_all = row_count * 2 * owners
    balance_factor = float(expert_count) / (float(top_count) * float(slots_all) * float(slots_all))
    score_scale = HEAD ** (-0.5)
    low = jnp.bfloat16
    full = jnp.float32
    chips = Grid(dims)
    devices = Grid(dims, cores=True)
    z, y, x = 0, 1, 2
    row_orders = [(x, z, y), (y, z, x), (z, x, y), (z, y, x)]
    row_shares = [5 * row_count // 16, 5 * row_count // 16, 3 * row_count // 16, 3 * row_count // 16]
    quarter = [weight_rows // 4] * 4
    wide_orders = [tuple(d + 1 for d in order) + (0,) for order in row_orders]
    expert = lax.axis_index("expert")
    core = lax.axis_index("dp")
    swap = [(0, 1), (1, 0)]

    small = jnp.concatenate(
        [w_router, gains.T, jnp.zeros((weight_rows, 128 - expert_count - 4), low)], axis=1
    )
    qkv_all, out_all, small_all = gather(
        [w_qkv, w_out, small],
        devices,
        cut(0, quarter, wide_orders)
        + cut(1, quarter, wide_orders[:2] * 2)
        + cut(2, [weight_rows], wide_orders[2:3]),
        1,
    )
    qkv_weight = qkv_all.reshape(D, 3 * D)
    out_weight = out_all.reshape(D, D)
    small_all = small_all.reshape(D, 128)
    router_weight = small_all[:, :expert_count]
    gain_float = small_all[:, expert_count : expert_count + 4].T.astype(full)
    gate_own, up_own, down_own = w_gate[0], w_up[0], w_down[0]
    gate_far, up_far, down_far = (lax.ppermute(w, "dp", swap) for w in (gate_own, up_own, down_own))

    positions = jnp.arange(row_count, dtype=jnp.int32)
    live_slots = positions < lengths[0]
    live_float = live_slots.astype(full)[:, None]
    expert_ids = jnp.arange(expert_count, dtype=jnp.int32)
    named = jnp.any(routes[0][:, :, None] == expert_ids, axis=1) & live_slots[:, None]
    before = (positions[None, :] < positions[:, None]).astype(low)
    rank = jnp.dot(before, named.astype(low), preferred_element_type=full)
    limit = jnp.minimum(send_counts[0], capacity).astype(full)
    kept = named & (rank < limit[None, :])
    kept_rank = jnp.where(kept, rank, -1.0)

    inputs = tokens[0].astype(full)
    attn_in, attn_norm_back = jax.vjp(norm_scale, inputs, gain_float[0])
    normed = attn_in.astype(low)
    projected = jnp.dot(normed, qkv_weight, preferred_element_type=full)
    (rot_query, rot_keys), query_key_back = jax.vjp(
        query_key, projected[:, :D], projected[:, D : 2 * D], gain_float[1], gain_float[2]
    )
    queries = rot_query.astype(low)
    keys_low = rot_keys.astype(low)
    values_low = projected[:, 2 * D :].astype(low).reshape(row_count, HEADS, HEAD)
    allowed = (positions[None, :] <= positions[:, None]) & live_slots[None, :]
    scores = jnp.einsum("qhd,khd->hqk", queries, keys_low, preferred_element_type=full) * score_scale
    scores = jnp.where(allowed[None], scores, -1e30)
    highest = jnp.max(scores, axis=-1, keepdims=True)
    expo_scores = jnp.exp(scores - highest)
    totals = jnp.sum(expo_scores, axis=-1, keepdims=True)
    attn_probs = expo_scores / totals
    log_total = highest + jnp.log(totals)
    mixed_heads = jnp.einsum("hqk,khd->qhd", attn_probs.astype(low), values_low, preferred_element_type=full)
    mixed_low = mixed_heads.reshape(row_count, D).astype(low)
    hidden_state = inputs + jnp.dot(mixed_low, out_weight, preferred_element_type=full)
    ffn_in, ffn_norm_back = jax.vjp(norm_scale, hidden_state, gain_float[3])
    ffn_low = ffn_in.astype(low)
    logits = jnp.dot(ffn_low, router_weight, preferred_element_type=full)
    router_probs = jax.nn.softmax(logits, axis=-1)
    prob_local = jnp.sum(router_probs * live_float, axis=0)
    sums = jnp.concatenate([send_counts[0].astype(full), prob_local])
    aside = jnp.concatenate(
        [
            jnp.where(kept, router_probs, 0.0).T,
            kept_rank.T,
            jnp.pad(sums[None, :], ((0, 7), (0, row_count - 2 * expert_count))),
        ],
        axis=0,
    )

    ffn_rows, aside_rows = gather(
        [ffn_low, aside],
        chips,
        cut(0, row_shares, row_orders) + cut(1, [aside.shape[0]], row_orders[2:3]),
        3,
    )
    sums_core = jnp.sum(aside_rows[:, 2 * expert_count, : 2 * expert_count], axis=0)
    sums_all = sums_core + lax.ppermute(sums_core, "dp", swap)
    count_total, prob_total = sums_all[:expert_count], sums_all[expert_count:]
    balance = jnp.sum(count_total * prob_total) * balance_factor
    weight_of = lax.dynamic_index_in_dim(aside_rows, expert, 1, keepdims=False)
    rank_of = lax.dynamic_index_in_dim(aside_rows, expert_count + expert, 1, keepdims=False)
    halves = (gate_own, gate_far, up_own, up_far, down_own, down_far)
    cot_rows, rows_in, gate_pre, up_pre, units, expert_out, mixture_part = gather(
        [cotangent[0]],
        chips,
        cut(0, row_shares, row_orders),
        2,
        forward_beside(ffn_rows, rank_of, rank_of.T, weight_of.T, halves, capacity),
        vmem=60 << 20,
    )
    mixture, grad_rows, grad_gate, grad_up, back_part, dot_route = scatter(
        [mixture_part],
        chips,
        cut(0, row_shares, row_orders),
        5,
        backward_beside(
            cot_rows, rank_of, rank_of.T, weight_of, gate_pre, up_pre, expert_out, halves, capacity
        ),
    )
    route_part = jnp.where((expert_ids == expert)[None, :, None], dot_route[:, None, :], 0.0)
    grad_ffn, grad_route, *halves_grads = scatter(
        [back_part, route_part],
        chips,
        cut(0, row_shares, row_orders) + cut(1, [expert_count], row_orders[2:3]),
        4,
        outer_beside(rows_in, grad_rows, grad_gate, grad_up, units),
    )
    expert_grads = [
        (own + lax.ppermute(far, "dp", swap).astype(full))[None]
        for own, far in zip(halves_grads[::2], halves_grads[1::2])
    ]
    result = (live_float * (hidden_state + mixture)).astype(low)[None]

    balance_coef = BALANCE_WEIGHT * balance_factor
    grad_probs = grad_route.T + balance_coef * count_total[None, :] * live_float
    grad_logits = router_probs * (
        grad_probs - jnp.sum(router_probs * grad_probs, axis=-1, keepdims=True)
    )
    grad_logits_low = grad_logits.astype(low)
    grad_ffn = grad_ffn + jnp.einsum("te,de->td", grad_logits_low, router_weight, preferred_element_type=full)
    grad_router_w = jnp.einsum("td,te->de", ffn_low, grad_logits_low, preferred_element_type=full)

    grad_layer = cotangent[0].astype(full) * live_float
    grad_hidden_part, grad_gain_ffn = ffn_norm_back(grad_ffn)
    grad_hidden_state = grad_layer + grad_hidden_part
    grad_attn_low = grad_hidden_state.astype(low)
    grad_mixed = jnp.einsum("te,de->td", grad_attn_low, out_weight, preferred_element_type=full)
    grad_mixed = grad_mixed.astype(low).reshape(row_count, HEADS, HEAD)
    scores_again = jnp.einsum("qhd,khd->hqk", queries, keys_low, preferred_element_type=full) * score_scale
    probs_again = jnp.where(allowed[None], jnp.exp(scores_again - log_total), 0.0)
    grad_values = jnp.einsum("hqk,qhd->khd", probs_again.astype(low), grad_mixed, preferred_element_type=full)
    grad_attn_probs = jnp.einsum("qhd,khd->hqk", grad_mixed, values_low, preferred_element_type=full)
    grad_scores = probs_again * (
        grad_attn_probs - jnp.sum(probs_again * grad_attn_probs, axis=-1, keepdims=True)
    )
    grad_scores_low = grad_scores.astype(low)
    grad_queries = jnp.einsum("hqk,khd->qhd", grad_scores_low, keys_low, preferred_element_type=full) * score_scale
    grad_keys = jnp.einsum("hqk,qhd->khd", grad_scores_low, queries, preferred_element_type=full) * score_scale
    grad_query_part, grad_key_part, grad_gain_query, grad_gain_key = query_key_back(
        (grad_queries, grad_keys)
    )
    grad_projected = jnp.concatenate(
        [grad_query_part, grad_key_part, grad_values.reshape(row_count, D)], axis=1
    ).astype(low)
    grad_normed = jnp.einsum("te,de->td", grad_projected, qkv_weight, preferred_element_type=full)
    grad_input_part, grad_gain_attn = attn_norm_back(grad_normed)
    grad_inputs = grad_hidden_state + grad_input_part
    grad_gain_rows = jnp.stack([grad_gain_attn, grad_gain_query, grad_gain_key, grad_gain_ffn])

    half = D // 2

    def outer(left, right):
        return jnp.einsum("sa,sb->ab", left, right, preferred_element_type=full)

    def core_half(value, side):
        return lax.dynamic_slice_in_dim(value, side * half, half, 1)

    small_grads = jnp.concatenate(
        [grad_router_w, grad_gain_rows.T, jnp.zeros((D, 128 - expert_count - 4), full)], axis=1
    )

    def mixer_grads(side):
        return (
            outer(core_half(normed, side), grad_projected),
            outer(core_half(mixed_low, side), grad_attn_low),
            lax.dynamic_slice_in_dim(small_grads, side * half, half, 0),
        )

    far_qkv, far_out, far_small = mixer_grads(1 - core)
    far_parts = [
        lax.ppermute(g, "dp", swap) for g in (far_qkv.astype(low), far_out.astype(low), far_small)
    ]
    shares = [
        (a + b.astype(full)).astype(b.dtype).reshape(owners, weight_rows, a.shape[1])
        for a, b in zip(mixer_grads(core), far_parts)
    ]
    grad_qkv, grad_out, grad_small = scatter(
        shares,
        chips,
        cut(0, quarter, row_orders)
        + cut(1, quarter, row_orders[:2] * 2)
        + cut(2, [weight_rows], row_orders[2:3]),
        6,
    )
    return (
        result,
        grad_inputs[None],
        grad_qkv,
        grad_out,
        grad_small[:, :expert_count],
        grad_small[:, expert_count : expert_count + 4].T,
        *expert_grads,
        balance,
    )


def solution(mesh):
    dims = {4: (1, 2, 2), 8: (2, 2, 2), 16: (4, 2, 2)}.get(mesh.shape["expert"])
    plan = routed_body if dims is None or mesh.shape["dp"] != 2 else functools.partial(gathered_body, dims)
    placed = (
        P(("dp", "expert"), None, None),
        P(("dp", "expert"), None),
        P(("dp", "expert"), None),
        P(("dp", "expert"), None),
        P(None, ("dp", "expert")),
        P("expert", None, "dp"),
        P("expert", None, "dp"),
        P("expert", "dp", None),
        P(("dp", "expert")),
        P(("dp", "expert"), None, None),
        P(("dp", "expert"), None),
        P(("dp", "expert"), None, None),
    )
    return jax.shard_map(
        plan,
        mesh=mesh,
        in_specs=placed,
        out_specs=(
            P(("dp", "expert"), None, None),
            P(("dp", "expert"), None, None),
            P(("dp", "expert"), None),
            P(("dp", "expert"), None),
            P(("dp", "expert"), None),
            P(None, ("dp", "expert")),
            P("expert", None, "dp"),
            P("expert", None, "dp"),
            P("expert", "dp", None),
            P(),
        ),
        check_vma=False,
    )
```

```python
import functools
import itertools
import math

import jax
import jax.numpy as jnp
from jax import lax
from jax.experimental import pallas as pl
from jax.experimental.pallas import tpu as pltpu
from jax.sharding import PartitionSpec as P

D = 2048
HEADS = 16
HEAD = 128


NORM_EPS = 1e-05
BALANCE_WEIGHT = 0.01


def norm_scale(values, gain_row):
    return (
        values * lax.rsqrt(jnp.mean(values * values, axis=-1, keepdims=True) + NORM_EPS) * gain_row
    )


def rope_tables(positions_count, head_width):
    half_width = head_width // 2
    frequency = jnp.exp(
        jnp.arange(half_width, dtype=jnp.float32) * (-2.0 * math.log(10000.0) / head_width)
    )
    angles = jnp.arange(positions_count, dtype=jnp.float32)[:, None] * frequency[None, :]
    angles = jnp.concatenate([angles, angles], axis=1)
    return (jnp.cos(angles)[:, None, :], jnp.sin(angles)[:, None, :])


def rotate(values, cosine, sine_part):
    half_width = values.shape[-1] // 2
    turned = jnp.concatenate([-values[..., half_width:], values[..., :half_width]], axis=-1)
    return values * cosine + turned * sine_part


def query_key(query_part, key_part, query_gain, key_gain):
    positions_count = query_part.shape[0]
    cosine, sine_part = rope_tables(positions_count, HEAD)
    queries = norm_scale(query_part, query_gain).reshape(positions_count, HEADS, HEAD)
    key_heads = norm_scale(key_part, key_gain).reshape(positions_count, HEADS, HEAD)
    return (rotate(queries, cosine, sine_part), rotate(key_heads, cosine, sine_part))


def expert_forward(rows_in, gate_weight, up_weight, down_weight):
    gate_pre = jnp.einsum(
        "nkcd,kdf->nkcf", rows_in, gate_weight, preferred_element_type=jnp.float32
    )
    up_pre = jnp.einsum("nkcd,kdf->nkcf", rows_in, up_weight, preferred_element_type=jnp.float32)
    hidden_low = (jax.nn.silu(gate_pre) * up_pre).astype(jnp.bfloat16)
    output = jnp.einsum(
        "nkcf,kfd->nkcd", hidden_low, down_weight, preferred_element_type=jnp.float32
    )
    return (gate_pre, up_pre, hidden_low, output)


def routed_body(
    tokens,
    w_qkv,
    w_out,
    w_router,
    gains,
    w_gate,
    w_up,
    w_down,
    lengths,
    routes,
    send_counts,
    cotangent,
):
    row_count = tokens.shape[1]
    top_count = routes.shape[2]
    expert_count = w_router.shape[1]
    owners = lax.axis_size("expert")
    local_experts = expert_count // owners
    capacity = row_count * top_count // expert_count
    slots_all = row_count * lax.axis_size("dp") * owners
    balance_factor = float(expert_count) / (float(top_count) * float(slots_all) * float(slots_all))
    score_scale = HEAD ** (-0.5)
    inputs = tokens[0].astype(jnp.float32)
    positions = jnp.arange(row_count, dtype=jnp.int32)
    live_slots = positions < lengths[0]
    live_float = live_slots.astype(jnp.float32)[:, None]
    mixer_parts = (
        lax.all_gather(w_qkv, ("dp", "expert"), axis=0, tiled=True),
        lax.all_gather(w_out, ("dp", "expert"), axis=0, tiled=True),
        lax.all_gather(w_router, ("dp", "expert"), axis=0, tiled=True),
        lax.all_gather(gains, ("dp", "expert"), axis=1, tiled=True),
    )
    qkv_weight, out_weight, router_weight, gain_rows = mixer_parts
    gain_float = gain_rows.astype(jnp.float32)
    attn_in, attn_norm_back = jax.vjp(norm_scale, inputs, gain_float[0])
    normed = attn_in.astype(jnp.bfloat16)
    projected = jnp.dot(normed, qkv_weight, preferred_element_type=jnp.float32)
    (rot_query, rot_keys), query_key_back = jax.vjp(
        query_key, projected[:, :D], projected[:, D : 2 * D], gain_float[1], gain_float[2]
    )
    queries = rot_query.astype(jnp.bfloat16)
    keys_low = rot_keys.astype(jnp.bfloat16)
    values_low = projected[:, 2 * D :].astype(jnp.bfloat16).reshape(row_count, HEADS, HEAD)
    allowed = (positions[None, :] <= positions[:, None]) & live_slots[None, :]
    scores = (
        jnp.einsum("qhd,khd->hqk", queries, keys_low, preferred_element_type=jnp.float32)
        * score_scale
    )
    scores = jnp.where(allowed[None], scores, -1e30)
    highest = jnp.max(scores, axis=-1, keepdims=True)
    expo_scores = jnp.exp(scores - highest)
    totals = jnp.sum(expo_scores, axis=-1, keepdims=True)
    attn_probs = expo_scores / totals
    log_total = highest + jnp.log(totals)
    mixed_heads = jnp.einsum(
        "hqk,khd->qhd",
        attn_probs.astype(jnp.bfloat16),
        values_low,
        preferred_element_type=jnp.float32,
    )
    mixed_low = mixed_heads.reshape(row_count, D).astype(jnp.bfloat16)
    hidden_state = inputs + jnp.dot(mixed_low, out_weight, preferred_element_type=jnp.float32)
    ffn_in, ffn_norm_back = jax.vjp(norm_scale, hidden_state, gain_float[3])
    ffn_low = ffn_in.astype(jnp.bfloat16)
    logits = jnp.dot(ffn_low, router_weight, preferred_element_type=jnp.float32)
    router_probs = jax.nn.softmax(logits, axis=-1)
    count_float = send_counts[0].astype(jnp.float32)
    prob_local = jnp.sum(router_probs * live_float, axis=0)
    count_total, prob_total = lax.psum((count_float, prob_local), ("dp", "expert"))
    balance = jnp.sum(count_total * prob_total) * balance_factor
    route_rows = routes[0]
    expert_ids = jnp.arange(expert_count, dtype=jnp.int32)
    route_hot = (route_rows[:, :, None] == expert_ids) & live_slots[:, None, None]
    route_int = route_hot.astype(jnp.int32)
    per_token = jnp.sum(route_int, axis=1)
    earlier = jnp.cumsum(per_token, axis=0) - per_token
    route_rank = jnp.sum(earlier[:, None, :] * route_int, axis=-1)
    limits = jnp.sum(jnp.minimum(send_counts[0], capacity)[None, None, :] * route_int, axis=-1)
    kept_route = route_rank < limits
    target_expert = jnp.where(kept_route, route_rows, expert_count)
    target_slot = jnp.where(kept_route, route_rank, 0)
    token_ids = jnp.broadcast_to(positions[:, None], route_rows.shape)
    source = (
        jnp.full((expert_count, capacity), row_count, jnp.int32)
        .at[target_expert, target_slot]
        .set(token_ids, mode="drop")
    )
    padded_in = jnp.concatenate([ffn_low, jnp.zeros((1, D), jnp.bfloat16)], axis=0)
    send_rows = padded_in[source].reshape(owners, local_experts, capacity, D)
    expert_weights = (w_gate, w_up, w_down)
    gathered = lax.all_gather(
        lax.all_to_all(send_rows, "expert", split_axis=0, concat_axis=0, tiled=True),
        "dp",
        axis=0,
        tiled=True,
    )
    gate_pre, up_pre, hidden_low, partial_out = expert_forward(gathered, w_gate, w_up, w_down)
    summed = lax.psum_scatter(
        partial_out.astype(jnp.bfloat16), "dp", scatter_dimension=0, tiled=True
    )
    expert_out, expert_rows, gate_pre, up_pre, hidden_low = (
        summed,
        gathered,
        gate_pre,
        up_pre,
        hidden_low,
    )
    returned = lax.all_to_all(
        expert_out, "expert", split_axis=0, concat_axis=0, tiled=True
    ).reshape(expert_count * capacity, D)
    flat_index = jnp.where(kept_route, route_rows * capacity + route_rank, 0)
    picked = returned[flat_index]
    route_prob = jnp.sum(router_probs[:, None, :] * route_hot.astype(jnp.float32), axis=-1)
    combine_weight = jnp.where(kept_route, route_prob, 0.0)
    mixture = jnp.sum(combine_weight[:, :, None] * picked, axis=1)
    layer = live_float * (hidden_state + mixture)
    result = layer.astype(jnp.bfloat16)[None]
    qkv_back, out_back, router_back = (
        lax.all_gather(w_qkv, ("dp", "expert"), axis=0, tiled=True),
        lax.all_gather(w_out, ("dp", "expert"), axis=0, tiled=True),
        lax.all_gather(w_router, ("dp", "expert"), axis=0, tiled=True),
    )
    grad_layer = cotangent[0].astype(jnp.float32) * live_float
    dot_route = jnp.sum(grad_layer[:, None, :] * picked, axis=-1)
    balance_coef = BALANCE_WEIGHT * balance_factor
    grad_probs = jnp.sum(
        jnp.where(kept_route, dot_route, 0.0)[:, :, None] * route_hot.astype(jnp.float32), axis=1
    )
    grad_probs = grad_probs + balance_coef * count_total[None, :] * live_float
    grad_logits = router_probs * (
        grad_probs - jnp.sum(router_probs * grad_probs, axis=-1, keepdims=True)
    )
    grad_logits_low = grad_logits.astype(jnp.bfloat16)
    route_scale = (
        jnp.zeros((expert_count, capacity), jnp.float32)
        .at[target_expert, target_slot]
        .set(combine_weight, mode="drop")
    )
    padded_grad = jnp.concatenate([grad_layer, jnp.zeros((1, D), jnp.float32)], axis=0)
    grad_send = (
        (padded_grad[source] * route_scale[:, :, None])
        .astype(jnp.bfloat16)
        .reshape(owners, local_experts, capacity, D)
    )
    arrived = lax.all_to_all(grad_send, "expert", split_axis=0, concat_axis=0, tiled=True)
    grad_rows_all = lax.all_gather(arrived, "dp", axis=0, tiled=True)
    gate_weight, up_weight, down_weight = expert_weights
    grad_down_w = jnp.einsum(
        "nkcf,nkcd->kfd", hidden_low, grad_rows_all, preferred_element_type=jnp.float32
    )
    grad_units = jnp.einsum(
        "nkcd,kfd->nkcf", grad_rows_all, down_weight, preferred_element_type=jnp.float32
    )
    gate_sigmoid = jax.nn.sigmoid(gate_pre)
    grad_gate_low = (
        grad_units * up_pre * gate_sigmoid * (1.0 + gate_pre * (1.0 - gate_sigmoid))
    ).astype(jnp.bfloat16)
    grad_up_low = (grad_units * gate_pre * gate_sigmoid).astype(jnp.bfloat16)
    grad_gate_w = jnp.einsum(
        "nkcd,nkcf->kdf", expert_rows, grad_gate_low, preferred_element_type=jnp.float32
    )
    grad_up_w = jnp.einsum(
        "nkcd,nkcf->kdf", expert_rows, grad_up_low, preferred_element_type=jnp.float32
    )
    back_part = jnp.einsum(
        "nkcf,kdf->nkcd", grad_gate_low, gate_weight, preferred_element_type=jnp.float32
    )
    back_part = back_part + jnp.einsum(
        "nkcf,kdf->nkcd", grad_up_low, up_weight, preferred_element_type=jnp.float32
    )
    back_rows = lax.psum_scatter(
        back_part.astype(jnp.bfloat16), "dp", scatter_dimension=0, tiled=True
    )
    expert_grads = (grad_gate_w, grad_up_w, grad_down_w)
    sent_back = lax.all_to_all(
        back_rows, "expert", split_axis=0, concat_axis=0, tiled=True
    ).reshape(expert_count * capacity, D)
    grad_ffn = jnp.einsum(
        "tj,tjd->td",
        kept_route.astype(jnp.bfloat16),
        sent_back[flat_index],
        preferred_element_type=jnp.float32,
    )
    grad_ffn = grad_ffn + jnp.einsum(
        "te,de->td", grad_logits_low, router_back, preferred_element_type=jnp.float32
    )
    grad_router_w = jnp.einsum(
        "td,te->de", ffn_low, grad_logits_low, preferred_element_type=jnp.float32
    )
    grad_hidden_part, grad_gain_ffn = ffn_norm_back(grad_ffn)
    grad_hidden_state = grad_layer + grad_hidden_part
    grad_attn_low = grad_hidden_state.astype(jnp.bfloat16)
    grad_out_w = jnp.einsum(
        "td,te->de", mixed_low, grad_attn_low, preferred_element_type=jnp.float32
    )
    grad_mixed = jnp.einsum(
        "te,de->td", grad_attn_low, out_back, preferred_element_type=jnp.float32
    )
    grad_mixed = grad_mixed.astype(jnp.bfloat16).reshape(row_count, HEADS, HEAD)
    scores_again = (
        jnp.einsum("qhd,khd->hqk", queries, keys_low, preferred_element_type=jnp.float32)
        * score_scale
    )
    probs_again = jnp.where(allowed[None], jnp.exp(scores_again - log_total), 0.0)
    grad_values = jnp.einsum(
        "hqk,qhd->khd",
        probs_again.astype(jnp.bfloat16),
        grad_mixed,
        preferred_element_type=jnp.float32,
    )
    grad_attn_probs = jnp.einsum(
        "qhd,khd->hqk", grad_mixed, values_low, preferred_element_type=jnp.float32
    )
    grad_scores = probs_again * (
        grad_attn_probs - jnp.sum(probs_again * grad_attn_probs, axis=-1, keepdims=True)
    )
    grad_scores_low = grad_scores.astype(jnp.bfloat16)
    grad_queries = (
        jnp.einsum("hqk,khd->qhd", grad_scores_low, keys_low, preferred_element_type=jnp.float32)
        * score_scale
    )
    grad_keys = (
        jnp.einsum("hqk,qhd->khd", grad_scores_low, queries, preferred_element_type=jnp.float32)
        * score_scale
    )
    grad_query_part, grad_key_part, grad_gain_query, grad_gain_key = query_key_back(
        (grad_queries, grad_keys)
    )
    grad_projected = jnp.concatenate(
        [grad_query_part, grad_key_part, grad_values.reshape(row_count, D)], axis=1
    ).astype(jnp.bfloat16)
    grad_qkv_w = jnp.einsum("td,te->de", normed, grad_projected, preferred_element_type=jnp.float32)
    grad_normed = jnp.einsum(
        "te,de->td", grad_projected, qkv_back, preferred_element_type=jnp.float32
    )
    grad_input_part, grad_gain_attn = attn_norm_back(grad_normed)
    grad_inputs = grad_hidden_state + grad_input_part
    grad_gain_rows = jnp.stack([grad_gain_attn, grad_gain_query, grad_gain_key, grad_gain_ffn])
    mixer_grads = (
        lax.psum_scatter(grad_qkv_w, ("dp", "expert"), scatter_dimension=0, tiled=True),
        lax.psum_scatter(grad_out_w, ("dp", "expert"), scatter_dimension=0, tiled=True),
        lax.psum_scatter(grad_router_w, ("dp", "expert"), scatter_dimension=0, tiled=True),
        lax.psum_scatter(grad_gain_rows, ("dp", "expert"), scatter_dimension=1, tiled=True),
    )
    return (
        result,
        grad_inputs[None],
        mixer_grads[0],
        mixer_grads[1],
        mixer_grads[2],
        mixer_grads[3],
        expert_grads[0],
        expert_grads[1],
        expert_grads[2],
        balance,
    )


MESH = pl.DeviceIdType.MESH


class Grid:
    def __init__(self, dims, cores=False):
        self.cores = cores
        self.dims = ((2,) if cores else ()) + tuple(dims)
        self.size = math.prod(self.dims)
        self.strides = [math.prod(self.dims[d + 1 :]) for d in range(len(self.dims))]
        self.lanes = {}
        for d in range(len(self.dims)):
            for side in self.sides(d):
                self.lanes[(d, side)] = len(self.lanes)

    def coords(self):
        expert = lax.axis_index("expert")
        c = [lax.axis_index("dp")] if self.cores else []
        first = len(c)
        for d in range(first, len(self.dims)):
            c.append(lax.rem(expert // self.strides[d], self.dims[d]))
        return c

    def rels(self, d):
        n = self.dims[d]
        if n == 1:
            return []
        if n == 2:
            return [(1, 0)]
        return [(k, side) for k in range(1, n) for side in (-1, 1)]

    def sides(self, d):
        n = self.dims[d]
        return [] if n == 1 else [0] if n == 2 else [-1, 1]

    def at(self, c, d, rel):
        k, side = rel
        return 1 - c[d] if side == 0 else c[d] + side * k

    def valid(self, c, d, rel):
        k, side = rel
        if side == 0:
            return None
        return c[d] - k >= 0 if side < 0 else c[d] + k < self.dims[d]

    def index(self, coords):
        return sum(x * s for x, s in zip(coords, self.strides))

    def neighbor(self, c, d, side):
        other = list(c)
        other[d] = self.at(c, d, (1, side))
        ok = self.valid(c, d, (1, side))
        if self.cores and d == 0:
            return {"dp": other[0]}, ok
        first = 1 if self.cores else 0
        expert = sum(x * s for x, s in zip(other[first:], self.strides[first:]))
        return {"expert": expert}, ok

    def events(self, order):
        return [
            dict(zip(order, combo))
            for combo in itertools.product(*[[None] + self.rels(d) for d in order])
        ]

    def place(self, c, order, event):
        pred, o, last = None, list(c), -1
        for i, d in enumerate(order):
            if event[d]:
                pred = both(pred, self.valid(c, d, event[d]))
                o[d] = self.at(c, d, event[d])
                last = i
        return o, pred, last


def both(a, b):
    if a is None:
        return b
    if b is None:
        return a
    return jnp.logical_and(a, b)


def when(pred, f):
    if pred is None:
        f()
    else:
        pl.when(pred)(f)


def greet(grid, c):
    barrier = pltpu.get_barrier_semaphore()
    total = jnp.int32(0)
    for d, side in grid.lanes:
        device, ok = grid.neighbor(c, d, side)
        when(
            ok,
            lambda device=device: pl.semaphore_signal(
                barrier, inc=1, device_id=device, device_id_type=MESH
            ),
        )
        total = total + (1 if ok is None else ok.astype(jnp.int32))
    pl.semaphore_wait(barrier, total)


def farthest(order, event):
    return tuple(event[d][0] if event[d] else 0 for d in reversed(order))


class Beside:
    def __init__(self, ins=(), in_specs=(), outs=(), scratch=(), steps=None, lead=0.0, span=1.0):
        self.lead, self.span = lead, span
        self.ins, self.in_specs, self.outs, self.scratch = ins, in_specs, outs, scratch
        self.steps = steps

    def share(self, refs, count, own_scratch):
        cuts = [count, len(self.ins), count, len(self.outs), own_scratch, len(self.scratch)]
        groups, at = [], 0
        for n in cuts:
            groups.append(refs[at : at + n])
            at += n
        steps = self.steps(groups[1], groups[3], groups[5]) if self.steps else []
        return groups[0], groups[2], groups[4], steps


def mingle(events, steps, free, lead, span):
    for event in events[:free]:
        event()
    first = round(lead * len(steps))
    for step in steps[:first]:
        step()
    rest, left = events[free:], steps[first:]
    done = 0
    for n, event in enumerate(rest):
        event()
        while done < len(left) and done * len(rest) * span < (n + 1) * len(left):
            left[done]()
            done += 1
    for step in left[done:]:
        step()


def gather_kernel(grid, parts, count, beside, *refs):
    srcs, outs, (send_sem, recv_sem, own_sem), steps = beside.share(refs, count, 3)
    c = grid.coords()
    me = grid.index(c)
    own = [pltpu.make_async_copy(s, o.at[me], own_sem.at[i]) for i, (s, o) in enumerate(zip(srcs, outs))]
    for copy in own:
        copy.start()
    greet(grid, c)
    sent = []

    def piece(p, ref):
        _, row0, rows, _ = parts[p]
        return ref.at[pl.ds(row0, rows)]

    def push(p, origin, source, d, side, pred):
        device, ok = grid.neighbor(c, d, side)
        pred = both(pred, ok)
        copy = pltpu.make_async_remote_copy(
            src_ref=source,
            dst_ref=piece(p, outs[parts[p][0]].at[origin]),
            send_sem=send_sem.at[p, origin, grid.lanes[(d, side)]],
            recv_sem=recv_sem.at[p, origin],
            device_id=device,
            device_id_type=MESH,
        )
        when(pred, copy.start)
        sent.append((pred, copy))

    todo = []
    for p, (_, _, _, order) in enumerate(parts):
        for event in grid.events(order):
            todo.append((farthest(order, event), p, event))
    todo.sort(key=lambda t: t[:2])

    def handle(p, event):
        a, _, _, order = parts[p]
        o, pred, last = grid.place(c, order, event)
        origin = grid.index(o)
        if last < 0:
            source = piece(p, srcs[a])
        else:
            source = piece(p, outs[a].at[origin])
            arrival = pltpu.make_async_remote_copy(
                src_ref=source,
                dst_ref=source,
                send_sem=send_sem.at[p, origin, 0],
                recv_sem=recv_sem.at[p, origin],
                device_id={"expert": lax.axis_index("expert")},
                device_id_type=MESH,
            )
            when(pred, arrival.wait_recv)
            side = event[order[last]][1]
            if side:
                push(p, origin, source, order[last], -side, pred)
        for d in order[last + 1 :]:
            for side in grid.sides(d):
                push(p, origin, source, d, side, pred)

    mingle(
        [functools.partial(handle, p, event) for _, p, event in todo],
        steps,
        sum(not any(event.values()) for _, _, event in todo),
        beside.lead,
        beside.span,
    )
    for pred, copy in sent:
        when(pred, copy.wait_send)
    for copy in own:
        copy.wait()


def gather(arrays, grid, parts, cid, beside=Beside()):
    n, count = grid.size, len(arrays)
    return pl.pallas_call(
        functools.partial(gather_kernel, grid, parts, count, beside),
        out_shape=[jax.ShapeDtypeStruct((n,) + x.shape, x.dtype) for x in arrays] + list(beside.outs),
        in_specs=[pl.BlockSpec(memory_space=pl.ANY)] * count + list(beside.in_specs),
        out_specs=[pl.BlockSpec(memory_space=pl.ANY)] * (count + len(beside.outs)),
        scratch_shapes=[
            pltpu.SemaphoreType.DMA((len(parts), n, len(grid.lanes))),
            pltpu.SemaphoreType.DMA((len(parts), n)),
            pltpu.SemaphoreType.DMA((count,)),
        ]
        + list(beside.scratch),
        compiler_params=pltpu.CompilerParams(
            collective_id=cid, has_side_effects=True, vmem_limit_bytes=60 << 20
        ),
    )(*arrays, *beside.ins)


def landing_slots(grid, order):
    base, total, earlier = {}, 0, 1
    for d in order:
        base[d] = total
        total += len(grid.rels(d)) * earlier
        earlier *= grid.dims[d]
    return base, total


def scatter_kernel(grid, parts, count, beside, *refs):
    k = len(parts)
    srcs, outs, scratch, steps = beside.share(refs, count, 2 * k + count + 4)
    held, mine, totals = scratch[:k], scratch[k : 2 * k], scratch[2 * k : 2 * k + count]
    send_sem, recv_sem, mine_sem, out_sem = scratch[2 * k + count :]
    c = grid.coords()

    def piece(p, ref):
        _, row0, rows, _ = parts[p]
        return ref.at[pl.ds(row0, rows)]

    def own_slot(order, o):
        slot = 0
        for d in order[:-1]:
            slot = slot * grid.dims[d] + o[d]
        return slot

    def landing(order, d, rel, o):
        base, _ = landing_slots(grid, order)
        slot = grid.rels(d).index(rel)
        for q in order[: order.index(d)]:
            slot = slot * grid.dims[q] + o[q]
        return base[d] + slot

    def own_copy(p, o):
        a, _, _, order = parts[p]
        slot = own_slot(order, o)
        return pltpu.make_async_copy(
            piece(p, srcs[a].at[grid.index(o)]), mine[p].at[slot], mine_sem.at[p, slot]
        )

    for p, (_, _, _, order) in enumerate(parts):
        for position in itertools.product(*[range(grid.dims[d]) for d in order[:-1]]):
            o = list(c)
            for d, v in zip(order[:-1], position):
                o[d] = v
            own_copy(p, o).start()
    greet(grid, c)
    todo = []
    for p, (_, _, _, order) in enumerate(parts):
        for event in grid.events(order):
            todo.append((tuple(-far for far in farthest(order, event)), p, event))
    todo.sort(key=lambda t: t[:2])
    sent = []

    def handle(p, event):
        a, row0, rows, order = parts[p]
        o, pred, last = grid.place(c, order, event)
        always, sometimes = [], []
        if last >= 0:
            far, side = event[order[last]]
            if side and far + 1 < grid.dims[order[last]]:
                _, ok = grid.neighbor(c, order[last], -side)
                sometimes.append((landing(order, order[last], (far + 1, side), o), ok))
        for d in order[last + 1 :]:
            for side in grid.sides(d):
                _, ok = grid.neighbor(c, d, side)
                slot = landing(order, d, (1, -side), o)
                if ok is None:
                    always.append(slot)
                else:
                    sometimes.append((slot, ok))
        final = last < 0
        if not always and not sometimes and not final:
            source = piece(p, srcs[a].at[grid.index(o)])
        else:
            source = mine[p].at[own_slot(order, o)]
            when(pred, own_copy(p, o).wait)
            steps = [(slot, ok) for slot, ok in sometimes]
            if always or final:
                steps.insert(0, (always, None))

            def add(slots, opening, final=final, source=source, p=p, row0=row0, rows=rows, a=a):
                for slot in slots:
                    landed = held[p].at[slot]
                    pltpu.make_async_remote_copy(
                        src_ref=landed,
                        dst_ref=landed,
                        send_sem=send_sem.at[p, 0],
                        recv_sem=recv_sem.at[p, slot],
                        device_id={"expert": lax.axis_index("expert")},
                        device_id_type=MESH,
                    ).wait_recv()
                tile = min(16, rows)

                @pl.loop(0, rows // tile)
                def _(t):
                    here = pl.ds(pl.multiple_of(t * tile, tile), tile)
                    there = pl.ds(pl.multiple_of(row0 + t * tile, tile), tile)
                    if final and not opening:
                        value = totals[a][there, :]
                    else:
                        value = source[here, :].astype(jnp.float32)
                    for slot in slots:
                        value = value + held[p][slot, here, :].astype(jnp.float32)
                    if final:
                        totals[a][there, :] = value
                    else:
                        source[here, :] = value.astype(source.dtype)

            for n, (slots, ok) in enumerate(steps):
                slots = slots if isinstance(slots, list) else [slots]
                when(both(pred, ok), functools.partial(add, slots, n == 0))
        if last >= 0:
            d = order[last]
            device, _ = grid.neighbor(c, d, event[d][1])
            slot = landing(order, d, event[d], o)
            copy = pltpu.make_async_remote_copy(
                src_ref=source,
                dst_ref=held[p].at[slot],
                send_sem=send_sem.at[p, slot],
                recv_sem=recv_sem.at[p, slot],
                device_id=device,
                device_id_type=MESH,
            )
            when(pred, copy.start)
            sent.append((pred, copy))

    mingle(
        [functools.partial(handle, p, event) for _, p, event in todo],
        steps,
        sum(event[parts[p][3][-1]] is not None for _, p, event in todo),
        beside.lead,
        beside.span,
    )
    done = [pltpu.make_async_copy(t, o, out_sem.at[i]) for i, (t, o) in enumerate(zip(totals, outs))]
    for copy in done:
        copy.start()
    for pred, copy in sent:
        when(pred, copy.wait_send)
    for copy in done:
        copy.wait()


def scatter(arrays, grid, parts, cid, beside=Beside()):
    count = len(arrays)
    slots = [landing_slots(grid, order)[1] for _, _, _, order in parts]
    mine = [grid.size // grid.dims[order[-1]] for _, _, _, order in parts]
    blocks = [((rows, arrays[a].shape[2]), arrays[a].dtype) for a, _, rows, _ in parts]
    flat = [jax.ShapeDtypeStruct(x.shape[1:], jnp.float32) for x in arrays]
    return pl.pallas_call(
        functools.partial(scatter_kernel, grid, parts, count, beside),
        out_shape=flat + list(beside.outs),
        in_specs=[pl.BlockSpec(memory_space=pl.ANY)] * count + list(beside.in_specs),
        out_specs=[pl.BlockSpec(memory_space=pl.ANY)] * (count + len(beside.outs)),
        scratch_shapes=[pltpu.VMEM((s,) + b, t) for s, (b, t) in zip(slots, blocks)]
        + [pltpu.VMEM((s,) + b, t) for s, (b, t) in zip(mine, blocks)]
        + [pltpu.VMEM(x.shape, x.dtype) for x in flat]
        + [
            pltpu.SemaphoreType.DMA((len(parts), max(slots))),
            pltpu.SemaphoreType.DMA((len(parts), max(slots))),
            pltpu.SemaphoreType.DMA((len(parts), max(mine))),
            pltpu.SemaphoreType.DMA((count,)),
        ]
        + list(beside.scratch),
        compiler_params=pltpu.CompilerParams(
            collective_id=cid, has_side_effects=True, vmem_limit_bytes=60 << 20
        ),
    )(*arrays, *beside.ins)


def cut(array, shares, orders):
    starts = [sum(shares[:i]) for i in range(len(shares))]
    return tuple((array, start, share, order) for start, share, order in zip(starts, shares, orders))


def each_tile(total, width, f):
    @pl.loop(0, total // width, unroll=4)
    def _(t):
        f(pl.ds(pl.multiple_of(t * width, width), width))


def dot(left, right):
    return jnp.dot(left, right, preferred_element_type=jnp.float32)


def dot_across(left, right):
    return lax.dot_general(left, right, (((1,), (1,)), ((), ())), preferred_element_type=jnp.float32)


class Move:
    def __init__(self, *refs):
        self.refs = refs

    def start(self):
        pltpu.make_async_copy(*self.refs).start()

    def wait(self):
        pltpu.make_async_copy(*self.refs).wait()


ANYWHERE = pl.BlockSpec(memory_space=pl.ANY)
ON_CORE = pl.BlockSpec(memory_space=pltpu.VMEM)


def weight_copies(halves, held, sem):
    gate_own, gate_far, up_own, up_far, down_own, down_far = halves
    gate, up, down = held
    half = gate.shape[1] // 2
    own, far = pl.ds(0, half), pl.ds(half, half)
    pairs = [
        (gate_own, gate.at[:, own]),
        (gate_far, gate.at[:, far]),
        (up_own, up.at[:, own]),
        (up_far, up.at[:, far]),
        (down_own, down.at[own, :]),
        (down_far, down.at[far, :]),
    ]
    return [Move(a, b, sem.at[i]) for i, (a, b) in enumerate(pairs)]


def pick_of(ranks, row, capacity):
    line = ranks[row : row + 1, :]
    slot = lax.broadcasted_iota(jnp.int32, (capacity, line.shape[1]), 0).astype(jnp.float32)
    return line == slot


def put_of(ranks, row, capacity):
    line = ranks[:, row : row + 1]
    slot = lax.broadcasted_iota(jnp.int32, (line.shape[0], capacity), 1).astype(jnp.float32)
    return (line == slot).astype(jnp.float32).astype(jnp.bfloat16)


def forward_beside(ffn_rows, rank_rows, rank_cols, weight_cols, halves, capacity):
    row_count, tokens, width = ffn_rows.shape
    hidden = 2 * halves[0].shape[1]
    pairs, pair = row_count // 2, 2 * capacity
    slots = row_count * capacity
    low, full = jnp.bfloat16, jnp.float32

    def steps(ins, outs, scratch):
        ffn_in, ranks, ranks_t, weights_t = ins[:4]
        weights, (ffn, xs, pre, units, out, mix), sems = scratch[:3], scratch[3:9], scratch[9:]
        load_sem, row_sem, out_sem = sems
        heavy = weight_copies(ins[4:], weights, load_sem)
        gate_w, up_w, down_w = weights

        def load(q):
            return Move(ffn_in.at[pl.ds(2 * q, 2)], ffn.at[q % 2], row_sem.at[q % 2])

        def leave(q):
            here = pl.ds(q * pair, pair)
            moves = [
                (xs, outs[0].at[here]),
                (pre.at[0], outs[1].at[here]),
                (pre.at[1], outs[2].at[here]),
                (units, outs[3].at[here]),
                (out, outs[4].at[here]),
                (mix, outs[5].at[pl.ds(2 * q, 2)]),
            ]
            return [Move(a, b, out_sem.at[i]) for i, (a, b) in enumerate(moves)]

        def opening():
            for copy in heavy:
                copy.start()
            load(0).start()

        def choose(q):
            load(q).wait()
            if q + 1 < pairs:
                load(q + 1).start()
            if q:
                leave(q - 1)[0].wait()
            for i in range(2):
                pick = pick_of(ranks, 2 * q + i, capacity).astype(full).astype(low)
                rows = pl.ds(i * capacity, capacity)

                def tile(cols, i=i, pick=pick, rows=rows):
                    xs[rows, cols] = dot(pick, ffn[q % 2, i, :, cols]).astype(low)

                each_tile(width, 512, tile)
            leave(q)[0].start()

        def widen(q):
            if q == 0:
                for copy in heavy[:4]:
                    copy.wait()
            else:
                for copy in leave(q - 1)[1:4]:
                    copy.wait()

            def tile(cols):
                gate = dot(xs[...], gate_w[:, cols])
                up = dot(xs[...], up_w[:, cols])
                pre[0, :, cols] = gate
                pre[1, :, cols] = up
                units[:, cols] = (gate * jax.nn.sigmoid(gate) * up).astype(low)

            each_tile(hidden, 256, tile)
            for copy in leave(q)[1:4]:
                copy.start()

        def narrow(q):
            if q == 0:
                for copy in heavy[4:]:
                    copy.wait()
            else:
                for copy in leave(q - 1)[4:]:
                    copy.wait()
            puts = [put_of(ranks_t, 2 * q + i, capacity) for i in range(2)]
            scales = [weights_t[:, 2 * q + i : 2 * q + i + 1] for i in range(2)]

            def tile(cols):
                value = dot(units[...], down_w[:, cols]).astype(low)
                out[:, cols] = value
                for i in range(2):
                    part = dot(puts[i], value[i * capacity : (i + 1) * capacity]) * scales[i]
                    mix[i, :, cols] = part.astype(low)

            each_tile(width, 256, tile)
            for copy in leave(q)[4:]:
                copy.start()

        def closing():
            for copy in leave(pairs - 1):
                copy.wait()

        listed = [opening]
        for q in range(pairs):
            listed += [functools.partial(f, q) for f in (choose, widen, narrow)]
        return listed + [closing]

    return Beside(
        ins=(ffn_rows, rank_rows, rank_cols, weight_cols) + tuple(halves),
        in_specs=(ANYWHERE, ON_CORE, ON_CORE, ON_CORE) + (ANYWHERE,) * 6,
        outs=[
            jax.ShapeDtypeStruct((slots, width), low),
            jax.ShapeDtypeStruct((slots, hidden), full),
            jax.ShapeDtypeStruct((slots, hidden), full),
            jax.ShapeDtypeStruct((slots, hidden), low),
            jax.ShapeDtypeStruct((slots, width), low),
            jax.ShapeDtypeStruct((row_count, tokens, width), low),
        ],
        scratch=[
            pltpu.VMEM((width, hidden), low),
            pltpu.VMEM((width, hidden), low),
            pltpu.VMEM((hidden, width), low),
            pltpu.VMEM((2, 2, tokens, width), low),
            pltpu.VMEM((pair, width), low),
            pltpu.VMEM((2, pair, hidden), full),
            pltpu.VMEM((pair, hidden), low),
            pltpu.VMEM((pair, width), low),
            pltpu.VMEM((2, tokens, width), low),
            pltpu.SemaphoreType.DMA((6,)),
            pltpu.SemaphoreType.DMA((2,)),
            pltpu.SemaphoreType.DMA((6,)),
        ],
        steps=steps,
        lead=0.3,
        span=0.6,
    )


def backward_beside(cot_early, cot_late, rank_rows, rank_cols, weight_rows, gate_pre, up_pre, expert_out, halves, capacity):
    row_count, late, width = cot_late.shape
    early = cot_early.shape[1]
    tokens = early + late
    hidden = 2 * halves[0].shape[1]
    pairs, pair = row_count // 2, 2 * capacity
    slots = row_count * capacity
    low, full = jnp.bfloat16, jnp.float32

    def steps(ins, outs, scratch):
        early_in, late_in, ranks, ranks_t, weights, gate_in, up_in, out_in = ins[:8]
        heavy_refs, (cot, ge, pre, out, gg, gu, gx, dots, sums), sems = scratch[:3], scratch[3:12], scratch[12:]
        load_sem, row_sem, out_sem = sems
        heavy = weight_copies(ins[8:], heavy_refs, load_sem)
        gate_w, up_w, down_w = heavy_refs

        first = lax.axis_index("dp") * row_count

        def load(q):
            held = cot.at[q % 2]
            return [
                Move(early_in.at[pl.ds(first + 2 * q, 2)], held.at[:, pl.ds(0, early)], row_sem.at[q % 2]),
                Move(late_in.at[pl.ds(2 * q, 2)], held.at[:, pl.ds(early, late)], row_sem.at[5 + q % 2]),
            ]

        def fetch(q):
            here = pl.ds(q * pair, pair)
            moves = [(out_in, out), (gate_in, pre.at[0]), (up_in, pre.at[1])]
            return [Move(a.at[here], b, row_sem.at[2 + i]) for i, (a, b) in enumerate(moves)]

        def leave(q):
            here = pl.ds(q * pair, pair)
            moves = [(ge, outs[0].at[here]), (gg, outs[1].at[here]), (gu, outs[2].at[here])]
            moves.append((gx, outs[3].at[pl.ds(2 * q, 2)]))
            return [Move(a, b, out_sem.at[i]) for i, (a, b) in enumerate(moves)]

        last = Move(dots, outs[4], out_sem.at[4])

        def opening():
            for copy in load(0):
                copy.start()
            for copy in fetch(0):
                copy.start()
            for copy in heavy:
                copy.start()

        def choose(q):
            for copy in load(q):
                copy.wait()
            fetch(q)[0].wait()
            if q + 1 < pairs:
                for copy in load(q + 1):
                    copy.start()
            if q:
                leave(q - 1)[0].wait()
            for i in range(2):
                row = 2 * q + i
                pick = pick_of(ranks, row, capacity)
                pick_low = pick.astype(full).astype(low)
                scale = jnp.sum(jnp.where(pick, weights[row : row + 1, :], 0.0), axis=1, keepdims=True)
                rows = pl.ds(i * capacity, capacity)
                sums[...] = jnp.zeros_like(sums)

                def tile(cols, i=i, pick_low=pick_low, scale=scale, rows=rows):
                    value = dot(pick_low, cot[q % 2, i, :, cols])
                    ge[rows, cols] = (value * scale).astype(low)
                    product = value * out[rows, cols].astype(full)
                    total = product[:, :128]
                    for lane in range(128, product.shape[1], 128):
                        total = total + product[:, lane : lane + 128]
                    sums[...] += total

                each_tile(width, 512, tile)
                slot_dot = jnp.sum(sums[...], axis=1, keepdims=True)
                dots[row : row + 1, :] = jnp.sum(jnp.where(pick, slot_dot, 0.0), axis=0, keepdims=True)
            leave(q)[0].start()
            if q + 1 < pairs:
                fetch(q + 1)[0].start()

        def narrow(q):
            for copy in fetch(q)[1:]:
                copy.wait()
            if q == 0:
                for copy in heavy:
                    copy.wait()
            else:
                for copy in leave(q - 1)[1:3]:
                    copy.wait()

            def tile(cols):
                grad = dot_across(ge[...], down_w[cols, :])
                gate, up = pre[0, :, cols], pre[1, :, cols]
                sigmoid = jax.nn.sigmoid(gate)
                gg[:, cols] = (grad * up * sigmoid * (1.0 + gate * (1.0 - sigmoid))).astype(low)
                gu[:, cols] = (grad * gate * sigmoid).astype(low)

            each_tile(hidden, 256, tile)
            for copy in leave(q)[1:3]:
                copy.start()
            if q + 1 < pairs:
                for copy in fetch(q + 1)[1:]:
                    copy.start()

        def widen(q):
            if q:
                leave(q - 1)[3].wait()
            puts = [put_of(ranks_t, 2 * q + i, capacity) for i in range(2)]

            def tile(cols):
                value = dot_across(gg[...], gate_w[cols, :]) + dot_across(gu[...], up_w[cols, :])
                value = value.astype(low)
                for i in range(2):
                    part = dot(puts[i], value[i * capacity : (i + 1) * capacity])
                    gx[i, :, cols] = part.astype(low)

            each_tile(width, 256, tile)
            leave(q)[3].start()

        def closing():
            last.start()
            for copy in leave(pairs - 1):
                copy.wait()
            last.wait()

        listed = [opening]
        for q in range(pairs):
            listed += [functools.partial(f, q) for f in (choose, narrow, widen)]
        return listed + [closing]

    return Beside(
        ins=(cot_early, cot_late, rank_rows, rank_cols, weight_rows, gate_pre, up_pre, expert_out) + tuple(halves),
        in_specs=(ANYWHERE, ANYWHERE, ON_CORE, ON_CORE, ON_CORE) + (ANYWHERE,) * 9,
        outs=[
            jax.ShapeDtypeStruct((slots, width), low),
            jax.ShapeDtypeStruct((slots, hidden), low),
            jax.ShapeDtypeStruct((slots, hidden), low),
            jax.ShapeDtypeStruct((row_count, tokens, width), low),
            jax.ShapeDtypeStruct((row_count, tokens), full),
        ],
        scratch=[
            pltpu.VMEM((width, hidden), low),
            pltpu.VMEM((width, hidden), low),
            pltpu.VMEM((hidden, width), low),
            pltpu.VMEM((2, 2, tokens, width), low),
            pltpu.VMEM((pair, width), low),
            pltpu.VMEM((2, pair, hidden), full),
            pltpu.VMEM((pair, width), low),
            pltpu.VMEM((pair, hidden), low),
            pltpu.VMEM((pair, hidden), low),
            pltpu.VMEM((2, tokens, width), low),
            pltpu.VMEM((row_count, tokens), full),
            pltpu.VMEM((capacity, 128), full),
            pltpu.SemaphoreType.DMA((6,)),
            pltpu.SemaphoreType.DMA((7,)),
            pltpu.SemaphoreType.DMA((5,)),
        ],
        steps=steps,
        span=0.8,
    )


def outer_beside(rows_in, grad_rows, grad_gate, grad_up, units):
    slots, width = rows_in.shape
    hidden = units.shape[1]
    half = hidden // 2
    block = 256
    low, full = jnp.bfloat16, jnp.float32

    def steps(ins, outs, scratch):
        rows_ref, grads_ref, gate_ref, up_ref, units_ref = ins
        left, turned, gate, up, grads, wide_own, wide_far, tall_own, tall_far, load_sem, left_sem, out_sem = scratch
        heavy = [
            Move(a, b, load_sem.at[i])
            for i, (a, b) in enumerate([(gate_ref, gate), (up_ref, up), (grads_ref, grads)])
        ]
        jobs = [(rows_ref, t) for t in range(width // block)] + [
            (units_ref, t) for t in range(hidden // block)
        ]

        def load(n):
            ref, t = jobs[n]
            return Move(
                ref.at[:, pl.ds(t * block, block)], left.at[n % 2], left_sem.at[n % 2]
            )

        def turn(n):
            load(n).wait()
            if n + 1 < len(jobs):
                load(n + 1).start()

            @pl.loop(0, slots // block)
            def _(k):
                here = pl.ds(pl.multiple_of(k * block, block), block)
                turned[:, here] = left[n % 2, here, :].astype(full).T.astype(low)

        def leave_wide(which, t):
            here = pl.ds(t * block, block)
            return [
                Move(wide_own.at[which], outs[2 * which].at[here], out_sem.at[2 * which]),
                Move(wide_far.at[which], outs[2 * which + 1].at[here], out_sem.at[2 * which + 1]),
            ]

        def leave_tall(t):
            far = t * block >= half
            here = pl.ds(t * block - (half if far else 0), block)
            return Move(
                tall_far if far else tall_own, outs[5 if far else 4].at[here], out_sem.at[5 if far else 4]
            )

        def wide(which, t):
            right = (gate, up)[which]
            if t == 0:
                heavy[which].wait()
            else:
                for copy in leave_wide(which, t - 1):
                    copy.wait()

            def own(cols):
                wide_own[which, :, cols] = dot(turned[...], right[:, cols])

            each_tile(half, 256, own)

            @pl.loop(0, half // 256)
            def _(k):
                cols = pl.ds(pl.multiple_of(k * 256, 256), 256)
                there = pl.ds(pl.multiple_of(half + k * 256, 256), 256)
                wide_far[which, :, cols] = dot(turned[...], right[:, there]).astype(low)

            for copy in leave_wide(which, t):
                copy.start()

        def tall(t):
            far = t * block >= half
            if t == 0:
                heavy[2].wait()
            if t * block not in (0, half):
                leave_tall(t - 1).wait()

            def tile(cols):
                value = dot(turned[...], grads[:, cols])
                if far:
                    tall_far[:, cols] = value.astype(low)
                else:
                    tall_own[:, cols] = value

            each_tile(width, 256, tile)
            leave_tall(t).start()

        def opening():
            load(0).start()
            for copy in heavy:
                copy.start()

        def closing():
            for which in range(2):
                for copy in leave_wide(which, width // block - 1):
                    copy.wait()
            leave_tall(half // block - 1).wait()
            leave_tall(hidden // block - 1).wait()

        listed = [opening]
        for n, (ref, t) in enumerate(jobs):
            listed.append(functools.partial(turn, n))
            if n < width // block:
                listed += [functools.partial(wide, which, t) for which in range(2)]
            else:
                listed.append(functools.partial(tall, t))
        return listed + [closing]

    return Beside(
        ins=(rows_in, grad_rows, grad_gate, grad_up, units),
        in_specs=(ANYWHERE,) * 5,
        outs=[
            jax.ShapeDtypeStruct((width, half), full),
            jax.ShapeDtypeStruct((width, half), low),
            jax.ShapeDtypeStruct((width, half), full),
            jax.ShapeDtypeStruct((width, half), low),
            jax.ShapeDtypeStruct((half, width), full),
            jax.ShapeDtypeStruct((half, width), low),
        ],
        scratch=[
            pltpu.VMEM((2, slots, block), low),
            pltpu.VMEM((block, slots), low),
            pltpu.VMEM((slots, hidden), low),
            pltpu.VMEM((slots, hidden), low),
            pltpu.VMEM((slots, width), low),
            pltpu.VMEM((2, block, half), full),
            pltpu.VMEM((2, block, half), low),
            pltpu.VMEM((block, width), full),
            pltpu.VMEM((block, width), low),
            pltpu.SemaphoreType.DMA((3,)),
            pltpu.SemaphoreType.DMA((2,)),
            pltpu.SemaphoreType.DMA((6,)),
        ],
        steps=steps,
        span=0.6,
    )


def turn_half(values):
    return pltpu.roll(values, values.shape[1] // 2, 1)


def attend_beside(tokens, gain_rows, qkv_weight, live_row, cosine, sine):
    row_count, width = tokens.shape
    low, full = jnp.bfloat16, jnp.float32
    block, group, strip = 256, 2, 32
    tiles, per_part = 3 * width // block, width // block
    score_scale = HEAD ** (-0.5)

    def steps(ins, outs, scratch):
        tokens_ref, gains, weight, live, cos, sin = ins
        normed, proj, panel, queries, keys, values, mixed, probs, scale, panel_sem, out_sem, probs_sem = scratch

        def load(t):
            return Move(weight.at[:, pl.ds(t * block, block)], panel.at[t % 3], panel_sem.at[t % 3])

        leaves = [
            Move(ref, outs[i], out_sem.at[i])
            for i, ref in enumerate((normed, proj.at[:, pl.ds(0, 2 * width)], queries, keys, values, mixed))
        ]

        def leave_probs(n):
            return Move(probs.at[n % 2], outs[6].at[pl.ds(n * group, group)], probs_sem.at[n % 2])

        def opening():
            load(0).start()
            load(1).start()

            @pl.loop(0, row_count // strip)
            def _(k):
                here = pl.ds(pl.multiple_of(k * strip, strip), strip)
                value = tokens_ref[here, :].astype(full)
                value = value * lax.rsqrt(jnp.mean(value * value, axis=1, keepdims=True) + NORM_EPS)
                normed[here, :] = (value * gains[0:1, :]).astype(low)

            leaves[0].start()

        def project(t):
            load(t).wait()
            if t + 2 < tiles:
                load(t + 2).start()
            proj[:, t * block : (t + 1) * block] = dot(normed[...], panel[t % 3])

        def measure(part):
            @pl.loop(0, row_count // strip)
            def _(k):
                here = pl.ds(pl.multiple_of(k * strip, strip), strip)
                value = proj[here, part * width : (part + 1) * width]
                inverse = lax.rsqrt(jnp.mean(value * value, axis=1, keepdims=True) + NORM_EPS)
                scale[part, here, :] = jnp.broadcast_to(inverse, (strip, HEAD))

        def attend(n):
            if n == 0:
                leaves[1].start()
            if n >= 2:
                leave_probs(n - 2).wait()
            query_slot = lax.broadcasted_iota(jnp.int32, (row_count, row_count), 0)
            key_slot = lax.broadcasted_iota(jnp.int32, (row_count, row_count), 1)
            allowed = (key_slot <= query_slot) & (live[...] > 0.5)

            @pl.loop(0, group)
            def _(i):
                head = n * group + i
                cols = pl.ds(pl.multiple_of(head * HEAD, HEAD), HEAD)

                def place(part, gain):
                    there = pl.ds(pl.multiple_of(part * width + head * HEAD, HEAD), HEAD)
                    value = proj[:, there] * scale[part] * gains[gain : gain + 1, cols]
                    return (value * cos[...] + turn_half(value) * sin[...]).astype(low)

                query, key = place(0, 1), place(1, 2)
                value = proj[:, pl.ds(pl.multiple_of(2 * width + head * HEAD, HEAD), HEAD)].astype(low)
                queries[:, cols], keys[:, cols], values[:, cols] = query, key, value
                score = jnp.where(allowed, dot_across(query, key) * score_scale, -1e30)
                expo = jnp.exp(score - jnp.max(score, axis=1, keepdims=True))
                prob = expo / jnp.sum(expo, axis=1, keepdims=True)
                probs[n % 2, i] = prob
                mixed[:, cols] = dot(prob.astype(low), value).astype(low)

            leave_probs(n).start()

        def closing():
            for move in leaves[2:]:
                move.start()
            for move in leaves:
                move.wait()
            for n in range(HEADS // group - 2, HEADS // group):
                leave_probs(n).wait()

        listed = [opening] + [functools.partial(project, t) for t in range(tiles)]
        listed += [functools.partial(measure, 0), functools.partial(measure, 1)]
        return listed + [functools.partial(attend, n) for n in range(HEADS // group)] + [closing]

    shape = (row_count, width)
    return Beside(
        ins=(tokens, gain_rows, qkv_weight, live_row, cosine, sine),
        in_specs=(ON_CORE, ON_CORE, ANYWHERE, ON_CORE, ON_CORE, ON_CORE),
        outs=[
            jax.ShapeDtypeStruct(shape, low),
            jax.ShapeDtypeStruct((row_count, 2 * width), full),
            jax.ShapeDtypeStruct(shape, low),
            jax.ShapeDtypeStruct(shape, low),
            jax.ShapeDtypeStruct(shape, low),
            jax.ShapeDtypeStruct(shape, low),
            jax.ShapeDtypeStruct((HEADS, row_count, row_count), full),
        ],
        scratch=[
            pltpu.VMEM(shape, low),
            pltpu.VMEM((row_count, 3 * width), full),
            pltpu.VMEM((3, width, block), low),
            pltpu.VMEM(shape, low),
            pltpu.VMEM(shape, low),
            pltpu.VMEM(shape, low),
            pltpu.VMEM(shape, low),
            pltpu.VMEM((2, group, row_count, row_count), full),
            pltpu.VMEM((2, row_count, HEAD), full),
            pltpu.SemaphoreType.DMA((3,)),
            pltpu.SemaphoreType.DMA((6,)),
            pltpu.SemaphoreType.DMA((2,)),
        ],
        steps=steps,
        lead=0.2,
        span=0.6,
    )


def attend_back_beside(grad_attn, out_weight, queries, keys, values, probs, parts, gain_rows, cosine, sine):
    row_count, width = grad_attn.shape
    low, full = jnp.bfloat16, jnp.float32
    block, group, strip = 256, 2, 32
    score_scale = HEAD ** (-0.5)
    across_rows = (((0,), (0,)), ((), ()))

    def steps(ins, outs, scratch):
        grad_ref, weight, query_ref, key_ref, value_ref, probs_in, parts_ref, gains, cos, sin = ins
        grad_mixed, grads, panel, prob_ref, projected, sums, panel_sem, probs_sem, out_sem = scratch
        tiles = width // block

        def load(t):
            return Move(weight.at[pl.ds(t * block, block)], panel.at[t % 3], panel_sem.at[t % 3])

        def load_probs(n):
            return Move(probs_in.at[pl.ds(n * group, group)], prob_ref.at[n % 2], probs_sem.at[n % 2])

        leaves = [Move(projected, outs[0], out_sem.at[0]), Move(sums, outs[1], out_sem.at[1])]

        def opening():
            load(0).start()
            load(1).start()
            load_probs(0).start()

        def unmix(t):
            load(t).wait()
            if t + 2 < tiles:
                load(t + 2).start()
            grad_mixed[:, t * block : (t + 1) * block] = dot_across(grad_ref[...], panel[t % 3]).astype(low)

        def attend(n):
            load_probs(n).wait()
            if n + 1 < HEADS // group:
                load_probs(n + 1).start()

            @pl.loop(0, group)
            def _(i):
                head = n * group + i
                cols = pl.ds(pl.multiple_of(head * HEAD, HEAD), HEAD)
                prob, grad = prob_ref[n % 2, i], grad_mixed[:, cols]
                grad_value = lax.dot_general(prob.astype(low), grad, across_rows, preferred_element_type=full)
                there = pl.ds(pl.multiple_of(2 * width + head * HEAD, HEAD), HEAD)
                projected[:, there] = grad_value.astype(low)
                grad_prob = dot_across(grad, value_ref[:, cols])
                centre = jnp.sum(prob * grad_prob, axis=1, keepdims=True)
                grad_score = (prob * (grad_prob - centre)).astype(low)
                grad_query = dot(grad_score, key_ref[:, cols]) * score_scale
                grad_key = lax.dot_general(grad_score, query_ref[:, cols], across_rows, preferred_element_type=full)
                for part, value in enumerate((grad_query, grad_key * score_scale)):
                    grads[part, :, cols] = value * cos[...] - turn_half(value) * sin[...]

        def settle(part):
            sums[part] = jnp.zeros((8, width), full)

            @pl.loop(0, row_count // strip)
            def _(k):
                here = pl.ds(pl.multiple_of(k * strip, strip), strip)
                value = parts_ref[here, part * width : (part + 1) * width]
                inverse = lax.rsqrt(jnp.mean(value * value, axis=1, keepdims=True) + NORM_EPS)
                unit = value * inverse
                grad = grads[part, here, :]
                product = grad * unit
                total = product[0:8]
                for first in range(8, strip, 8):
                    total = total + product[first : first + 8]
                sums[part] += total
                grad = grad * gains[part + 1 : part + 2, :]
                grad = inverse * (grad - unit * jnp.mean(grad * unit, axis=1, keepdims=True))
                projected[here, part * width : (part + 1) * width] = grad.astype(low)

        def closing():
            for move in leaves:
                move.start()
            for move in leaves:
                move.wait()

        listed = [opening] + [functools.partial(unmix, t) for t in range(tiles)]
        listed += [functools.partial(attend, n) for n in range(HEADS // group)]
        return listed + [functools.partial(settle, part) for part in range(2)] + [closing]

    shape = (row_count, width)
    return Beside(
        ins=(grad_attn, out_weight, queries, keys, values, probs, parts, gain_rows, cosine, sine),
        in_specs=(ON_CORE, ANYWHERE, ON_CORE, ON_CORE, ON_CORE, ANYWHERE, ON_CORE, ON_CORE, ON_CORE, ON_CORE),
        outs=[
            jax.ShapeDtypeStruct((row_count, 3 * width), low),
            jax.ShapeDtypeStruct((2, 8, width), full),
        ],
        scratch=[
            pltpu.VMEM(shape, low),
            pltpu.VMEM((2,) + shape, full),
            pltpu.VMEM((3, block, width), low),
            pltpu.VMEM((2, group, row_count, row_count), full),
            pltpu.VMEM((row_count, 3 * width), low),
            pltpu.VMEM((2, 8, width), full),
            pltpu.SemaphoreType.DMA((3,)),
            pltpu.SemaphoreType.DMA((2,)),
            pltpu.SemaphoreType.DMA((2,)),
        ],
        steps=steps,
    )


def alone(beside):
    def kernel(*refs):
        a, b = len(beside.ins), len(beside.ins) + len(beside.outs)
        for step in beside.steps(refs[:a], refs[a:b], refs[b:]):
            step()

    return pl.pallas_call(
        kernel,
        out_shape=beside.outs,
        in_specs=list(beside.in_specs),
        out_specs=[ANYWHERE] * len(beside.outs),
        scratch_shapes=list(beside.scratch),
        compiler_params=pltpu.CompilerParams(vmem_limit_bytes=40 << 20),
    )(*beside.ins)


def gathered_body(
    dims,
    tokens,
    w_qkv,
    w_out,
    w_router,
    gains,
    w_gate,
    w_up,
    w_down,
    lengths,
    routes,
    send_counts,
    cotangent,
):
    row_count = tokens.shape[1]
    top_count = routes.shape[2]
    expert_count = w_router.shape[1]
    owners = math.prod(dims)
    weight_rows = w_qkv.shape[0]
    capacity = row_count * top_count // expert_count
    slots_all = row_count * 2 * owners
    balance_factor = float(expert_count) / (float(top_count) * float(slots_all) * float(slots_all))
    low = jnp.bfloat16
    full = jnp.float32
    chips = Grid(dims)
    devices = Grid(dims, cores=True)
    z, y, x = 0, 1, 2
    row_orders = [(x, z, y), (y, z, x), (z, x, y), (z, y, x)]
    row_shares = [5 * row_count // 16, 5 * row_count // 16, 3 * row_count // 16, 3 * row_count // 16]
    quarter = [weight_rows // 4] * 4
    wide_orders = [tuple(d + 1 for d in order) + (0,) for order in row_orders]
    late_shares = [row_count // 4, row_count // 4, row_count // 8, row_count // 8]
    narrow_orders = [order[:-1] for order in wide_orders]
    expert = lax.axis_index("expert")
    core = lax.axis_index("dp")
    swap = [(0, 1), (1, 0)]

    small = jnp.concatenate(
        [w_router, gains.T, jnp.zeros((weight_rows, 128 - expert_count - 4), low)], axis=1
    )
    qkv_all, small_all = gather(
        [w_qkv, small], devices, cut(0, quarter, wide_orders) + cut(1, [weight_rows], wide_orders[2:3]), 1
    )
    small_all = small_all.reshape(D, 128)
    router_weight = small_all[:, :expert_count]
    gain_float = small_all[:, expert_count : expert_count + 4].T.astype(full)
    qkv_weight = qkv_all.reshape(D, 3 * D)
    gate_own, up_own, down_own = w_gate[0], w_up[0], w_down[0]
    gate_far, up_far, down_far = (lax.ppermute(w, "dp", swap) for w in (gate_own, up_own, down_own))

    positions = jnp.arange(row_count, dtype=jnp.int32)
    live_slots = positions < lengths[0]
    live_float = live_slots.astype(full)[:, None]
    expert_ids = jnp.arange(expert_count, dtype=jnp.int32)
    named = jnp.any(routes[0][:, :, None] == expert_ids, axis=1) & live_slots[:, None]
    before = (positions[None, :] < positions[:, None]).astype(low)
    rank = jnp.dot(before, named.astype(low), preferred_element_type=full)
    limit = jnp.minimum(send_counts[0], capacity).astype(full)
    kept = named & (rank < limit[None, :])
    kept_rank = jnp.where(kept, rank, -1.0)

    cosine, sine = (table[:, 0] for table in rope_tables(row_count, HEAD))
    sine = jnp.concatenate([-sine[:, : HEAD // 2], sine[:, HEAD // 2 :]], axis=1)
    early = row_count // 4
    out_all, cot_early, normed, qk_parts, queries, keys_low, values_low, mixed_low, probs = gather(
        [w_out, cotangent[0, :early]],
        devices,
        cut(0, quarter, wide_orders) + cut(1, [early // 4] * 4, narrow_orders),
        7,
        attend_beside(tokens[0], gain_float, qkv_weight, live_slots[None, :].astype(full), cosine, sine),
    )
    out_weight = out_all.reshape(D, D)
    inputs = tokens[0].astype(full)
    _, attn_norm_back = jax.vjp(norm_scale, inputs, gain_float[0])
    hidden_state = inputs + jnp.dot(mixed_low, out_weight, preferred_element_type=full)
    ffn_in, ffn_norm_back = jax.vjp(norm_scale, hidden_state, gain_float[3])
    ffn_low = ffn_in.astype(low)
    logits = jnp.dot(ffn_low, router_weight, preferred_element_type=full)
    router_probs = jax.nn.softmax(logits, axis=-1)
    prob_local = jnp.sum(router_probs * live_float, axis=0)
    sums = jnp.concatenate([send_counts[0].astype(full), prob_local])
    aside = jnp.concatenate(
        [
            jnp.where(kept, router_probs, 0.0).T,
            kept_rank.T,
            jnp.pad(sums[None, :], ((0, 7), (0, row_count - 2 * expert_count))),
        ],
        axis=0,
    )

    ffn_rows, aside_rows = gather(
        [ffn_low, aside],
        chips,
        cut(0, row_shares, row_orders) + cut(1, [aside.shape[0]], row_orders[2:3]),
        3,
    )
    sums_core = jnp.sum(aside_rows[:, 2 * expert_count, : 2 * expert_count], axis=0)
    sums_all = sums_core + lax.ppermute(sums_core, "dp", swap)
    count_total, prob_total = sums_all[:expert_count], sums_all[expert_count:]
    balance = jnp.sum(count_total * prob_total) * balance_factor
    weight_of = lax.dynamic_index_in_dim(aside_rows, expert, 1, keepdims=False)
    rank_of = lax.dynamic_index_in_dim(aside_rows, expert_count + expert, 1, keepdims=False)
    halves = (gate_own, gate_far, up_own, up_far, down_own, down_far)
    cot_late, rows_in, gate_pre, up_pre, units, expert_out, mixture_part = gather(
        [cotangent[0, early:]],
        chips,
        cut(0, late_shares, row_orders),
        2,
        forward_beside(ffn_rows, rank_of, rank_of.T, weight_of.T, halves, capacity),
    )
    mixture, grad_rows, grad_gate, grad_up, back_part, dot_route = scatter(
        [mixture_part],
        chips,
        cut(0, row_shares, row_orders),
        5,
        backward_beside(
            cot_early, cot_late, rank_of, rank_of.T, weight_of, gate_pre, up_pre, expert_out, halves, capacity
        ),
    )
    route_part = jnp.where((expert_ids == expert)[None, :, None], dot_route[:, None, :], 0.0)
    grad_ffn, grad_route, *halves_grads = scatter(
        [back_part, route_part],
        chips,
        cut(0, row_shares, row_orders) + cut(1, [expert_count], row_orders[2:3]),
        4,
        outer_beside(rows_in, grad_rows, grad_gate, grad_up, units),
    )
    expert_grads = [
        (own + lax.ppermute(far, "dp", swap).astype(full))[None]
        for own, far in zip(halves_grads[::2], halves_grads[1::2])
    ]
    result = (live_float * (hidden_state + mixture)).astype(low)[None]

    balance_coef = BALANCE_WEIGHT * balance_factor
    grad_probs = grad_route.T + balance_coef * count_total[None, :] * live_float
    grad_logits = router_probs * (
        grad_probs - jnp.sum(router_probs * grad_probs, axis=-1, keepdims=True)
    )
    grad_logits_low = grad_logits.astype(low)
    grad_ffn = grad_ffn + jnp.einsum("te,de->td", grad_logits_low, router_weight, preferred_element_type=full)
    grad_router_w = jnp.einsum("td,te->de", ffn_low, grad_logits_low, preferred_element_type=full)

    grad_layer = cotangent[0].astype(full) * live_float
    grad_hidden_part, grad_gain_ffn = ffn_norm_back(grad_ffn)
    grad_hidden_state = grad_layer + grad_hidden_part
    grad_attn_low = grad_hidden_state.astype(low)
    grad_projected, head_sums = alone(
        attend_back_beside(
            grad_attn_low, out_weight, queries, keys_low, values_low, probs, qk_parts, gain_float, cosine, sine
        )
    )
    grad_gain_query, grad_gain_key = jnp.sum(head_sums, axis=1)
    grad_normed = jnp.einsum("te,de->td", grad_projected, qkv_weight, preferred_element_type=full)
    grad_input_part, grad_gain_attn = attn_norm_back(grad_normed)
    grad_inputs = grad_hidden_state + grad_input_part
    grad_gain_rows = jnp.stack([grad_gain_attn, grad_gain_query, grad_gain_key, grad_gain_ffn])

    def outer(left, right):
        return jnp.einsum("sa,sb->ab", left, right, preferred_element_type=full)

    small_grads = jnp.concatenate(
        [grad_router_w, grad_gain_rows.T, jnp.zeros((D, 128 - expert_count - 4), full)], axis=1
    )
    shares = [
        g.reshape(devices.size, weight_rows, g.shape[1])
        for g in (outer(normed, grad_projected).astype(low), outer(mixed_low, grad_attn_low).astype(low), small_grads)
    ]
    grad_qkv, grad_out, grad_small = scatter(
        shares,
        devices,
        cut(0, quarter, wide_orders)
        + cut(1, quarter, wide_orders[:2] * 2)
        + cut(2, [weight_rows], wide_orders[2:3]),
        6,
    )
    return (
        result,
        grad_inputs[None],
        grad_qkv,
        grad_out,
        grad_small[:, :expert_count],
        grad_small[:, expert_count : expert_count + 4].T,
        *expert_grads,
        balance,
    )


def solution(mesh):
    dims = {4: (1, 2, 2), 8: (2, 2, 2), 16: (4, 2, 2)}.get(mesh.shape["expert"])
    plan = routed_body if dims is None or mesh.shape["dp"] != 2 else functools.partial(gathered_body, dims)
    placed = (
        P(("dp", "expert"), None, None),
        P(("dp", "expert"), None),
        P(("dp", "expert"), None),
        P(("dp", "expert"), None),
        P(None, ("dp", "expert")),
        P("expert", None, "dp"),
        P("expert", None, "dp"),
        P("expert", "dp", None),
        P(("dp", "expert")),
        P(("dp", "expert"), None, None),
        P(("dp", "expert"), None),
        P(("dp", "expert"), None, None),
    )
    return jax.shard_map(
        plan,
        mesh=mesh,
        in_specs=placed,
        out_specs=(
            P(("dp", "expert"), None, None),
            P(("dp", "expert"), None, None),
            P(("dp", "expert"), None),
            P(("dp", "expert"), None),
            P(("dp", "expert"), None),
            P(None, ("dp", "expert")),
            P("expert", None, "dp"),
            P("expert", None, "dp"),
            P("expert", "dp", None),
            P(),
        ),
        check_vma=False,
    )
```

```python
import functools
import itertools
import math

import jax
import jax.numpy as jnp
from jax import lax
from jax.experimental import pallas as pl
from jax.experimental.pallas import tpu as pltpu
from jax.sharding import PartitionSpec as P

D = 2048
HEADS = 16
HEAD = 128


NORM_EPS = 1e-05
BALANCE_WEIGHT = 0.01


def norm_scale(values, gain_row):
    return (
        values * lax.rsqrt(jnp.mean(values * values, axis=-1, keepdims=True) + NORM_EPS) * gain_row
    )


def rope_tables(positions_count, head_width):
    half_width = head_width // 2
    frequency = jnp.exp(
        jnp.arange(half_width, dtype=jnp.float32) * (-2.0 * math.log(10000.0) / head_width)
    )
    angles = jnp.arange(positions_count, dtype=jnp.float32)[:, None] * frequency[None, :]
    angles = jnp.concatenate([angles, angles], axis=1)
    return (jnp.cos(angles)[:, None, :], jnp.sin(angles)[:, None, :])


def rotate(values, cosine, sine_part):
    half_width = values.shape[-1] // 2
    turned = jnp.concatenate([-values[..., half_width:], values[..., :half_width]], axis=-1)
    return values * cosine + turned * sine_part


def query_key(query_part, key_part, query_gain, key_gain):
    positions_count = query_part.shape[0]
    cosine, sine_part = rope_tables(positions_count, HEAD)
    queries = norm_scale(query_part, query_gain).reshape(positions_count, HEADS, HEAD)
    key_heads = norm_scale(key_part, key_gain).reshape(positions_count, HEADS, HEAD)
    return (rotate(queries, cosine, sine_part), rotate(key_heads, cosine, sine_part))


def expert_forward(rows_in, gate_weight, up_weight, down_weight):
    gate_pre = jnp.einsum(
        "nkcd,kdf->nkcf", rows_in, gate_weight, preferred_element_type=jnp.float32
    )
    up_pre = jnp.einsum("nkcd,kdf->nkcf", rows_in, up_weight, preferred_element_type=jnp.float32)
    hidden_low = (jax.nn.silu(gate_pre) * up_pre).astype(jnp.bfloat16)
    output = jnp.einsum(
        "nkcf,kfd->nkcd", hidden_low, down_weight, preferred_element_type=jnp.float32
    )
    return (gate_pre, up_pre, hidden_low, output)


def routed_body(
    tokens,
    w_qkv,
    w_out,
    w_router,
    gains,
    w_gate,
    w_up,
    w_down,
    lengths,
    routes,
    send_counts,
    cotangent,
):
    row_count = tokens.shape[1]
    top_count = routes.shape[2]
    expert_count = w_router.shape[1]
    owners = lax.axis_size("expert")
    local_experts = expert_count // owners
    capacity = row_count * top_count // expert_count
    slots_all = row_count * lax.axis_size("dp") * owners
    balance_factor = float(expert_count) / (float(top_count) * float(slots_all) * float(slots_all))
    score_scale = HEAD ** (-0.5)
    inputs = tokens[0].astype(jnp.float32)
    positions = jnp.arange(row_count, dtype=jnp.int32)
    live_slots = positions < lengths[0]
    live_float = live_slots.astype(jnp.float32)[:, None]
    mixer_parts = (
        lax.all_gather(w_qkv, ("dp", "expert"), axis=0, tiled=True),
        lax.all_gather(w_out, ("dp", "expert"), axis=0, tiled=True),
        lax.all_gather(w_router, ("dp", "expert"), axis=0, tiled=True),
        lax.all_gather(gains, ("dp", "expert"), axis=1, tiled=True),
    )
    qkv_weight, out_weight, router_weight, gain_rows = mixer_parts
    gain_float = gain_rows.astype(jnp.float32)
    attn_in, attn_norm_back = jax.vjp(norm_scale, inputs, gain_float[0])
    normed = attn_in.astype(jnp.bfloat16)
    projected = jnp.dot(normed, qkv_weight, preferred_element_type=jnp.float32)
    (rot_query, rot_keys), query_key_back = jax.vjp(
        query_key, projected[:, :D], projected[:, D : 2 * D], gain_float[1], gain_float[2]
    )
    queries = rot_query.astype(jnp.bfloat16)
    keys_low = rot_keys.astype(jnp.bfloat16)
    values_low = projected[:, 2 * D :].astype(jnp.bfloat16).reshape(row_count, HEADS, HEAD)
    allowed = (positions[None, :] <= positions[:, None]) & live_slots[None, :]
    scores = (
        jnp.einsum("qhd,khd->hqk", queries, keys_low, preferred_element_type=jnp.float32)
        * score_scale
    )
    scores = jnp.where(allowed[None], scores, -1e30)
    highest = jnp.max(scores, axis=-1, keepdims=True)
    expo_scores = jnp.exp(scores - highest)
    totals = jnp.sum(expo_scores, axis=-1, keepdims=True)
    attn_probs = expo_scores / totals
    log_total = highest + jnp.log(totals)
    mixed_heads = jnp.einsum(
        "hqk,khd->qhd",
        attn_probs.astype(jnp.bfloat16),
        values_low,
        preferred_element_type=jnp.float32,
    )
    mixed_low = mixed_heads.reshape(row_count, D).astype(jnp.bfloat16)
    hidden_state = inputs + jnp.dot(mixed_low, out_weight, preferred_element_type=jnp.float32)
    ffn_in, ffn_norm_back = jax.vjp(norm_scale, hidden_state, gain_float[3])
    ffn_low = ffn_in.astype(jnp.bfloat16)
    logits = jnp.dot(ffn_low, router_weight, preferred_element_type=jnp.float32)
    router_probs = jax.nn.softmax(logits, axis=-1)
    count_float = send_counts[0].astype(jnp.float32)
    prob_local = jnp.sum(router_probs * live_float, axis=0)
    count_total, prob_total = lax.psum((count_float, prob_local), ("dp", "expert"))
    balance = jnp.sum(count_total * prob_total) * balance_factor
    route_rows = routes[0]
    expert_ids = jnp.arange(expert_count, dtype=jnp.int32)
    route_hot = (route_rows[:, :, None] == expert_ids) & live_slots[:, None, None]
    route_int = route_hot.astype(jnp.int32)
    per_token = jnp.sum(route_int, axis=1)
    earlier = jnp.cumsum(per_token, axis=0) - per_token
    route_rank = jnp.sum(earlier[:, None, :] * route_int, axis=-1)
    limits = jnp.sum(jnp.minimum(send_counts[0], capacity)[None, None, :] * route_int, axis=-1)
    kept_route = route_rank < limits
    target_expert = jnp.where(kept_route, route_rows, expert_count)
    target_slot = jnp.where(kept_route, route_rank, 0)
    token_ids = jnp.broadcast_to(positions[:, None], route_rows.shape)
    source = (
        jnp.full((expert_count, capacity), row_count, jnp.int32)
        .at[target_expert, target_slot]
        .set(token_ids, mode="drop")
    )
    padded_in = jnp.concatenate([ffn_low, jnp.zeros((1, D), jnp.bfloat16)], axis=0)
    send_rows = padded_in[source].reshape(owners, local_experts, capacity, D)
    expert_weights = (w_gate, w_up, w_down)
    gathered = lax.all_gather(
        lax.all_to_all(send_rows, "expert", split_axis=0, concat_axis=0, tiled=True),
        "dp",
        axis=0,
        tiled=True,
    )
    gate_pre, up_pre, hidden_low, partial_out = expert_forward(gathered, w_gate, w_up, w_down)
    summed = lax.psum_scatter(
        partial_out.astype(jnp.bfloat16), "dp", scatter_dimension=0, tiled=True
    )
    expert_out, expert_rows, gate_pre, up_pre, hidden_low = (
        summed,
        gathered,
        gate_pre,
        up_pre,
        hidden_low,
    )
    returned = lax.all_to_all(
        expert_out, "expert", split_axis=0, concat_axis=0, tiled=True
    ).reshape(expert_count * capacity, D)
    flat_index = jnp.where(kept_route, route_rows * capacity + route_rank, 0)
    picked = returned[flat_index]
    route_prob = jnp.sum(router_probs[:, None, :] * route_hot.astype(jnp.float32), axis=-1)
    combine_weight = jnp.where(kept_route, route_prob, 0.0)
    mixture = jnp.sum(combine_weight[:, :, None] * picked, axis=1)
    layer = live_float * (hidden_state + mixture)
    result = layer.astype(jnp.bfloat16)[None]
    qkv_back, out_back, router_back = (
        lax.all_gather(w_qkv, ("dp", "expert"), axis=0, tiled=True),
        lax.all_gather(w_out, ("dp", "expert"), axis=0, tiled=True),
        lax.all_gather(w_router, ("dp", "expert"), axis=0, tiled=True),
    )
    grad_layer = cotangent[0].astype(jnp.float32) * live_float
    dot_route = jnp.sum(grad_layer[:, None, :] * picked, axis=-1)
    balance_coef = BALANCE_WEIGHT * balance_factor
    grad_probs = jnp.sum(
        jnp.where(kept_route, dot_route, 0.0)[:, :, None] * route_hot.astype(jnp.float32), axis=1
    )
    grad_probs = grad_probs + balance_coef * count_total[None, :] * live_float
    grad_logits = router_probs * (
        grad_probs - jnp.sum(router_probs * grad_probs, axis=-1, keepdims=True)
    )
    grad_logits_low = grad_logits.astype(jnp.bfloat16)
    route_scale = (
        jnp.zeros((expert_count, capacity), jnp.float32)
        .at[target_expert, target_slot]
        .set(combine_weight, mode="drop")
    )
    padded_grad = jnp.concatenate([grad_layer, jnp.zeros((1, D), jnp.float32)], axis=0)
    grad_send = (
        (padded_grad[source] * route_scale[:, :, None])
        .astype(jnp.bfloat16)
        .reshape(owners, local_experts, capacity, D)
    )
    arrived = lax.all_to_all(grad_send, "expert", split_axis=0, concat_axis=0, tiled=True)
    grad_rows_all = lax.all_gather(arrived, "dp", axis=0, tiled=True)
    gate_weight, up_weight, down_weight = expert_weights
    grad_down_w = jnp.einsum(
        "nkcf,nkcd->kfd", hidden_low, grad_rows_all, preferred_element_type=jnp.float32
    )
    grad_units = jnp.einsum(
        "nkcd,kfd->nkcf", grad_rows_all, down_weight, preferred_element_type=jnp.float32
    )
    gate_sigmoid = jax.nn.sigmoid(gate_pre)
    grad_gate_low = (
        grad_units * up_pre * gate_sigmoid * (1.0 + gate_pre * (1.0 - gate_sigmoid))
    ).astype(jnp.bfloat16)
    grad_up_low = (grad_units * gate_pre * gate_sigmoid).astype(jnp.bfloat16)
    grad_gate_w = jnp.einsum(
        "nkcd,nkcf->kdf", expert_rows, grad_gate_low, preferred_element_type=jnp.float32
    )
    grad_up_w = jnp.einsum(
        "nkcd,nkcf->kdf", expert_rows, grad_up_low, preferred_element_type=jnp.float32
    )
    back_part = jnp.einsum(
        "nkcf,kdf->nkcd", grad_gate_low, gate_weight, preferred_element_type=jnp.float32
    )
    back_part = back_part + jnp.einsum(
        "nkcf,kdf->nkcd", grad_up_low, up_weight, preferred_element_type=jnp.float32
    )
    back_rows = lax.psum_scatter(
        back_part.astype(jnp.bfloat16), "dp", scatter_dimension=0, tiled=True
    )
    expert_grads = (grad_gate_w, grad_up_w, grad_down_w)
    sent_back = lax.all_to_all(
        back_rows, "expert", split_axis=0, concat_axis=0, tiled=True
    ).reshape(expert_count * capacity, D)
    grad_ffn = jnp.einsum(
        "tj,tjd->td",
        kept_route.astype(jnp.bfloat16),
        sent_back[flat_index],
        preferred_element_type=jnp.float32,
    )
    grad_ffn = grad_ffn + jnp.einsum(
        "te,de->td", grad_logits_low, router_back, preferred_element_type=jnp.float32
    )
    grad_router_w = jnp.einsum(
        "td,te->de", ffn_low, grad_logits_low, preferred_element_type=jnp.float32
    )
    grad_hidden_part, grad_gain_ffn = ffn_norm_back(grad_ffn)
    grad_hidden_state = grad_layer + grad_hidden_part
    grad_attn_low = grad_hidden_state.astype(jnp.bfloat16)
    grad_out_w = jnp.einsum(
        "td,te->de", mixed_low, grad_attn_low, preferred_element_type=jnp.float32
    )
    grad_mixed = jnp.einsum(
        "te,de->td", grad_attn_low, out_back, preferred_element_type=jnp.float32
    )
    grad_mixed = grad_mixed.astype(jnp.bfloat16).reshape(row_count, HEADS, HEAD)
    scores_again = (
        jnp.einsum("qhd,khd->hqk", queries, keys_low, preferred_element_type=jnp.float32)
        * score_scale
    )
    probs_again = jnp.where(allowed[None], jnp.exp(scores_again - log_total), 0.0)
    grad_values = jnp.einsum(
        "hqk,qhd->khd",
        probs_again.astype(jnp.bfloat16),
        grad_mixed,
        preferred_element_type=jnp.float32,
    )
    grad_attn_probs = jnp.einsum(
        "qhd,khd->hqk", grad_mixed, values_low, preferred_element_type=jnp.float32
    )
    grad_scores = probs_again * (
        grad_attn_probs - jnp.sum(probs_again * grad_attn_probs, axis=-1, keepdims=True)
    )
    grad_scores_low = grad_scores.astype(jnp.bfloat16)
    grad_queries = (
        jnp.einsum("hqk,khd->qhd", grad_scores_low, keys_low, preferred_element_type=jnp.float32)
        * score_scale
    )
    grad_keys = (
        jnp.einsum("hqk,qhd->khd", grad_scores_low, queries, preferred_element_type=jnp.float32)
        * score_scale
    )
    grad_query_part, grad_key_part, grad_gain_query, grad_gain_key = query_key_back(
        (grad_queries, grad_keys)
    )
    grad_projected = jnp.concatenate(
        [grad_query_part, grad_key_part, grad_values.reshape(row_count, D)], axis=1
    ).astype(jnp.bfloat16)
    grad_qkv_w = jnp.einsum("td,te->de", normed, grad_projected, preferred_element_type=jnp.float32)
    grad_normed = jnp.einsum(
        "te,de->td", grad_projected, qkv_back, preferred_element_type=jnp.float32
    )
    grad_input_part, grad_gain_attn = attn_norm_back(grad_normed)
    grad_inputs = grad_hidden_state + grad_input_part
    grad_gain_rows = jnp.stack([grad_gain_attn, grad_gain_query, grad_gain_key, grad_gain_ffn])
    mixer_grads = (
        lax.psum_scatter(grad_qkv_w, ("dp", "expert"), scatter_dimension=0, tiled=True),
        lax.psum_scatter(grad_out_w, ("dp", "expert"), scatter_dimension=0, tiled=True),
        lax.psum_scatter(grad_router_w, ("dp", "expert"), scatter_dimension=0, tiled=True),
        lax.psum_scatter(grad_gain_rows, ("dp", "expert"), scatter_dimension=1, tiled=True),
    )
    return (
        result,
        grad_inputs[None],
        mixer_grads[0],
        mixer_grads[1],
        mixer_grads[2],
        mixer_grads[3],
        expert_grads[0],
        expert_grads[1],
        expert_grads[2],
        balance,
    )


MESH = pl.DeviceIdType.MESH


class Grid:
    def __init__(self, dims, cores=False):
        self.cores = cores
        self.dims = ((2,) if cores else ()) + tuple(dims)
        self.size = math.prod(self.dims)
        self.strides = [math.prod(self.dims[d + 1 :]) for d in range(len(self.dims))]
        self.lanes = {}
        for d in range(len(self.dims)):
            for side in self.sides(d):
                self.lanes[(d, side)] = len(self.lanes)

    def coords(self):
        expert = lax.axis_index("expert")
        c = [lax.axis_index("dp")] if self.cores else []
        first = len(c)
        for d in range(first, len(self.dims)):
            c.append(lax.rem(expert // self.strides[d], self.dims[d]))
        return c

    def rels(self, d):
        n = self.dims[d]
        if n == 1:
            return []
        if n == 2:
            return [(1, 0)]
        return [(k, side) for k in range(1, n) for side in (-1, 1)]

    def sides(self, d):
        n = self.dims[d]
        return [] if n == 1 else [0] if n == 2 else [-1, 1]

    def at(self, c, d, rel):
        k, side = rel
        return 1 - c[d] if side == 0 else c[d] + side * k

    def valid(self, c, d, rel):
        k, side = rel
        if side == 0:
            return None
        return c[d] - k >= 0 if side < 0 else c[d] + k < self.dims[d]

    def index(self, coords):
        return sum(x * s for x, s in zip(coords, self.strides))

    def neighbor(self, c, d, side):
        other = list(c)
        other[d] = self.at(c, d, (1, side))
        ok = self.valid(c, d, (1, side))
        if self.cores and d == 0:
            return {"dp": other[0]}, ok
        first = 1 if self.cores else 0
        expert = sum(x * s for x, s in zip(other[first:], self.strides[first:]))
        return {"expert": expert}, ok

    def events(self, order):
        return [
            dict(zip(order, combo))
            for combo in itertools.product(*[[None] + self.rels(d) for d in order])
        ]

    def place(self, c, order, event):
        pred, o, last = None, list(c), -1
        for i, d in enumerate(order):
            if event[d]:
                pred = both(pred, self.valid(c, d, event[d]))
                o[d] = self.at(c, d, event[d])
                last = i
        return o, pred, last


def both(a, b):
    if a is None:
        return b
    if b is None:
        return a
    return jnp.logical_and(a, b)


def when(pred, f):
    if pred is None:
        f()
    else:
        pl.when(pred)(f)


def greet(grid, c):
    barrier = pltpu.get_barrier_semaphore()
    total = jnp.int32(0)
    for d, side in grid.lanes:
        device, ok = grid.neighbor(c, d, side)
        when(
            ok,
            lambda device=device: pl.semaphore_signal(
                barrier, inc=1, device_id=device, device_id_type=MESH
            ),
        )
        total = total + (1 if ok is None else ok.astype(jnp.int32))
    pl.semaphore_wait(barrier, total)


def farthest(order, event):
    return tuple(event[d][0] if event[d] else 0 for d in reversed(order))


class Beside:
    def __init__(self, ins=(), in_specs=(), outs=(), scratch=(), steps=None, lead=0.0, span=1.0):
        self.lead, self.span = lead, span
        self.ins, self.in_specs, self.outs, self.scratch = ins, in_specs, outs, scratch
        self.steps = steps

    def share(self, refs, count, own_scratch):
        cuts = [count, len(self.ins), count, len(self.outs), own_scratch, len(self.scratch)]
        groups, at = [], 0
        for n in cuts:
            groups.append(refs[at : at + n])
            at += n
        steps = self.steps(groups[1], groups[3], groups[5], groups[2]) if self.steps else []
        return groups[0], groups[2], groups[4], steps


def mingle(events, gate, steps, free, lead, span):
    for event in events[:free]:
        event()
    gate()
    first = round(lead * len(steps))
    for step in steps[:first]:
        step()
    rest, left = events[free:], steps[first:]
    done = 0
    for n, event in enumerate(rest):
        event()
        while done < len(left) and done * len(rest) * span < (n + 1) * len(left):
            left[done]()
            done += 1
    for step in left[done:]:
        step()


def gather_kernel(grid, parts, lags, count, beside, *refs):
    srcs, outs, (send_sem, recv_sem, own_sem), steps = beside.share(refs, count, 3)
    c = grid.coords()
    me = grid.index(c)
    own = [pltpu.make_async_copy(s, o.at[me], own_sem.at[i]) for i, (s, o) in enumerate(zip(srcs, outs))]
    for copy in own:
        copy.start()
    greet(grid, c)
    sent = []

    def piece(p, ref):
        _, row0, rows, _ = parts[p]
        return ref.at[pl.ds(row0, rows)]

    def push(p, origin, source, d, side, pred):
        device, ok = grid.neighbor(c, d, side)
        pred = both(pred, ok)
        copy = pltpu.make_async_remote_copy(
            src_ref=source,
            dst_ref=piece(p, outs[parts[p][0]].at[origin]),
            send_sem=send_sem.at[p, origin, grid.lanes[(d, side)]],
            recv_sem=recv_sem.at[p, origin],
            device_id=device,
            device_id_type=MESH,
        )
        when(pred, copy.start)
        sent.append((pred, copy))

    todo = []
    for lag in sorted(set(lags)):
        group = []
        for p, (_, _, _, order) in enumerate(parts):
            if lags[p] == lag:
                group += [(farthest(order, event), p, event) for event in grid.events(order)]
        group.sort(key=lambda t: t[:2])
        todo += [(lag + n / len(group), p, event) for n, (_, p, event) in enumerate(group)]
    todo.sort(key=lambda t: t[0])
    free = 1 + max(n for n, (_, p, _) in enumerate(todo) if lags[p] == 0)
    if len(set(lags)) == 1:
        free = len(parts)

    def gate():
        for copy in own:
            copy.wait()

    def handle(p, event):
        a, _, _, order = parts[p]
        o, pred, last = grid.place(c, order, event)
        origin = grid.index(o)
        if last < 0:
            source = piece(p, srcs[a])
        else:
            source = piece(p, outs[a].at[origin])
            arrival = pltpu.make_async_remote_copy(
                src_ref=source,
                dst_ref=source,
                send_sem=send_sem.at[p, origin, 0],
                recv_sem=recv_sem.at[p, origin],
                device_id={"expert": lax.axis_index("expert")},
                device_id_type=MESH,
            )
            when(pred, arrival.wait_recv)
            side = event[order[last]][1]
            if side:
                push(p, origin, source, order[last], -side, pred)
        for d in order[last + 1 :]:
            for side in grid.sides(d):
                push(p, origin, source, d, side, pred)

    events = [functools.partial(handle, p, event) for _, p, event in todo]
    mingle(events, gate, steps, free, beside.lead, beside.span)
    for pred, copy in sent:
        when(pred, copy.wait_send)


def gather(arrays, grid, parts, cid, beside=Beside(), lags=None):
    lags = lags or (0,) * len(parts)
    n, count = grid.size, len(arrays)
    return pl.pallas_call(
        functools.partial(gather_kernel, grid, parts, lags, count, beside),
        out_shape=[jax.ShapeDtypeStruct((n,) + x.shape, x.dtype) for x in arrays] + list(beside.outs),
        in_specs=[pl.BlockSpec(memory_space=pl.ANY)] * count + list(beside.in_specs),
        out_specs=[pl.BlockSpec(memory_space=pl.ANY)] * (count + len(beside.outs)),
        scratch_shapes=[
            pltpu.SemaphoreType.DMA((len(parts), n, len(grid.lanes))),
            pltpu.SemaphoreType.DMA((len(parts), n)),
            pltpu.SemaphoreType.DMA((count,)),
        ]
        + list(beside.scratch),
        compiler_params=pltpu.CompilerParams(
            collective_id=cid, has_side_effects=True, vmem_limit_bytes=60 << 20
        ),
    )(*arrays, *beside.ins)


def landing_slots(grid, order):
    base, total, earlier = {}, 0, 1
    for d in order:
        base[d] = total
        total += len(grid.rels(d)) * earlier
        earlier *= grid.dims[d]
    return base, total


def scatter_kernel(grid, parts, count, beside, *refs):
    k = len(parts)
    srcs, outs, scratch, steps = beside.share(refs, count, 2 * k + count + 4)
    held, mine, totals = scratch[:k], scratch[k : 2 * k], scratch[2 * k : 2 * k + count]
    send_sem, recv_sem, mine_sem, out_sem = scratch[2 * k + count :]
    c = grid.coords()

    def piece(p, ref):
        _, row0, rows, _ = parts[p]
        return ref.at[pl.ds(row0, rows)]

    def own_slot(order, o):
        slot = 0
        for d in order[:-1]:
            slot = slot * grid.dims[d] + o[d]
        return slot

    def landing(order, d, rel, o):
        base, _ = landing_slots(grid, order)
        slot = grid.rels(d).index(rel)
        for q in order[: order.index(d)]:
            slot = slot * grid.dims[q] + o[q]
        return base[d] + slot

    def own_copy(p, o):
        a, _, _, order = parts[p]
        slot = own_slot(order, o)
        return pltpu.make_async_copy(
            piece(p, srcs[a].at[grid.index(o)]), mine[p].at[slot], mine_sem.at[p, slot]
        )

    for p, (_, _, _, order) in enumerate(parts):
        for position in itertools.product(*[range(grid.dims[d]) for d in order[:-1]]):
            o = list(c)
            for d, v in zip(order[:-1], position):
                o[d] = v
            own_copy(p, o).start()
    greet(grid, c)
    todo = []
    for p, (_, _, _, order) in enumerate(parts):
        for event in grid.events(order):
            todo.append((tuple(-far for far in farthest(order, event)), p, event))
    todo.sort(key=lambda t: t[:2])
    sent = []

    def handle(p, event):
        a, row0, rows, order = parts[p]
        o, pred, last = grid.place(c, order, event)
        always, sometimes = [], []
        if last >= 0:
            far, side = event[order[last]]
            if side and far + 1 < grid.dims[order[last]]:
                _, ok = grid.neighbor(c, order[last], -side)
                sometimes.append((landing(order, order[last], (far + 1, side), o), ok))
        for d in order[last + 1 :]:
            for side in grid.sides(d):
                _, ok = grid.neighbor(c, d, side)
                slot = landing(order, d, (1, -side), o)
                if ok is None:
                    always.append(slot)
                else:
                    sometimes.append((slot, ok))
        final = last < 0
        if not always and not sometimes and not final:
            source = piece(p, srcs[a].at[grid.index(o)])
        else:
            source = mine[p].at[own_slot(order, o)]
            when(pred, own_copy(p, o).wait)
            steps = [(slot, ok) for slot, ok in sometimes]
            if always or final:
                steps.insert(0, (always, None))

            def add(slots, opening, final=final, source=source, p=p, row0=row0, rows=rows, a=a):
                for slot in slots:
                    landed = held[p].at[slot]
                    pltpu.make_async_remote_copy(
                        src_ref=landed,
                        dst_ref=landed,
                        send_sem=send_sem.at[p, 0],
                        recv_sem=recv_sem.at[p, slot],
                        device_id={"expert": lax.axis_index("expert")},
                        device_id_type=MESH,
                    ).wait_recv()
                tile = min(16, rows)

                @pl.loop(0, rows // tile)
                def _(t):
                    here = pl.ds(pl.multiple_of(t * tile, tile), tile)
                    there = pl.ds(pl.multiple_of(row0 + t * tile, tile), tile)
                    if final and not opening:
                        value = totals[a][there, :]
                    else:
                        value = source[here, :].astype(jnp.float32)
                    for slot in slots:
                        value = value + held[p][slot, here, :].astype(jnp.float32)
                    if final:
                        totals[a][there, :] = value
                    else:
                        source[here, :] = value.astype(source.dtype)

            for n, (slots, ok) in enumerate(steps):
                slots = slots if isinstance(slots, list) else [slots]
                when(both(pred, ok), functools.partial(add, slots, n == 0))
        if last >= 0:
            d = order[last]
            device, _ = grid.neighbor(c, d, event[d][1])
            slot = landing(order, d, event[d], o)
            copy = pltpu.make_async_remote_copy(
                src_ref=source,
                dst_ref=held[p].at[slot],
                send_sem=send_sem.at[p, slot],
                recv_sem=recv_sem.at[p, slot],
                device_id=device,
                device_id_type=MESH,
            )
            when(pred, copy.start)
            sent.append((pred, copy))

    mingle(
        [functools.partial(handle, p, event) for _, p, event in todo],
        lambda: None,
        steps,
        sum(event[parts[p][3][-1]] is not None for _, p, event in todo),
        beside.lead,
        beside.span,
    )
    done = [pltpu.make_async_copy(t, o, out_sem.at[i]) for i, (t, o) in enumerate(zip(totals, outs))]
    for copy in done:
        copy.start()
    for pred, copy in sent:
        when(pred, copy.wait_send)
    for copy in done:
        copy.wait()


def scatter(arrays, grid, parts, cid, beside=Beside()):
    count = len(arrays)
    slots = [landing_slots(grid, order)[1] for _, _, _, order in parts]
    mine = [grid.size // grid.dims[order[-1]] for _, _, _, order in parts]
    blocks = [((rows, arrays[a].shape[2]), arrays[a].dtype) for a, _, rows, _ in parts]
    flat = [jax.ShapeDtypeStruct(x.shape[1:], jnp.float32) for x in arrays]
    return pl.pallas_call(
        functools.partial(scatter_kernel, grid, parts, count, beside),
        out_shape=flat + list(beside.outs),
        in_specs=[pl.BlockSpec(memory_space=pl.ANY)] * count + list(beside.in_specs),
        out_specs=[pl.BlockSpec(memory_space=pl.ANY)] * (count + len(beside.outs)),
        scratch_shapes=[pltpu.VMEM((s,) + b, t) for s, (b, t) in zip(slots, blocks)]
        + [pltpu.VMEM((s,) + b, t) for s, (b, t) in zip(mine, blocks)]
        + [pltpu.VMEM(x.shape, x.dtype) for x in flat]
        + [
            pltpu.SemaphoreType.DMA((len(parts), max(slots))),
            pltpu.SemaphoreType.DMA((len(parts), max(slots))),
            pltpu.SemaphoreType.DMA((len(parts), max(mine))),
            pltpu.SemaphoreType.DMA((count,)),
        ]
        + list(beside.scratch),
        compiler_params=pltpu.CompilerParams(
            collective_id=cid, has_side_effects=True, vmem_limit_bytes=60 << 20
        ),
    )(*arrays, *beside.ins)


def cut(array, shares, orders):
    starts = [sum(shares[:i]) for i in range(len(shares))]
    return tuple((array, start, share, order) for start, share, order in zip(starts, shares, orders))


def each_tile(total, width, f):
    @pl.loop(0, total // width, unroll=4)
    def _(t):
        f(pl.ds(pl.multiple_of(t * width, width), width))


def dot(left, right):
    return jnp.dot(left, right, preferred_element_type=jnp.float32)


def dot_across(left, right):
    return lax.dot_general(left, right, (((1,), (1,)), ((), ())), preferred_element_type=jnp.float32)


class Move:
    def __init__(self, *refs):
        self.refs = refs

    def start(self):
        pltpu.make_async_copy(*self.refs).start()

    def wait(self):
        pltpu.make_async_copy(*self.refs).wait()


ANYWHERE = pl.BlockSpec(memory_space=pl.ANY)
ON_CORE = pl.BlockSpec(memory_space=pltpu.VMEM)


def weight_copies(halves, held, sem):
    gate_own, gate_far, up_own, up_far, down_own, down_far = halves
    gate, up, down = held
    half = gate.shape[1] // 2
    own, far = pl.ds(0, half), pl.ds(half, half)
    pairs = [
        (gate_own, gate.at[:, own]),
        (gate_far, gate.at[:, far]),
        (up_own, up.at[:, own]),
        (up_far, up.at[:, far]),
        (down_own, down.at[own, :]),
        (down_far, down.at[far, :]),
    ]
    return [Move(a, b, sem.at[i]) for i, (a, b) in enumerate(pairs)]


def pick_of(ranks, row, capacity):
    line = ranks[row : row + 1, :]
    slot = lax.broadcasted_iota(jnp.int32, (capacity, line.shape[1]), 0).astype(jnp.float32)
    return line == slot


def put_of(ranks, row, capacity):
    line = ranks[:, row : row + 1]
    slot = lax.broadcasted_iota(jnp.int32, (line.shape[0], capacity), 1).astype(jnp.float32)
    return (line == slot).astype(jnp.float32).astype(jnp.bfloat16)


def forward_beside(shape, aside_shape, halves, capacity):
    row_count, tokens, width = shape
    expert_count = (aside_shape[1] - 8) // 2
    hidden = 2 * halves[0].shape[1]
    pairs, pair = row_count // 2, 2 * capacity
    slots = row_count * capacity
    low, full = jnp.bfloat16, jnp.float32

    def steps(ins, outs, scratch, arrivals):
        ffn_in = arrivals[0]
        weights, (ffn, xs, pre, units, out, mix), sems = scratch[:3], scratch[3:9], scratch[9:12]
        notes, ranks, ranks_t, weights_t, notes_sem = scratch[12:]
        load_sem, row_sem, out_sem = sems
        heavy = weight_copies(ins, weights, load_sem)
        notes_copy = Move(arrivals[1], notes, notes_sem)
        gate_w, up_w, down_w = weights

        def load(q):
            return Move(ffn_in.at[pl.ds(2 * q, 2)], ffn.at[q % 2], row_sem.at[q % 2])

        def leave(q):
            here = pl.ds(q * pair, pair)
            moves = [
                (xs, outs[0].at[here]),
                (pre.at[0], outs[1].at[here]),
                (pre.at[1], outs[2].at[here]),
                (units, outs[3].at[here]),
                (out, outs[4].at[here]),
                (mix, outs[5].at[pl.ds(2 * q, 2)]),
            ]
            return [Move(a, b, out_sem.at[i]) for i, (a, b) in enumerate(moves)]

        def opening():
            notes_copy.start()
            load(0).start()
            for copy in heavy:
                copy.start()
            notes_copy.wait()
            expert = lax.axis_index("expert")
            for first, kept in ((expert_count, ranks_t), (0, weights_t)):
                for row in range(row_count):
                    ranks[row : row + 1, :] = notes[row, pl.ds(first + expert, 1), :]
                kept[...] = ranks[...].T
            for row in range(row_count):
                ranks[row : row + 1, :] = notes[row, pl.ds(expert_count + expert, 1), :]

        def choose(q):
            load(q).wait()
            if q + 1 < pairs:
                load(q + 1).start()
            if q:
                leave(q - 1)[0].wait()
            for i in range(2):
                pick = pick_of(ranks, 2 * q + i, capacity).astype(full).astype(low)
                rows = pl.ds(i * capacity, capacity)

                def tile(cols, i=i, pick=pick, rows=rows):
                    xs[rows, cols] = dot(pick, ffn[q % 2, i, :, cols]).astype(low)

                each_tile(width, 512, tile)
            leave(q)[0].start()

        def widen(q):
            if q == 0:
                for copy in heavy[:4]:
                    copy.wait()
            else:
                for copy in leave(q - 1)[1:4]:
                    copy.wait()

            def tile(cols):
                gate = dot(xs[...], gate_w[:, cols])
                up = dot(xs[...], up_w[:, cols])
                pre[0, :, cols] = gate
                pre[1, :, cols] = up
                units[:, cols] = (gate * jax.nn.sigmoid(gate) * up).astype(low)

            each_tile(hidden, 256, tile)
            for copy in leave(q)[1:4]:
                copy.start()

        def narrow(q):
            if q == 0:
                for copy in heavy[4:]:
                    copy.wait()
            else:
                for copy in leave(q - 1)[4:]:
                    copy.wait()
            puts = [put_of(ranks_t, 2 * q + i, capacity) for i in range(2)]
            scales = [weights_t[:, 2 * q + i : 2 * q + i + 1] for i in range(2)]

            def tile(cols):
                value = dot(units[...], down_w[:, cols]).astype(low)
                out[:, cols] = value
                for i in range(2):
                    part = dot(puts[i], value[i * capacity : (i + 1) * capacity]) * scales[i]
                    mix[i, :, cols] = part.astype(low)

            each_tile(width, 256, tile)
            for copy in leave(q)[4:]:
                copy.start()

        def closing():
            for copy in leave(pairs - 1):
                copy.wait()

        listed = [opening]
        for q in range(pairs):
            listed += [functools.partial(f, q) for f in (choose, widen, narrow)]
        return listed + [closing]

    return Beside(
        ins=tuple(halves),
        in_specs=(ANYWHERE,) * 6,
        outs=[
            jax.ShapeDtypeStruct((slots, width), low),
            jax.ShapeDtypeStruct((slots, hidden), full),
            jax.ShapeDtypeStruct((slots, hidden), full),
            jax.ShapeDtypeStruct((slots, hidden), low),
            jax.ShapeDtypeStruct((slots, width), low),
            jax.ShapeDtypeStruct((row_count, tokens, width), low),
        ],
        scratch=[
            pltpu.VMEM((width, hidden), low),
            pltpu.VMEM((width, hidden), low),
            pltpu.VMEM((hidden, width), low),
            pltpu.VMEM((2, 2, tokens, width), low),
            pltpu.VMEM((pair, width), low),
            pltpu.VMEM((2, pair, hidden), full),
            pltpu.VMEM((pair, hidden), low),
            pltpu.VMEM((pair, width), low),
            pltpu.VMEM((2, tokens, width), low),
            pltpu.SemaphoreType.DMA((6,)),
            pltpu.SemaphoreType.DMA((2,)),
            pltpu.SemaphoreType.DMA((6,)),
            pltpu.VMEM(aside_shape, full),
            pltpu.VMEM((row_count, tokens), full),
            pltpu.VMEM((tokens, row_count), full),
            pltpu.VMEM((tokens, row_count), full),
            pltpu.SemaphoreType.DMA,
        ],
        steps=steps,
        span=0.7,
    )


def backward_beside(cot_early, cot_late, rank_rows, rank_cols, weight_rows, gate_pre, up_pre, expert_out, halves, capacity):
    row_count, late, width = cot_late.shape
    early = cot_early.shape[1]
    tokens = early + late
    hidden = 2 * halves[0].shape[1]
    pairs, pair = row_count // 2, 2 * capacity
    slots = row_count * capacity
    low, full = jnp.bfloat16, jnp.float32

    def steps(ins, outs, scratch, arrivals):
        early_in, late_in, ranks, ranks_t, weights, gate_in, up_in, out_in = ins[:8]
        heavy_refs, (cot, ge, pre, out, gg, gu, gx, dots, sums), sems = scratch[:3], scratch[3:12], scratch[12:]
        load_sem, row_sem, out_sem = sems
        heavy = weight_copies(ins[8:], heavy_refs, load_sem)
        gate_w, up_w, down_w = heavy_refs

        first = lax.axis_index("dp") * row_count

        def load(q):
            held = cot.at[q % 2]
            return [
                Move(early_in.at[pl.ds(first + 2 * q, 2)], held.at[:, pl.ds(0, early)], row_sem.at[q % 2]),
                Move(late_in.at[pl.ds(2 * q, 2)], held.at[:, pl.ds(early, late)], row_sem.at[5 + q % 2]),
            ]

        def fetch(q):
            here = pl.ds(q * pair, pair)
            moves = [(out_in, out), (gate_in, pre.at[0]), (up_in, pre.at[1])]
            return [Move(a.at[here], b, row_sem.at[2 + i]) for i, (a, b) in enumerate(moves)]

        def leave(q):
            here = pl.ds(q * pair, pair)
            moves = [(ge, outs[0].at[here]), (gg, outs[1].at[here]), (gu, outs[2].at[here])]
            moves.append((gx, outs[3].at[pl.ds(2 * q, 2)]))
            return [Move(a, b, out_sem.at[i]) for i, (a, b) in enumerate(moves)]

        last = Move(dots, outs[4], out_sem.at[4])

        def opening():
            for copy in load(0):
                copy.start()
            for copy in fetch(0):
                copy.start()
            for copy in heavy:
                copy.start()

        def choose(q):
            for copy in load(q):
                copy.wait()
            fetch(q)[0].wait()
            if q + 1 < pairs:
                for copy in load(q + 1):
                    copy.start()
            if q:
                leave(q - 1)[0].wait()
            for i in range(2):
                row = 2 * q + i
                pick = pick_of(ranks, row, capacity)
                pick_low = pick.astype(full).astype(low)
                scale = jnp.sum(jnp.where(pick, weights[row : row + 1, :], 0.0), axis=1, keepdims=True)
                rows = pl.ds(i * capacity, capacity)
                sums[...] = jnp.zeros_like(sums)

                def tile(cols, i=i, pick_low=pick_low, scale=scale, rows=rows):
                    value = dot(pick_low, cot[q % 2, i, :, cols])
                    ge[rows, cols] = (value * scale).astype(low)
                    product = value * out[rows, cols].astype(full)
                    total = product[:, :128]
                    for lane in range(128, product.shape[1], 128):
                        total = total + product[:, lane : lane + 128]
                    sums[...] += total

                each_tile(width, 512, tile)
                slot_dot = jnp.sum(sums[...], axis=1, keepdims=True)
                dots[row : row + 1, :] = jnp.sum(jnp.where(pick, slot_dot, 0.0), axis=0, keepdims=True)
            leave(q)[0].start()
            if q + 1 < pairs:
                fetch(q + 1)[0].start()

        def narrow(q):
            for copy in fetch(q)[1:]:
                copy.wait()
            if q == 0:
                for copy in heavy:
                    copy.wait()
            else:
                for copy in leave(q - 1)[1:3]:
                    copy.wait()

            def tile(cols):
                grad = dot_across(ge[...], down_w[cols, :])
                gate, up = pre[0, :, cols], pre[1, :, cols]
                sigmoid = jax.nn.sigmoid(gate)
                gg[:, cols] = (grad * up * sigmoid * (1.0 + gate * (1.0 - sigmoid))).astype(low)
                gu[:, cols] = (grad * gate * sigmoid).astype(low)

            each_tile(hidden, 256, tile)
            for copy in leave(q)[1:3]:
                copy.start()
            if q + 1 < pairs:
                for copy in fetch(q + 1)[1:]:
                    copy.start()

        def widen(q):
            if q:
                leave(q - 1)[3].wait()
            puts = [put_of(ranks_t, 2 * q + i, capacity) for i in range(2)]

            def tile(cols):
                value = dot_across(gg[...], gate_w[cols, :]) + dot_across(gu[...], up_w[cols, :])
                value = value.astype(low)
                for i in range(2):
                    part = dot(puts[i], value[i * capacity : (i + 1) * capacity])
                    gx[i, :, cols] = part.astype(low)

            each_tile(width, 256, tile)
            leave(q)[3].start()

        def closing():
            last.start()
            for copy in leave(pairs - 1):
                copy.wait()
            last.wait()

        listed = [opening]
        for q in range(pairs):
            listed += [functools.partial(f, q) for f in (choose, narrow, widen)]
        return listed + [closing]

    return Beside(
        ins=(cot_early, cot_late, rank_rows, rank_cols, weight_rows, gate_pre, up_pre, expert_out) + tuple(halves),
        in_specs=(ANYWHERE, ANYWHERE, ON_CORE, ON_CORE, ON_CORE) + (ANYWHERE,) * 9,
        outs=[
            jax.ShapeDtypeStruct((slots, width), low),
            jax.ShapeDtypeStruct((slots, hidden), low),
            jax.ShapeDtypeStruct((slots, hidden), low),
            jax.ShapeDtypeStruct((row_count, tokens, width), low),
            jax.ShapeDtypeStruct((row_count, tokens), full),
        ],
        scratch=[
            pltpu.VMEM((width, hidden), low),
            pltpu.VMEM((width, hidden), low),
            pltpu.VMEM((hidden, width), low),
            pltpu.VMEM((2, 2, tokens, width), low),
            pltpu.VMEM((pair, width), low),
            pltpu.VMEM((2, pair, hidden), full),
            pltpu.VMEM((pair, width), low),
            pltpu.VMEM((pair, hidden), low),
            pltpu.VMEM((pair, hidden), low),
            pltpu.VMEM((2, tokens, width), low),
            pltpu.VMEM((row_count, tokens), full),
            pltpu.VMEM((capacity, 128), full),
            pltpu.SemaphoreType.DMA((6,)),
            pltpu.SemaphoreType.DMA((7,)),
            pltpu.SemaphoreType.DMA((5,)),
        ],
        steps=steps,
        span=0.8,
    )


def outer_beside(rows_in, grad_rows, grad_gate, grad_up, units):
    slots, width = rows_in.shape
    hidden = units.shape[1]
    half = hidden // 2
    block = 256
    low, full = jnp.bfloat16, jnp.float32

    def steps(ins, outs, scratch, arrivals):
        rows_ref, grads_ref, gate_ref, up_ref, units_ref = ins
        left, turned, gate, up, grads, wide_own, wide_far, tall_own, tall_far, load_sem, left_sem, out_sem = scratch
        heavy = [
            Move(a, b, load_sem.at[i])
            for i, (a, b) in enumerate([(gate_ref, gate), (up_ref, up), (grads_ref, grads)])
        ]
        jobs = [(rows_ref, t) for t in range(width // block)] + [
            (units_ref, t) for t in range(hidden // block)
        ]

        def load(n):
            ref, t = jobs[n]
            return Move(
                ref.at[:, pl.ds(t * block, block)], left.at[n % 2], left_sem.at[n % 2]
            )

        def turn(n):
            load(n).wait()
            if n + 1 < len(jobs):
                load(n + 1).start()

            @pl.loop(0, slots // block)
            def _(k):
                here = pl.ds(pl.multiple_of(k * block, block), block)
                turned[:, here] = left[n % 2, here, :].astype(full).T.astype(low)

        def leave_wide(which, t):
            here = pl.ds(t * block, block)
            return [
                Move(wide_own.at[which], outs[2 * which].at[here], out_sem.at[2 * which]),
                Move(wide_far.at[which], outs[2 * which + 1].at[here], out_sem.at[2 * which + 1]),
            ]

        def leave_tall(t):
            far = t * block >= half
            here = pl.ds(t * block - (half if far else 0), block)
            return Move(
                tall_far if far else tall_own, outs[5 if far else 4].at[here], out_sem.at[5 if far else 4]
            )

        def wide(which, t):
            right = (gate, up)[which]
            if t == 0:
                heavy[which].wait()
            else:
                for copy in leave_wide(which, t - 1):
                    copy.wait()

            def own(cols):
                wide_own[which, :, cols] = dot(turned[...], right[:, cols])

            each_tile(half, 256, own)

            @pl.loop(0, half // 256)
            def _(k):
                cols = pl.ds(pl.multiple_of(k * 256, 256), 256)
                there = pl.ds(pl.multiple_of(half + k * 256, 256), 256)
                wide_far[which, :, cols] = dot(turned[...], right[:, there]).astype(low)

            for copy in leave_wide(which, t):
                copy.start()

        def tall(t):
            far = t * block >= half
            if t == 0:
                heavy[2].wait()
            if t * block not in (0, half):
                leave_tall(t - 1).wait()

            def tile(cols):
                value = dot(turned[...], grads[:, cols])
                if far:
                    tall_far[:, cols] = value.astype(low)
                else:
                    tall_own[:, cols] = value

            each_tile(width, 256, tile)
            leave_tall(t).start()

        def opening():
            load(0).start()
            for copy in heavy:
                copy.start()

        def closing():
            for which in range(2):
                for copy in leave_wide(which, width // block - 1):
                    copy.wait()
            leave_tall(half // block - 1).wait()
            leave_tall(hidden // block - 1).wait()

        listed = [opening]
        for n, (ref, t) in enumerate(jobs):
            listed.append(functools.partial(turn, n))
            if n < width // block:
                listed += [functools.partial(wide, which, t) for which in range(2)]
            else:
                listed.append(functools.partial(tall, t))
        return listed + [closing]

    return Beside(
        ins=(rows_in, grad_rows, grad_gate, grad_up, units),
        in_specs=(ANYWHERE,) * 5,
        outs=[
            jax.ShapeDtypeStruct((width, half), full),
            jax.ShapeDtypeStruct((width, half), low),
            jax.ShapeDtypeStruct((width, half), full),
            jax.ShapeDtypeStruct((width, half), low),
            jax.ShapeDtypeStruct((half, width), full),
            jax.ShapeDtypeStruct((half, width), low),
        ],
        scratch=[
            pltpu.VMEM((2, slots, block), low),
            pltpu.VMEM((block, slots), low),
            pltpu.VMEM((slots, hidden), low),
            pltpu.VMEM((slots, hidden), low),
            pltpu.VMEM((slots, width), low),
            pltpu.VMEM((2, block, half), full),
            pltpu.VMEM((2, block, half), low),
            pltpu.VMEM((block, width), full),
            pltpu.VMEM((block, width), low),
            pltpu.SemaphoreType.DMA((3,)),
            pltpu.SemaphoreType.DMA((2,)),
            pltpu.SemaphoreType.DMA((6,)),
        ],
        steps=steps,
        span=0.6,
    )


def turn_half(values):
    return pltpu.roll(values, values.shape[1] // 2, 1)


def attend_beside(tokens, weight_rows, gain_column, live_row, cosine, sine):
    row_count, width = tokens.shape
    low, full = jnp.bfloat16, jnp.float32
    block, group, strip = 256, 2, 32
    tiles, per_part = 3 * width // block, width // block
    score_scale = HEAD ** (-0.5)

    def steps(ins, outs, scratch, arrivals):
        tokens_ref, live, cos, sin = ins
        normed, proj, panel, queries, keys, values, mixed, probs, scale, panel_sem, out_sem, probs_sem = scratch[:12]
        small, gains, small_sem = scratch[12:]
        weight = arrivals[0]
        small_copy = Move(arrivals[1], small, small_sem)

        def load(t):
            return Move(weight.at[:, :, pl.ds(t * block, block)], panel.at[t % 3], panel_sem.at[t % 3])

        leaves = [
            Move(ref, outs[i], out_sem.at[i])
            for i, ref in enumerate((normed, proj.at[:, pl.ds(0, 2 * width)], queries, keys, values, mixed))
        ]

        def leave_probs(n):
            return Move(probs.at[n % 2], outs[6].at[pl.ds(n * group, group)], probs_sem.at[n % 2])

        def opening():
            small_copy.start()
            load(0).start()
            load(1).start()
            small_copy.wait()
            blocks = 128 // small.shape[1]
            for k in range(width // 128):
                columns = small[k * blocks : (k + 1) * blocks].astype(full).reshape(128, 128)
                gains[:, k * 128 : (k + 1) * 128] = columns.T[gain_column : gain_column + 8]

            @pl.loop(0, row_count // strip)
            def _(k):
                here = pl.ds(pl.multiple_of(k * strip, strip), strip)
                value = tokens_ref[here, :].astype(full)
                value = value * lax.rsqrt(jnp.mean(value * value, axis=1, keepdims=True) + NORM_EPS)
                normed[here, :] = (value * gains[0:1, :]).astype(low)

            leaves[0].start()

        def project(t):
            load(t).wait()
            if t + 2 < tiles:
                load(t + 2).start()
            proj[:, t * block : (t + 1) * block] = dot(normed[...], panel[t % 3].reshape(width, block))

        def measure(part):
            @pl.loop(0, row_count // strip)
            def _(k):
                here = pl.ds(pl.multiple_of(k * strip, strip), strip)
                value = proj[here, part * width : (part + 1) * width]
                inverse = lax.rsqrt(jnp.mean(value * value, axis=1, keepdims=True) + NORM_EPS)
                scale[part, here, :] = jnp.broadcast_to(inverse, (strip, HEAD))

        def attend(n):
            if n == 0:
                leaves[1].start()
            if n >= 2:
                leave_probs(n - 2).wait()
            query_slot = lax.broadcasted_iota(jnp.int32, (row_count, row_count), 0)
            key_slot = lax.broadcasted_iota(jnp.int32, (row_count, row_count), 1)
            allowed = (key_slot <= query_slot) & (live[...] > 0.5)

            @pl.loop(0, group)
            def _(i):
                head = n * group + i
                cols = pl.ds(pl.multiple_of(head * HEAD, HEAD), HEAD)

                def place(part, gain):
                    there = pl.ds(pl.multiple_of(part * width + head * HEAD, HEAD), HEAD)
                    value = proj[:, there] * scale[part] * gains[gain : gain + 1, cols]
                    return (value * cos[...] + turn_half(value) * sin[...]).astype(low)

                query, key = place(0, 1), place(1, 2)
                value = proj[:, pl.ds(pl.multiple_of(2 * width + head * HEAD, HEAD), HEAD)].astype(low)
                queries[:, cols], keys[:, cols], values[:, cols] = query, key, value
                score = jnp.where(allowed, dot_across(query, key) * score_scale, -1e30)
                expo = jnp.exp(score - jnp.max(score, axis=1, keepdims=True))
                prob = expo / jnp.sum(expo, axis=1, keepdims=True)
                probs[n % 2, i] = prob
                mixed[:, cols] = dot(prob.astype(low), value).astype(low)

            leave_probs(n).start()

        def closing():
            for move in leaves[2:]:
                move.start()
            for move in leaves:
                move.wait()
            for n in range(HEADS // group - 2, HEADS // group):
                leave_probs(n).wait()

        listed = [opening] + [functools.partial(project, t) for t in range(tiles)]
        listed += [functools.partial(measure, 0), functools.partial(measure, 1)]
        return listed + [functools.partial(attend, n) for n in range(HEADS // group)] + [closing]

    shape = (row_count, width)
    return Beside(
        ins=(tokens, live_row, cosine, sine),
        in_specs=(ON_CORE,) * 4,
        outs=[
            jax.ShapeDtypeStruct(shape, low),
            jax.ShapeDtypeStruct((row_count, 2 * width), full),
            jax.ShapeDtypeStruct(shape, low),
            jax.ShapeDtypeStruct(shape, low),
            jax.ShapeDtypeStruct(shape, low),
            jax.ShapeDtypeStruct(shape, low),
            jax.ShapeDtypeStruct((HEADS, row_count, row_count), full),
        ],
        scratch=[
            pltpu.VMEM(shape, low),
            pltpu.VMEM((row_count, 3 * width), full),
            pltpu.VMEM((3, width // weight_rows, weight_rows, block), low),
            pltpu.VMEM(shape, low),
            pltpu.VMEM(shape, low),
            pltpu.VMEM(shape, low),
            pltpu.VMEM(shape, low),
            pltpu.VMEM((2, group, row_count, row_count), full),
            pltpu.VMEM((2, row_count, HEAD), full),
            pltpu.SemaphoreType.DMA((3,)),
            pltpu.SemaphoreType.DMA((6,)),
            pltpu.SemaphoreType.DMA((2,)),
            pltpu.VMEM((width // weight_rows, weight_rows, 128), low),
            pltpu.VMEM((8, width), full),
            pltpu.SemaphoreType.DMA,
        ],
        steps=steps,
        span=0.6,
    )


def attend_back_beside(grad_attn, out_weight, queries, keys, values, probs, parts, gain_rows, cosine, sine):
    row_count, width = grad_attn.shape
    low, full = jnp.bfloat16, jnp.float32
    block, group, strip = 256, 2, 32
    score_scale = HEAD ** (-0.5)
    across_rows = (((0,), (0,)), ((), ()))

    def steps(ins, outs, scratch, arrivals):
        grad_ref, weight, query_ref, key_ref, value_ref, probs_in, parts_ref, gains, cos, sin = ins
        grad_mixed, grads, panel, prob_ref, projected, sums, panel_sem, probs_sem, out_sem = scratch
        tiles = width // block

        def load(t):
            return Move(weight.at[pl.ds(t * block, block)], panel.at[t % 3], panel_sem.at[t % 3])

        def load_probs(n):
            return Move(probs_in.at[pl.ds(n * group, group)], prob_ref.at[n % 2], probs_sem.at[n % 2])

        leaves = [Move(projected, outs[0], out_sem.at[0]), Move(sums, outs[1], out_sem.at[1])]

        def opening():
            load(0).start()
            load(1).start()
            load_probs(0).start()

        def unmix(t):
            load(t).wait()
            if t + 2 < tiles:
                load(t + 2).start()
            grad_mixed[:, t * block : (t + 1) * block] = dot_across(grad_ref[...], panel[t % 3]).astype(low)

        def attend(n):
            load_probs(n).wait()
            if n + 1 < HEADS // group:
                load_probs(n + 1).start()

            @pl.loop(0, group)
            def _(i):
                head = n * group + i
                cols = pl.ds(pl.multiple_of(head * HEAD, HEAD), HEAD)
                prob, grad = prob_ref[n % 2, i], grad_mixed[:, cols]
                grad_value = lax.dot_general(prob.astype(low), grad, across_rows, preferred_element_type=full)
                there = pl.ds(pl.multiple_of(2 * width + head * HEAD, HEAD), HEAD)
                projected[:, there] = grad_value.astype(low)
                grad_prob = dot_across(grad, value_ref[:, cols])
                centre = jnp.sum(prob * grad_prob, axis=1, keepdims=True)
                grad_score = (prob * (grad_prob - centre)).astype(low)
                grad_query = dot(grad_score, key_ref[:, cols]) * score_scale
                grad_key = lax.dot_general(grad_score, query_ref[:, cols], across_rows, preferred_element_type=full)
                for part, value in enumerate((grad_query, grad_key * score_scale)):
                    grads[part, :, cols] = value * cos[...] - turn_half(value) * sin[...]

        def settle(part):
            sums[part] = jnp.zeros((8, width), full)

            @pl.loop(0, row_count // strip)
            def _(k):
                here = pl.ds(pl.multiple_of(k * strip, strip), strip)
                value = parts_ref[here, part * width : (part + 1) * width]
                inverse = lax.rsqrt(jnp.mean(value * value, axis=1, keepdims=True) + NORM_EPS)
                unit = value * inverse
                grad = grads[part, here, :]
                product = grad * unit
                total = product[0:8]
                for first in range(8, strip, 8):
                    total = total + product[first : first + 8]
                sums[part] += total
                grad = grad * gains[part + 1 : part + 2, :]
                grad = inverse * (grad - unit * jnp.mean(grad * unit, axis=1, keepdims=True))
                projected[here, part * width : (part + 1) * width] = grad.astype(low)

        def closing():
            for move in leaves:
                move.start()
            for move in leaves:
                move.wait()

        listed = [opening] + [functools.partial(unmix, t) for t in range(tiles)]
        listed += [functools.partial(attend, n) for n in range(HEADS // group)]
        return listed + [functools.partial(settle, part) for part in range(2)] + [closing]

    shape = (row_count, width)
    return Beside(
        ins=(grad_attn, out_weight, queries, keys, values, probs, parts, gain_rows, cosine, sine),
        in_specs=(ON_CORE, ANYWHERE, ON_CORE, ON_CORE, ON_CORE, ANYWHERE, ON_CORE, ON_CORE, ON_CORE, ON_CORE),
        outs=[
            jax.ShapeDtypeStruct((row_count, 3 * width), low),
            jax.ShapeDtypeStruct((2, 8, width), full),
        ],
        scratch=[
            pltpu.VMEM(shape, low),
            pltpu.VMEM((2,) + shape, full),
            pltpu.VMEM((3, block, width), low),
            pltpu.VMEM((2, group, row_count, row_count), full),
            pltpu.VMEM((row_count, 3 * width), low),
            pltpu.VMEM((2, 8, width), full),
            pltpu.SemaphoreType.DMA((3,)),
            pltpu.SemaphoreType.DMA((2,)),
            pltpu.SemaphoreType.DMA((2,)),
        ],
        steps=steps,
    )


def alone(beside):
    def kernel(*refs):
        a, b = len(beside.ins), len(beside.ins) + len(beside.outs)
        for step in beside.steps(refs[:a], refs[a:b], refs[b:], ()):
            step()

    return pl.pallas_call(
        kernel,
        out_shape=beside.outs,
        in_specs=list(beside.in_specs),
        out_specs=[ANYWHERE] * len(beside.outs),
        scratch_shapes=list(beside.scratch),
        compiler_params=pltpu.CompilerParams(vmem_limit_bytes=48 << 20),
    )(*beside.ins)


DEEP = 4


def total_beside(pairs):
    low, full = jnp.bfloat16, jnp.float32
    jobs, shapes = [], []
    for n, (own, _) in enumerate(pairs):
        rows = own.shape[0] // 8
        shape = (rows, own.shape[1])
        if shape not in shapes:
            shapes.append(shape)
        jobs += [(n, k, shapes.index(shape)) for k in range(8)]

    def steps(ins, outs, scratch, arrivals):
        count = len(shapes)
        owns, fars, sums = scratch[:count], scratch[count : 2 * count], scratch[2 * count : 3 * count]
        in_sem, out_sem = scratch[3 * count :]

        def load(m):
            n, k, s = jobs[m]
            here = pl.ds(k * shapes[s][0], shapes[s][0])
            return [
                Move(ins[2 * n].at[here], owns[s].at[m % DEEP], in_sem.at[m % DEEP, 0]),
                Move(ins[2 * n + 1].at[here], fars[s].at[m % DEEP], in_sem.at[m % DEEP, 1]),
            ]

        def leave(m):
            n, k, s = jobs[m]
            here = pl.ds(k * shapes[s][0], shapes[s][0])
            return Move(sums[s].at[m % DEEP], outs[n].at[here], out_sem.at[m % DEEP])

        def opening():
            for m in range(DEEP - 1):
                for move in load(m):
                    move.start()

        def add(m):
            for move in load(m):
                move.wait()
            if m + DEEP - 1 < len(jobs):
                for move in load(m + DEEP - 1):
                    move.start()
            if m >= DEEP:
                leave(m - DEEP).wait()
            s = jobs[m][2]
            sums[s][m % DEEP] = owns[s][m % DEEP] + fars[s][m % DEEP].astype(full)
            leave(m).start()

        def closing():
            for m in range(len(jobs) - DEEP, len(jobs)):
                leave(m).wait()

        return [opening] + [functools.partial(add, m) for m in range(len(jobs))] + [closing]

    return Beside(
        ins=[x for pair in pairs for x in pair],
        in_specs=(ANYWHERE,) * (2 * len(pairs)),
        outs=[jax.ShapeDtypeStruct(own.shape, full) for own, _ in pairs],
        scratch=[pltpu.VMEM((DEEP,) + shape, full) for shape in shapes]
        + [pltpu.VMEM((DEEP,) + shape, low) for shape in shapes]
        + [pltpu.VMEM((DEEP,) + shape, full) for shape in shapes]
        + [pltpu.SemaphoreType.DMA((DEEP, 2)), pltpu.SemaphoreType.DMA((DEEP,))],
        steps=steps,
    )


def together(first, second):
    cuts = [(len(getattr(first, kind)), len(getattr(second, kind))) for kind in ("ins", "outs", "scratch")]

    def steps(ins, outs, scratch, arrivals):
        groups = [(refs[:a], refs[a:]) for refs, (a, _) in zip((ins, outs, scratch), cuts)]
        left = first.steps(*(group[0] for group in groups), arrivals)
        right = second.steps(*(group[1] for group in groups), arrivals)
        listed, done = [], 0
        for n, step in enumerate(left):
            listed.append(step)
            until = (n + 1) * len(right) // len(left)
            listed += right[done:until]
            done = until
        return listed

    return Beside(
        ins=list(first.ins) + list(second.ins),
        in_specs=list(first.in_specs) + list(second.in_specs),
        outs=list(first.outs) + list(second.outs),
        scratch=list(first.scratch) + list(second.scratch),
        steps=steps,
    )


WEIGHTS_LAG = 0.9
ROWS_LAG = 0.9


def gathered_body(
    dims,
    tokens,
    w_qkv,
    w_out,
    w_router,
    gains,
    w_gate,
    w_up,
    w_down,
    lengths,
    routes,
    send_counts,
    cotangent,
):
    row_count = tokens.shape[1]
    top_count = routes.shape[2]
    expert_count = w_router.shape[1]
    owners = math.prod(dims)
    weight_rows = w_qkv.shape[0]
    capacity = row_count * top_count // expert_count
    slots_all = row_count * 2 * owners
    balance_factor = float(expert_count) / (float(top_count) * float(slots_all) * float(slots_all))
    low = jnp.bfloat16
    full = jnp.float32
    chips = Grid(dims)
    devices = Grid(dims, cores=True)
    z, y, x = 0, 1, 2
    row_orders = [(x, z, y), (y, z, x), (z, x, y), (z, y, x)]
    row_shares = [5 * row_count // 16, 5 * row_count // 16, 3 * row_count // 16, 3 * row_count // 16]
    quarter = [weight_rows // 4] * 4
    wide_orders = [tuple(d + 1 for d in order) + (0,) for order in row_orders]
    late_shares = [row_count // 4, row_count // 4, row_count // 8, row_count // 8]
    narrow_orders = [order[:-1] for order in wide_orders]
    expert = lax.axis_index("expert")
    core = lax.axis_index("dp")
    swap = [(0, 1), (1, 0)]

    small = jnp.concatenate(
        [w_router, gains.T, jnp.zeros((weight_rows, 128 - expert_count - 4), low)], axis=1
    )
    gate_own, up_own, down_own = w_gate[0], w_up[0], w_down[0]
    gate_far, up_far, down_far = (lax.ppermute(w, "dp", swap) for w in (gate_own, up_own, down_own))

    positions = jnp.arange(row_count, dtype=jnp.int32)
    live_slots = positions < lengths[0]
    live_float = live_slots.astype(full)[:, None]
    expert_ids = jnp.arange(expert_count, dtype=jnp.int32)
    named = jnp.any(routes[0][:, :, None] == expert_ids, axis=1) & live_slots[:, None]
    before = (positions[None, :] < positions[:, None]).astype(low)
    rank = jnp.dot(before, named.astype(low), preferred_element_type=full)
    limit = jnp.minimum(send_counts[0], capacity).astype(full)
    kept = named & (rank < limit[None, :])
    kept_rank = jnp.where(kept, rank, -1.0)

    cosine, sine = (table[:, 0] for table in rope_tables(row_count, HEAD))
    sine = jnp.concatenate([-sine[:, : HEAD // 2], sine[:, HEAD // 2 :]], axis=1)
    early = row_count // 4
    first_parts = cut(0, quarter, wide_orders) + cut(1, [weight_rows], wide_orders[2:3])
    later_parts = cut(2, quarter, wide_orders) + cut(3, [early // 4] * 4, narrow_orders)
    qkv_all, small_all, out_all, cot_early, normed, qk_parts, queries, keys_low, values_low, mixed_low, probs = gather(
        [w_qkv, small, w_out, cotangent[0, :early]],
        devices,
        first_parts + later_parts,
        1,
        attend_beside(tokens[0], weight_rows, expert_count, live_slots[None, :].astype(full), cosine, sine),
        (0,) * len(first_parts) + (WEIGHTS_LAG,) * len(later_parts),
    )
    small_all = small_all.reshape(D, 128)
    router_weight = small_all[:, :expert_count]
    gain_float = small_all[:, expert_count : expert_count + 4].T.astype(full)
    qkv_weight = qkv_all.reshape(D, 3 * D)
    out_weight = out_all.reshape(D, D)
    inputs = tokens[0].astype(full)
    _, attn_norm_back = jax.vjp(norm_scale, inputs, gain_float[0])
    hidden_state = inputs + jnp.dot(mixed_low, out_weight, preferred_element_type=full)
    ffn_in, ffn_norm_back = jax.vjp(norm_scale, hidden_state, gain_float[3])
    ffn_low = ffn_in.astype(low)
    logits = jnp.dot(ffn_low, router_weight, preferred_element_type=full)
    router_probs = jax.nn.softmax(logits, axis=-1)
    prob_local = jnp.sum(router_probs * live_float, axis=0)
    sums = jnp.concatenate([send_counts[0].astype(full), prob_local])
    aside = jnp.concatenate(
        [
            jnp.where(kept, router_probs, 0.0).T,
            kept_rank.T,
            jnp.pad(sums[None, :], ((0, 7), (0, row_count - 2 * expert_count))),
        ],
        axis=0,
    )

    halves = (gate_own, gate_far, up_own, up_far, down_own, down_far)
    first_parts = cut(0, row_shares, row_orders) + cut(1, [aside.shape[0]], row_orders[2:3])
    later_parts = cut(2, late_shares, row_orders)
    _, aside_rows, cot_late, rows_in, gate_pre, up_pre, units, expert_out, mixture_part = gather(
        [ffn_low, aside, cotangent[0, early:]],
        chips,
        first_parts + later_parts,
        2,
        forward_beside((owners, row_count, D), (owners,) + aside.shape, halves, capacity),
        (0,) * len(first_parts) + (ROWS_LAG,) * len(later_parts),
    )
    sums_core = jnp.sum(aside_rows[:, 2 * expert_count, : 2 * expert_count], axis=0)
    sums_all = sums_core + lax.ppermute(sums_core, "dp", swap)
    count_total, prob_total = sums_all[:expert_count], sums_all[expert_count:]
    balance = jnp.sum(count_total * prob_total) * balance_factor
    weight_of = lax.dynamic_index_in_dim(aside_rows, expert, 1, keepdims=False)
    rank_of = lax.dynamic_index_in_dim(aside_rows, expert_count + expert, 1, keepdims=False)
    mixture, grad_rows, grad_gate, grad_up, back_part, dot_route = scatter(
        [mixture_part],
        chips,
        cut(0, row_shares, row_orders),
        5,
        backward_beside(
            cot_early, cot_late, rank_of, rank_of.T, weight_of, gate_pre, up_pre, expert_out, halves, capacity
        ),
    )
    route_part = jnp.where((expert_ids == expert)[None, :, None], dot_route[:, None, :], 0.0)
    grad_ffn, grad_route, *halves_grads = scatter(
        [back_part, route_part],
        chips,
        cut(0, row_shares, row_orders) + cut(1, [expert_count], row_orders[2:3]),
        4,
        outer_beside(rows_in, grad_rows, grad_gate, grad_up, units),
    )
    far_grads = [lax.ppermute(far, "dp", swap) for far in halves_grads[1::2]]
    result = (live_float * (hidden_state + mixture)).astype(low)[None]

    balance_coef = BALANCE_WEIGHT * balance_factor
    grad_probs = grad_route.T + balance_coef * count_total[None, :] * live_float
    grad_logits = router_probs * (
        grad_probs - jnp.sum(router_probs * grad_probs, axis=-1, keepdims=True)
    )
    grad_logits_low = grad_logits.astype(low)
    grad_ffn = grad_ffn + jnp.einsum("te,de->td", grad_logits_low, router_weight, preferred_element_type=full)
    grad_router_w = jnp.einsum("td,te->de", ffn_low, grad_logits_low, preferred_element_type=full)

    grad_layer = cotangent[0].astype(full) * live_float
    grad_hidden_part, grad_gain_ffn = ffn_norm_back(grad_ffn)
    grad_hidden_state = grad_layer + grad_hidden_part
    grad_attn_low = grad_hidden_state.astype(low)
    grad_projected, head_sums, *expert_grads = alone(
        together(
            attend_back_beside(
                grad_attn_low, out_weight, queries, keys_low, values_low, probs, qk_parts, gain_float, cosine, sine
            ),
            total_beside(list(zip(halves_grads[::2], far_grads))),
        )
    )
    grad_gain_query, grad_gain_key = jnp.sum(head_sums, axis=1)
    grad_normed = jnp.einsum("te,de->td", grad_projected, qkv_weight, preferred_element_type=full)
    grad_input_part, grad_gain_attn = attn_norm_back(grad_normed)
    grad_inputs = grad_hidden_state + grad_input_part
    grad_gain_rows = jnp.stack([grad_gain_attn, grad_gain_query, grad_gain_key, grad_gain_ffn])

    def outer(left, right):
        return jnp.einsum("sa,sb->ab", left, right, preferred_element_type=full)

    small_grads = jnp.concatenate(
        [grad_router_w, grad_gain_rows.T, jnp.zeros((D, 128 - expert_count - 4), full)], axis=1
    )
    shares = [
        g.reshape(devices.size, weight_rows, g.shape[1])
        for g in (outer(normed, grad_projected).astype(low), outer(mixed_low, grad_attn_low).astype(low), small_grads)
    ]
    grad_qkv, grad_out, grad_small = scatter(
        shares,
        devices,
        cut(0, quarter, wide_orders)
        + cut(1, quarter, wide_orders[:2] * 2)
        + cut(2, [weight_rows], wide_orders[2:3]),
        6,
    )
    return (
        result,
        grad_inputs[None],
        grad_qkv,
        grad_out,
        grad_small[:, :expert_count],
        grad_small[:, expert_count : expert_count + 4].T,
        *(g[None] for g in expert_grads),
        balance,
    )


def solution(mesh):
    dims = {4: (1, 2, 2), 8: (2, 2, 2), 16: (4, 2, 2)}.get(mesh.shape["expert"])
    plan = routed_body if dims is None or mesh.shape["dp"] != 2 else functools.partial(gathered_body, dims)
    placed = (
        P(("dp", "expert"), None, None),
        P(("dp", "expert"), None),
        P(("dp", "expert"), None),
        P(("dp", "expert"), None),
        P(None, ("dp", "expert")),
        P("expert", None, "dp"),
        P("expert", None, "dp"),
        P("expert", "dp", None),
        P(("dp", "expert")),
        P(("dp", "expert"), None, None),
        P(("dp", "expert"), None),
        P(("dp", "expert"), None, None),
    )
    return jax.shard_map(
        plan,
        mesh=mesh,
        in_specs=placed,
        out_specs=(
            P(("dp", "expert"), None, None),
            P(("dp", "expert"), None, None),
            P(("dp", "expert"), None),
            P(("dp", "expert"), None),
            P(("dp", "expert"), None),
            P(None, ("dp", "expert")),
            P("expert", None, "dp"),
            P("expert", None, "dp"),
            P("expert", "dp", None),
            P(),
        ),
        check_vma=False,
    )
```

```python
import functools
import itertools
import math

import jax
import jax.numpy as jnp
from jax import lax
from jax.experimental import pallas as pl
from jax.experimental.pallas import tpu as pltpu
from jax.sharding import PartitionSpec as P

D = 2048
HEADS = 16
HEAD = 128


NORM_EPS = 1e-05
BALANCE_WEIGHT = 0.01


def norm_scale(values, gain_row):
    return (
        values * lax.rsqrt(jnp.mean(values * values, axis=-1, keepdims=True) + NORM_EPS) * gain_row
    )


def rope_tables(positions_count, head_width):
    half_width = head_width // 2
    frequency = jnp.exp(
        jnp.arange(half_width, dtype=jnp.float32) * (-2.0 * math.log(10000.0) / head_width)
    )
    angles = jnp.arange(positions_count, dtype=jnp.float32)[:, None] * frequency[None, :]
    angles = jnp.concatenate([angles, angles], axis=1)
    return (jnp.cos(angles)[:, None, :], jnp.sin(angles)[:, None, :])


def rotate(values, cosine, sine_part):
    half_width = values.shape[-1] // 2
    turned = jnp.concatenate([-values[..., half_width:], values[..., :half_width]], axis=-1)
    return values * cosine + turned * sine_part


def query_key(query_part, key_part, query_gain, key_gain):
    positions_count = query_part.shape[0]
    cosine, sine_part = rope_tables(positions_count, HEAD)
    queries = norm_scale(query_part, query_gain).reshape(positions_count, HEADS, HEAD)
    key_heads = norm_scale(key_part, key_gain).reshape(positions_count, HEADS, HEAD)
    return (rotate(queries, cosine, sine_part), rotate(key_heads, cosine, sine_part))


def expert_forward(rows_in, gate_weight, up_weight, down_weight):
    gate_pre = jnp.einsum(
        "nkcd,kdf->nkcf", rows_in, gate_weight, preferred_element_type=jnp.float32
    )
    up_pre = jnp.einsum("nkcd,kdf->nkcf", rows_in, up_weight, preferred_element_type=jnp.float32)
    hidden_low = (jax.nn.silu(gate_pre) * up_pre).astype(jnp.bfloat16)
    output = jnp.einsum(
        "nkcf,kfd->nkcd", hidden_low, down_weight, preferred_element_type=jnp.float32
    )
    return (gate_pre, up_pre, hidden_low, output)


def routed_body(
    tokens,
    w_qkv,
    w_out,
    w_router,
    gains,
    w_gate,
    w_up,
    w_down,
    lengths,
    routes,
    send_counts,
    cotangent,
):
    row_count = tokens.shape[1]
    top_count = routes.shape[2]
    expert_count = w_router.shape[1]
    owners = lax.axis_size("expert")
    local_experts = expert_count // owners
    capacity = row_count * top_count // expert_count
    slots_all = row_count * lax.axis_size("dp") * owners
    balance_factor = float(expert_count) / (float(top_count) * float(slots_all) * float(slots_all))
    score_scale = HEAD ** (-0.5)
    inputs = tokens[0].astype(jnp.float32)
    positions = jnp.arange(row_count, dtype=jnp.int32)
    live_slots = positions < lengths[0]
    live_float = live_slots.astype(jnp.float32)[:, None]
    mixer_parts = (
        lax.all_gather(w_qkv, ("dp", "expert"), axis=0, tiled=True),
        lax.all_gather(w_out, ("dp", "expert"), axis=0, tiled=True),
        lax.all_gather(w_router, ("dp", "expert"), axis=0, tiled=True),
        lax.all_gather(gains, ("dp", "expert"), axis=1, tiled=True),
    )
    qkv_weight, out_weight, router_weight, gain_rows = mixer_parts
    gain_float = gain_rows.astype(jnp.float32)
    attn_in, attn_norm_back = jax.vjp(norm_scale, inputs, gain_float[0])
    normed = attn_in.astype(jnp.bfloat16)
    projected = jnp.dot(normed, qkv_weight, preferred_element_type=jnp.float32)
    (rot_query, rot_keys), query_key_back = jax.vjp(
        query_key, projected[:, :D], projected[:, D : 2 * D], gain_float[1], gain_float[2]
    )
    queries = rot_query.astype(jnp.bfloat16)
    keys_low = rot_keys.astype(jnp.bfloat16)
    values_low = projected[:, 2 * D :].astype(jnp.bfloat16).reshape(row_count, HEADS, HEAD)
    allowed = (positions[None, :] <= positions[:, None]) & live_slots[None, :]
    scores = (
        jnp.einsum("qhd,khd->hqk", queries, keys_low, preferred_element_type=jnp.float32)
        * score_scale
    )
    scores = jnp.where(allowed[None], scores, -1e30)
    highest = jnp.max(scores, axis=-1, keepdims=True)
    expo_scores = jnp.exp(scores - highest)
    totals = jnp.sum(expo_scores, axis=-1, keepdims=True)
    attn_probs = expo_scores / totals
    log_total = highest + jnp.log(totals)
    mixed_heads = jnp.einsum(
        "hqk,khd->qhd",
        attn_probs.astype(jnp.bfloat16),
        values_low,
        preferred_element_type=jnp.float32,
    )
    mixed_low = mixed_heads.reshape(row_count, D).astype(jnp.bfloat16)
    hidden_state = inputs + jnp.dot(mixed_low, out_weight, preferred_element_type=jnp.float32)
    ffn_in, ffn_norm_back = jax.vjp(norm_scale, hidden_state, gain_float[3])
    ffn_low = ffn_in.astype(jnp.bfloat16)
    logits = jnp.dot(ffn_low, router_weight, preferred_element_type=jnp.float32)
    router_probs = jax.nn.softmax(logits, axis=-1)
    count_float = send_counts[0].astype(jnp.float32)
    prob_local = jnp.sum(router_probs * live_float, axis=0)
    count_total, prob_total = lax.psum((count_float, prob_local), ("dp", "expert"))
    balance = jnp.sum(count_total * prob_total) * balance_factor
    route_rows = routes[0]
    expert_ids = jnp.arange(expert_count, dtype=jnp.int32)
    route_hot = (route_rows[:, :, None] == expert_ids) & live_slots[:, None, None]
    route_int = route_hot.astype(jnp.int32)
    per_token = jnp.sum(route_int, axis=1)
    earlier = jnp.cumsum(per_token, axis=0) - per_token
    route_rank = jnp.sum(earlier[:, None, :] * route_int, axis=-1)
    limits = jnp.sum(jnp.minimum(send_counts[0], capacity)[None, None, :] * route_int, axis=-1)
    kept_route = route_rank < limits
    target_expert = jnp.where(kept_route, route_rows, expert_count)
    target_slot = jnp.where(kept_route, route_rank, 0)
    token_ids = jnp.broadcast_to(positions[:, None], route_rows.shape)
    source = (
        jnp.full((expert_count, capacity), row_count, jnp.int32)
        .at[target_expert, target_slot]
        .set(token_ids, mode="drop")
    )
    padded_in = jnp.concatenate([ffn_low, jnp.zeros((1, D), jnp.bfloat16)], axis=0)
    send_rows = padded_in[source].reshape(owners, local_experts, capacity, D)
    expert_weights = (w_gate, w_up, w_down)
    gathered = lax.all_gather(
        lax.all_to_all(send_rows, "expert", split_axis=0, concat_axis=0, tiled=True),
        "dp",
        axis=0,
        tiled=True,
    )
    gate_pre, up_pre, hidden_low, partial_out = expert_forward(gathered, w_gate, w_up, w_down)
    summed = lax.psum_scatter(
        partial_out.astype(jnp.bfloat16), "dp", scatter_dimension=0, tiled=True
    )
    expert_out, expert_rows, gate_pre, up_pre, hidden_low = (
        summed,
        gathered,
        gate_pre,
        up_pre,
        hidden_low,
    )
    returned = lax.all_to_all(
        expert_out, "expert", split_axis=0, concat_axis=0, tiled=True
    ).reshape(expert_count * capacity, D)
    flat_index = jnp.where(kept_route, route_rows * capacity + route_rank, 0)
    picked = returned[flat_index]
    route_prob = jnp.sum(router_probs[:, None, :] * route_hot.astype(jnp.float32), axis=-1)
    combine_weight = jnp.where(kept_route, route_prob, 0.0)
    mixture = jnp.sum(combine_weight[:, :, None] * picked, axis=1)
    layer = live_float * (hidden_state + mixture)
    result = layer.astype(jnp.bfloat16)[None]
    qkv_back, out_back, router_back = (
        lax.all_gather(w_qkv, ("dp", "expert"), axis=0, tiled=True),
        lax.all_gather(w_out, ("dp", "expert"), axis=0, tiled=True),
        lax.all_gather(w_router, ("dp", "expert"), axis=0, tiled=True),
    )
    grad_layer = cotangent[0].astype(jnp.float32) * live_float
    dot_route = jnp.sum(grad_layer[:, None, :] * picked, axis=-1)
    balance_coef = BALANCE_WEIGHT * balance_factor
    grad_probs = jnp.sum(
        jnp.where(kept_route, dot_route, 0.0)[:, :, None] * route_hot.astype(jnp.float32), axis=1
    )
    grad_probs = grad_probs + balance_coef * count_total[None, :] * live_float
    grad_logits = router_probs * (
        grad_probs - jnp.sum(router_probs * grad_probs, axis=-1, keepdims=True)
    )
    grad_logits_low = grad_logits.astype(jnp.bfloat16)
    route_scale = (
        jnp.zeros((expert_count, capacity), jnp.float32)
        .at[target_expert, target_slot]
        .set(combine_weight, mode="drop")
    )
    padded_grad = jnp.concatenate([grad_layer, jnp.zeros((1, D), jnp.float32)], axis=0)
    grad_send = (
        (padded_grad[source] * route_scale[:, :, None])
        .astype(jnp.bfloat16)
        .reshape(owners, local_experts, capacity, D)
    )
    arrived = lax.all_to_all(grad_send, "expert", split_axis=0, concat_axis=0, tiled=True)
    grad_rows_all = lax.all_gather(arrived, "dp", axis=0, tiled=True)
    gate_weight, up_weight, down_weight = expert_weights
    grad_down_w = jnp.einsum(
        "nkcf,nkcd->kfd", hidden_low, grad_rows_all, preferred_element_type=jnp.float32
    )
    grad_units = jnp.einsum(
        "nkcd,kfd->nkcf", grad_rows_all, down_weight, preferred_element_type=jnp.float32
    )
    gate_sigmoid = jax.nn.sigmoid(gate_pre)
    grad_gate_low = (
        grad_units * up_pre * gate_sigmoid * (1.0 + gate_pre * (1.0 - gate_sigmoid))
    ).astype(jnp.bfloat16)
    grad_up_low = (grad_units * gate_pre * gate_sigmoid).astype(jnp.bfloat16)
    grad_gate_w = jnp.einsum(
        "nkcd,nkcf->kdf", expert_rows, grad_gate_low, preferred_element_type=jnp.float32
    )
    grad_up_w = jnp.einsum(
        "nkcd,nkcf->kdf", expert_rows, grad_up_low, preferred_element_type=jnp.float32
    )
    back_part = jnp.einsum(
        "nkcf,kdf->nkcd", grad_gate_low, gate_weight, preferred_element_type=jnp.float32
    )
    back_part = back_part + jnp.einsum(
        "nkcf,kdf->nkcd", grad_up_low, up_weight, preferred_element_type=jnp.float32
    )
    back_rows = lax.psum_scatter(
        back_part.astype(jnp.bfloat16), "dp", scatter_dimension=0, tiled=True
    )
    expert_grads = (grad_gate_w, grad_up_w, grad_down_w)
    sent_back = lax.all_to_all(
        back_rows, "expert", split_axis=0, concat_axis=0, tiled=True
    ).reshape(expert_count * capacity, D)
    grad_ffn = jnp.einsum(
        "tj,tjd->td",
        kept_route.astype(jnp.bfloat16),
        sent_back[flat_index],
        preferred_element_type=jnp.float32,
    )
    grad_ffn = grad_ffn + jnp.einsum(
        "te,de->td", grad_logits_low, router_back, preferred_element_type=jnp.float32
    )
    grad_router_w = jnp.einsum(
        "td,te->de", ffn_low, grad_logits_low, preferred_element_type=jnp.float32
    )
    grad_hidden_part, grad_gain_ffn = ffn_norm_back(grad_ffn)
    grad_hidden_state = grad_layer + grad_hidden_part
    grad_attn_low = grad_hidden_state.astype(jnp.bfloat16)
    grad_out_w = jnp.einsum(
        "td,te->de", mixed_low, grad_attn_low, preferred_element_type=jnp.float32
    )
    grad_mixed = jnp.einsum(
        "te,de->td", grad_attn_low, out_back, preferred_element_type=jnp.float32
    )
    grad_mixed = grad_mixed.astype(jnp.bfloat16).reshape(row_count, HEADS, HEAD)
    scores_again = (
        jnp.einsum("qhd,khd->hqk", queries, keys_low, preferred_element_type=jnp.float32)
        * score_scale
    )
    probs_again = jnp.where(allowed[None], jnp.exp(scores_again - log_total), 0.0)
    grad_values = jnp.einsum(
        "hqk,qhd->khd",
        probs_again.astype(jnp.bfloat16),
        grad_mixed,
        preferred_element_type=jnp.float32,
    )
    grad_attn_probs = jnp.einsum(
        "qhd,khd->hqk", grad_mixed, values_low, preferred_element_type=jnp.float32
    )
    grad_scores = probs_again * (
        grad_attn_probs - jnp.sum(probs_again * grad_attn_probs, axis=-1, keepdims=True)
    )
    grad_scores_low = grad_scores.astype(jnp.bfloat16)
    grad_queries = (
        jnp.einsum("hqk,khd->qhd", grad_scores_low, keys_low, preferred_element_type=jnp.float32)
        * score_scale
    )
    grad_keys = (
        jnp.einsum("hqk,qhd->khd", grad_scores_low, queries, preferred_element_type=jnp.float32)
        * score_scale
    )
    grad_query_part, grad_key_part, grad_gain_query, grad_gain_key = query_key_back(
        (grad_queries, grad_keys)
    )
    grad_projected = jnp.concatenate(
        [grad_query_part, grad_key_part, grad_values.reshape(row_count, D)], axis=1
    ).astype(jnp.bfloat16)
    grad_qkv_w = jnp.einsum("td,te->de", normed, grad_projected, preferred_element_type=jnp.float32)
    grad_normed = jnp.einsum(
        "te,de->td", grad_projected, qkv_back, preferred_element_type=jnp.float32
    )
    grad_input_part, grad_gain_attn = attn_norm_back(grad_normed)
    grad_inputs = grad_hidden_state + grad_input_part
    grad_gain_rows = jnp.stack([grad_gain_attn, grad_gain_query, grad_gain_key, grad_gain_ffn])
    mixer_grads = (
        lax.psum_scatter(grad_qkv_w, ("dp", "expert"), scatter_dimension=0, tiled=True),
        lax.psum_scatter(grad_out_w, ("dp", "expert"), scatter_dimension=0, tiled=True),
        lax.psum_scatter(grad_router_w, ("dp", "expert"), scatter_dimension=0, tiled=True),
        lax.psum_scatter(grad_gain_rows, ("dp", "expert"), scatter_dimension=1, tiled=True),
    )
    return (
        result,
        grad_inputs[None],
        mixer_grads[0],
        mixer_grads[1],
        mixer_grads[2],
        mixer_grads[3],
        expert_grads[0],
        expert_grads[1],
        expert_grads[2],
        balance,
    )


MESH = pl.DeviceIdType.MESH


class Grid:
    def __init__(self, dims, cores=False):
        self.cores = cores
        self.dims = ((2,) if cores else ()) + tuple(dims)
        self.size = math.prod(self.dims)
        self.strides = [math.prod(self.dims[d + 1 :]) for d in range(len(self.dims))]
        self.lanes = {}
        for d in range(len(self.dims)):
            for side in self.sides(d):
                self.lanes[(d, side)] = len(self.lanes)

    def coords(self):
        expert = lax.axis_index("expert")
        c = [lax.axis_index("dp")] if self.cores else []
        first = len(c)
        for d in range(first, len(self.dims)):
            c.append(lax.rem(expert // self.strides[d], self.dims[d]))
        return c

    def rels(self, d):
        n = self.dims[d]
        if n == 1:
            return []
        if n == 2:
            return [(1, 0)]
        return [(k, side) for k in range(1, n) for side in (-1, 1)]

    def sides(self, d):
        n = self.dims[d]
        return [] if n == 1 else [0] if n == 2 else [-1, 1]

    def at(self, c, d, rel):
        k, side = rel
        return 1 - c[d] if side == 0 else c[d] + side * k

    def valid(self, c, d, rel):
        k, side = rel
        if side == 0:
            return None
        return c[d] - k >= 0 if side < 0 else c[d] + k < self.dims[d]

    def index(self, coords):
        return sum(x * s for x, s in zip(coords, self.strides))

    def neighbor(self, c, d, side):
        other = list(c)
        other[d] = self.at(c, d, (1, side))
        ok = self.valid(c, d, (1, side))
        if self.cores and d == 0:
            return {"dp": other[0]}, ok
        first = 1 if self.cores else 0
        expert = sum(x * s for x, s in zip(other[first:], self.strides[first:]))
        return {"expert": expert}, ok

    def events(self, order):
        return [
            dict(zip(order, combo))
            for combo in itertools.product(*[[None] + self.rels(d) for d in order])
        ]

    def place(self, c, order, event):
        pred, o, last = None, list(c), -1
        for i, d in enumerate(order):
            if event[d]:
                pred = both(pred, self.valid(c, d, event[d]))
                o[d] = self.at(c, d, event[d])
                last = i
        return o, pred, last


def both(a, b):
    if a is None:
        return b
    if b is None:
        return a
    return jnp.logical_and(a, b)


def when(pred, f):
    if pred is None:
        f()
    else:
        pl.when(pred)(f)


def greet(grid, c):
    barrier = pltpu.get_barrier_semaphore()
    total = jnp.int32(0)
    for d, side in grid.lanes:
        device, ok = grid.neighbor(c, d, side)
        when(
            ok,
            lambda device=device: pl.semaphore_signal(
                barrier, inc=1, device_id=device, device_id_type=MESH
            ),
        )
        total = total + (1 if ok is None else ok.astype(jnp.int32))
    pl.semaphore_wait(barrier, total)


def farthest(order, event):
    return tuple(event[d][0] if event[d] else 0 for d in reversed(order))


class Beside:
    def __init__(self, ins=(), in_specs=(), outs=(), scratch=(), steps=None, lead=0.0, span=1.0):
        self.lead, self.span = lead, span
        self.ins, self.in_specs, self.outs, self.scratch = ins, in_specs, outs, scratch
        self.steps = steps

    def share(self, refs, count, own_scratch):
        cuts = [count, len(self.ins), count, len(self.outs), own_scratch, len(self.scratch)]
        groups, at = [], 0
        for n in cuts:
            groups.append(refs[at : at + n])
            at += n
        steps = self.steps(groups[1], groups[3], groups[5], groups[2]) if self.steps else []
        return groups[0], groups[2], groups[4], steps


def mingle(events, gate, steps, free, lead, span):
    for event in events[:free]:
        event()
    gate()
    first = round(lead * len(steps))
    for step in steps[:first]:
        step()
    rest, left = events[free:], steps[first:]
    done = 0
    for n, event in enumerate(rest):
        event()
        while done < len(left) and done * len(rest) * span < (n + 1) * len(left):
            left[done]()
            done += 1
    for step in left[done:]:
        step()


def gather_kernel(grid, parts, lags, count, beside, *refs):
    srcs, outs, (send_sem, recv_sem, own_sem), steps = beside.share(refs, count, 3)
    c = grid.coords()
    me = grid.index(c)
    own = [pltpu.make_async_copy(s, o.at[me], own_sem.at[i]) for i, (s, o) in enumerate(zip(srcs, outs))]
    for copy in own:
        copy.start()
    greet(grid, c)
    sent = []

    def piece(p, ref):
        _, row0, rows, _ = parts[p]
        return ref.at[pl.ds(row0, rows)]

    def push(p, origin, source, d, side, pred):
        device, ok = grid.neighbor(c, d, side)
        pred = both(pred, ok)
        copy = pltpu.make_async_remote_copy(
            src_ref=source,
            dst_ref=piece(p, outs[parts[p][0]].at[origin]),
            send_sem=send_sem.at[p, origin, grid.lanes[(d, side)]],
            recv_sem=recv_sem.at[p, origin],
            device_id=device,
            device_id_type=MESH,
        )
        when(pred, copy.start)
        sent.append((pred, copy))

    todo = []
    for lag in sorted(set(lags)):
        group = []
        for p, (_, _, _, order) in enumerate(parts):
            if lags[p] == lag:
                group += [(farthest(order, event), p, event) for event in grid.events(order)]
        group.sort(key=lambda t: t[:2])
        todo += [(lag + n / len(group), p, event) for n, (_, p, event) in enumerate(group)]
    todo.sort(key=lambda t: t[0])
    free = 1 + max(n for n, (_, p, _) in enumerate(todo) if lags[p] == 0)
    if len(set(lags)) == 1:
        free = len(parts)

    def gate():
        for copy in own:
            copy.wait()

    def handle(p, event):
        a, _, _, order = parts[p]
        o, pred, last = grid.place(c, order, event)
        origin = grid.index(o)
        if last < 0:
            source = piece(p, srcs[a])
        else:
            source = piece(p, outs[a].at[origin])
            arrival = pltpu.make_async_remote_copy(
                src_ref=source,
                dst_ref=source,
                send_sem=send_sem.at[p, origin, 0],
                recv_sem=recv_sem.at[p, origin],
                device_id={"expert": lax.axis_index("expert")},
                device_id_type=MESH,
            )
            when(pred, arrival.wait_recv)
            side = event[order[last]][1]
            if side:
                push(p, origin, source, order[last], -side, pred)
        for d in order[last + 1 :]:
            for side in grid.sides(d):
                push(p, origin, source, d, side, pred)

    events = [functools.partial(handle, p, event) for _, p, event in todo]
    mingle(events, gate, steps, free, beside.lead, beside.span)
    for pred, copy in sent:
        when(pred, copy.wait_send)


def gather(arrays, grid, parts, cid, beside=Beside(), lags=None):
    lags = lags or (0,) * len(parts)
    n, count = grid.size, len(arrays)
    return pl.pallas_call(
        functools.partial(gather_kernel, grid, parts, lags, count, beside),
        out_shape=[jax.ShapeDtypeStruct((n,) + x.shape, x.dtype) for x in arrays] + list(beside.outs),
        in_specs=[pl.BlockSpec(memory_space=pl.ANY)] * count + list(beside.in_specs),
        out_specs=[pl.BlockSpec(memory_space=pl.ANY)] * (count + len(beside.outs)),
        scratch_shapes=[
            pltpu.SemaphoreType.DMA((len(parts), n, len(grid.lanes))),
            pltpu.SemaphoreType.DMA((len(parts), n)),
            pltpu.SemaphoreType.DMA((count,)),
        ]
        + list(beside.scratch),
        compiler_params=pltpu.CompilerParams(
            collective_id=cid, has_side_effects=True, vmem_limit_bytes=60 << 20
        ),
    )(*arrays, *beside.ins)


def landing_slots(grid, order):
    base, total, earlier = {}, 0, 1
    for d in order:
        base[d] = total
        total += len(grid.rels(d)) * earlier
        earlier *= grid.dims[d]
    return base, total


def scatter_kernel(grid, parts, count, beside, *refs):
    k = len(parts)
    srcs, outs, scratch, steps = beside.share(refs, count, 2 * k + count + 4)
    held, mine, totals = scratch[:k], scratch[k : 2 * k], scratch[2 * k : 2 * k + count]
    send_sem, recv_sem, mine_sem, out_sem = scratch[2 * k + count :]
    c = grid.coords()

    def piece(p, ref):
        _, row0, rows, _ = parts[p]
        return ref.at[pl.ds(row0, rows)]

    def own_slot(order, o):
        slot = 0
        for d in order[:-1]:
            slot = slot * grid.dims[d] + o[d]
        return slot

    def landing(order, d, rel, o):
        base, _ = landing_slots(grid, order)
        slot = grid.rels(d).index(rel)
        for q in order[: order.index(d)]:
            slot = slot * grid.dims[q] + o[q]
        return base[d] + slot

    def own_copy(p, o):
        a, _, _, order = parts[p]
        slot = own_slot(order, o)
        return pltpu.make_async_copy(
            piece(p, srcs[a].at[grid.index(o)]), mine[p].at[slot], mine_sem.at[p, slot]
        )

    for p, (_, _, _, order) in enumerate(parts):
        for position in itertools.product(*[range(grid.dims[d]) for d in order[:-1]]):
            o = list(c)
            for d, v in zip(order[:-1], position):
                o[d] = v
            own_copy(p, o).start()
    greet(grid, c)
    todo = []
    for p, (_, _, _, order) in enumerate(parts):
        for event in grid.events(order):
            todo.append((tuple(-far for far in farthest(order, event)), p, event))
    todo.sort(key=lambda t: t[:2])
    sent = []

    def handle(p, event):
        a, row0, rows, order = parts[p]
        o, pred, last = grid.place(c, order, event)
        always, sometimes = [], []
        if last >= 0:
            far, side = event[order[last]]
            if side and far + 1 < grid.dims[order[last]]:
                _, ok = grid.neighbor(c, order[last], -side)
                sometimes.append((landing(order, order[last], (far + 1, side), o), ok))
        for d in order[last + 1 :]:
            for side in grid.sides(d):
                _, ok = grid.neighbor(c, d, side)
                slot = landing(order, d, (1, -side), o)
                if ok is None:
                    always.append(slot)
                else:
                    sometimes.append((slot, ok))
        final = last < 0
        if not always and not sometimes and not final:
            source = piece(p, srcs[a].at[grid.index(o)])
        else:
            source = mine[p].at[own_slot(order, o)]
            when(pred, own_copy(p, o).wait)
            steps = [(slot, ok) for slot, ok in sometimes]
            if always or final:
                steps.insert(0, (always, None))

            def add(slots, opening, final=final, source=source, p=p, row0=row0, rows=rows, a=a):
                for slot in slots:
                    landed = held[p].at[slot]
                    pltpu.make_async_remote_copy(
                        src_ref=landed,
                        dst_ref=landed,
                        send_sem=send_sem.at[p, 0],
                        recv_sem=recv_sem.at[p, slot],
                        device_id={"expert": lax.axis_index("expert")},
                        device_id_type=MESH,
                    ).wait_recv()
                tile = min(16, rows)

                @pl.loop(0, rows // tile)
                def _(t):
                    here = pl.ds(pl.multiple_of(t * tile, tile), tile)
                    there = pl.ds(pl.multiple_of(row0 + t * tile, tile), tile)
                    if final and not opening:
                        value = totals[a][there, :]
                    else:
                        value = source[here, :].astype(jnp.float32)
                    for slot in slots:
                        value = value + held[p][slot, here, :].astype(jnp.float32)
                    if final:
                        totals[a][there, :] = value
                    else:
                        source[here, :] = value.astype(source.dtype)

            for n, (slots, ok) in enumerate(steps):
                slots = slots if isinstance(slots, list) else [slots]
                when(both(pred, ok), functools.partial(add, slots, n == 0))
        if last >= 0:
            d = order[last]
            device, _ = grid.neighbor(c, d, event[d][1])
            slot = landing(order, d, event[d], o)
            copy = pltpu.make_async_remote_copy(
                src_ref=source,
                dst_ref=held[p].at[slot],
                send_sem=send_sem.at[p, slot],
                recv_sem=recv_sem.at[p, slot],
                device_id=device,
                device_id_type=MESH,
            )
            when(pred, copy.start)
            sent.append((pred, copy))

    mingle(
        [functools.partial(handle, p, event) for _, p, event in todo],
        lambda: None,
        steps,
        sum(event[parts[p][3][-1]] is not None for _, p, event in todo),
        beside.lead,
        beside.span,
    )
    done = [pltpu.make_async_copy(t, o, out_sem.at[i]) for i, (t, o) in enumerate(zip(totals, outs))]
    for copy in done:
        copy.start()
    for pred, copy in sent:
        when(pred, copy.wait_send)
    for copy in done:
        copy.wait()


def scatter(arrays, grid, parts, cid, beside=Beside()):
    count = len(arrays)
    slots = [landing_slots(grid, order)[1] for _, _, _, order in parts]
    mine = [grid.size // grid.dims[order[-1]] for _, _, _, order in parts]
    blocks = [((rows, arrays[a].shape[2]), arrays[a].dtype) for a, _, rows, _ in parts]
    flat = [jax.ShapeDtypeStruct(x.shape[1:], jnp.float32) for x in arrays]
    return pl.pallas_call(
        functools.partial(scatter_kernel, grid, parts, count, beside),
        out_shape=flat + list(beside.outs),
        in_specs=[pl.BlockSpec(memory_space=pl.ANY)] * count + list(beside.in_specs),
        out_specs=[pl.BlockSpec(memory_space=pl.ANY)] * (count + len(beside.outs)),
        scratch_shapes=[pltpu.VMEM((s,) + b, t) for s, (b, t) in zip(slots, blocks)]
        + [pltpu.VMEM((s,) + b, t) for s, (b, t) in zip(mine, blocks)]
        + [pltpu.VMEM(x.shape, x.dtype) for x in flat]
        + [
            pltpu.SemaphoreType.DMA((len(parts), max(slots))),
            pltpu.SemaphoreType.DMA((len(parts), max(slots))),
            pltpu.SemaphoreType.DMA((len(parts), max(mine))),
            pltpu.SemaphoreType.DMA((count,)),
        ]
        + list(beside.scratch),
        compiler_params=pltpu.CompilerParams(
            collective_id=cid, has_side_effects=True, vmem_limit_bytes=60 << 20
        ),
    )(*arrays, *beside.ins)


def cut(array, shares, orders):
    starts = [sum(shares[:i]) for i in range(len(shares))]
    return tuple((array, start, share, order) for start, share, order in zip(starts, shares, orders))


def each_tile(total, width, f):
    @pl.loop(0, total // width, unroll=4)
    def _(t):
        f(pl.ds(pl.multiple_of(t * width, width), width))


def dot(left, right):
    return jnp.dot(left, right, preferred_element_type=jnp.float32)


def dot_across(left, right):
    return lax.dot_general(left, right, (((1,), (1,)), ((), ())), preferred_element_type=jnp.float32)


class Move:
    def __init__(self, *refs):
        self.refs = refs

    def start(self):
        pltpu.make_async_copy(*self.refs).start()

    def wait(self):
        pltpu.make_async_copy(*self.refs).wait()


ANYWHERE = pl.BlockSpec(memory_space=pl.ANY)
ON_CORE = pl.BlockSpec(memory_space=pltpu.VMEM)


def weight_copies(halves, held, sem):
    gate_own, gate_far, up_own, up_far, down_own, down_far = halves
    gate, up, down = held
    half = gate.shape[1] // 2
    own, far = pl.ds(0, half), pl.ds(half, half)
    pairs = [
        (gate_own, gate.at[:, own]),
        (gate_far, gate.at[:, far]),
        (up_own, up.at[:, own]),
        (up_far, up.at[:, far]),
        (down_own, down.at[own, :]),
        (down_far, down.at[far, :]),
    ]
    return [Move(a, b, sem.at[i]) for i, (a, b) in enumerate(pairs)]


def pick_of(ranks, row, capacity):
    line = ranks[row : row + 1, :]
    slot = lax.broadcasted_iota(jnp.int32, (capacity, line.shape[1]), 0).astype(jnp.float32)
    return line == slot


def put_of(ranks, row, capacity):
    line = ranks[:, row : row + 1]
    slot = lax.broadcasted_iota(jnp.int32, (line.shape[0], capacity), 1).astype(jnp.float32)
    return (line == slot).astype(jnp.float32).astype(jnp.bfloat16)


def forward_beside(shape, aside_shape, halves, capacity):
    row_count, tokens, width = shape
    expert_count = (aside_shape[1] - 8) // 2
    hidden = 2 * halves[0].shape[1]
    pairs, pair = row_count // 2, 2 * capacity
    slots = row_count * capacity
    low, full = jnp.bfloat16, jnp.float32

    def steps(ins, outs, scratch, arrivals):
        ffn_in = arrivals[0]
        weights, (ffn, xs, pre, units, out, mix), sems = scratch[:3], scratch[3:9], scratch[9:12]
        notes, ranks, ranks_t, weights_t, notes_sem = scratch[12:]
        load_sem, row_sem, out_sem = sems
        heavy = weight_copies(ins, weights, load_sem)
        notes_copy = Move(arrivals[1], notes, notes_sem)
        gate_w, up_w, down_w = weights

        def load(q):
            return Move(ffn_in.at[pl.ds(2 * q, 2)], ffn.at[q % 2], row_sem.at[q % 2])

        def leave(q):
            here = pl.ds(q * pair, pair)
            moves = [
                (xs, outs[0].at[here]),
                (pre.at[0], outs[1].at[here]),
                (pre.at[1], outs[2].at[here]),
                (units, outs[3].at[here]),
                (out, outs[4].at[here]),
                (mix, outs[5].at[pl.ds(2 * q, 2)]),
            ]
            return [Move(a, b, out_sem.at[i]) for i, (a, b) in enumerate(moves)]

        def opening():
            notes_copy.start()
            load(0).start()
            for copy in heavy:
                copy.start()
            notes_copy.wait()
            expert = lax.axis_index("expert")
            for first, kept in ((expert_count, ranks_t), (0, weights_t)):
                for row in range(row_count):
                    ranks[row : row + 1, :] = notes[row, pl.ds(first + expert, 1), :]
                kept[...] = ranks[...].T
            for row in range(row_count):
                ranks[row : row + 1, :] = notes[row, pl.ds(expert_count + expert, 1), :]

        def choose(q):
            load(q).wait()
            if q + 1 < pairs:
                load(q + 1).start()
            if q:
                leave(q - 1)[0].wait()
            for i in range(2):
                pick = pick_of(ranks, 2 * q + i, capacity).astype(full).astype(low)
                rows = pl.ds(i * capacity, capacity)

                def tile(cols, i=i, pick=pick, rows=rows):
                    xs[rows, cols] = dot(pick, ffn[q % 2, i, :, cols]).astype(low)

                each_tile(width, 512, tile)
            leave(q)[0].start()

        def widen(q):
            if q == 0:
                for copy in heavy[:4]:
                    copy.wait()
            else:
                for copy in leave(q - 1)[1:4]:
                    copy.wait()

            def tile(cols):
                gate = dot(xs[...], gate_w[:, cols])
                up = dot(xs[...], up_w[:, cols])
                pre[0, :, cols] = gate
                pre[1, :, cols] = up
                units[:, cols] = (gate * jax.nn.sigmoid(gate) * up).astype(low)

            each_tile(hidden, 256, tile)
            for copy in leave(q)[1:4]:
                copy.start()

        def narrow(q):
            if q == 0:
                for copy in heavy[4:]:
                    copy.wait()
            else:
                for copy in leave(q - 1)[4:]:
                    copy.wait()
            puts = [put_of(ranks_t, 2 * q + i, capacity) for i in range(2)]
            scales = [weights_t[:, 2 * q + i : 2 * q + i + 1] for i in range(2)]

            def tile(cols):
                value = dot(units[...], down_w[:, cols]).astype(low)
                out[:, cols] = value
                for i in range(2):
                    part = dot(puts[i], value[i * capacity : (i + 1) * capacity]) * scales[i]
                    mix[i, :, cols] = part.astype(low)

            each_tile(width, 256, tile)
            for copy in leave(q)[4:]:
                copy.start()

        def closing():
            for copy in leave(pairs - 1):
                copy.wait()

        listed = [opening]
        for q in range(pairs):
            listed += [functools.partial(f, q) for f in (choose, widen, narrow)]
        return listed + [closing]

    return Beside(
        ins=tuple(halves),
        in_specs=(ANYWHERE,) * 6,
        outs=[
            jax.ShapeDtypeStruct((slots, width), low),
            jax.ShapeDtypeStruct((slots, hidden), full),
            jax.ShapeDtypeStruct((slots, hidden), full),
            jax.ShapeDtypeStruct((slots, hidden), low),
            jax.ShapeDtypeStruct((slots, width), low),
            jax.ShapeDtypeStruct((row_count, tokens, width), low),
        ],
        scratch=[
            pltpu.VMEM((width, hidden), low),
            pltpu.VMEM((width, hidden), low),
            pltpu.VMEM((hidden, width), low),
            pltpu.VMEM((2, 2, tokens, width), low),
            pltpu.VMEM((pair, width), low),
            pltpu.VMEM((2, pair, hidden), full),
            pltpu.VMEM((pair, hidden), low),
            pltpu.VMEM((pair, width), low),
            pltpu.VMEM((2, tokens, width), low),
            pltpu.SemaphoreType.DMA((6,)),
            pltpu.SemaphoreType.DMA((2,)),
            pltpu.SemaphoreType.DMA((6,)),
            pltpu.VMEM(aside_shape, full),
            pltpu.VMEM((row_count, tokens), full),
            pltpu.VMEM((tokens, row_count), full),
            pltpu.VMEM((tokens, row_count), full),
            pltpu.SemaphoreType.DMA,
        ],
        steps=steps,
        lead=0,
        span=0.6,
    )


def backward_beside(cot_early, cot_late, rank_rows, rank_cols, weight_rows, gate_pre, up_pre, expert_out, halves, capacity):
    row_count, late, width = cot_late.shape
    early = cot_early.shape[1]
    tokens = early + late
    hidden = 2 * halves[0].shape[1]
    pairs, pair = row_count // 2, 2 * capacity
    slots = row_count * capacity
    low, full = jnp.bfloat16, jnp.float32

    def steps(ins, outs, scratch, arrivals):
        early_in, late_in, ranks, ranks_t, weights, gate_in, up_in, out_in = ins[:8]
        heavy_refs, (cot, ge, pre, out, gg, gu, gx, dots, sums), sems = scratch[:3], scratch[3:12], scratch[12:]
        load_sem, row_sem, out_sem = sems
        heavy = weight_copies(ins[8:], heavy_refs, load_sem)
        gate_w, up_w, down_w = heavy_refs

        first = lax.axis_index("dp") * row_count

        def load(q):
            held = cot.at[q % 2]
            return [
                Move(early_in.at[pl.ds(first + 2 * q, 2)], held.at[:, pl.ds(0, early)], row_sem.at[q % 2]),
                Move(late_in.at[pl.ds(2 * q, 2)], held.at[:, pl.ds(early, late)], row_sem.at[5 + q % 2]),
            ]

        def fetch(q):
            here = pl.ds(q * pair, pair)
            moves = [(out_in, out), (gate_in, pre.at[0]), (up_in, pre.at[1])]
            return [Move(a.at[here], b, row_sem.at[2 + i]) for i, (a, b) in enumerate(moves)]

        def leave(q):
            here = pl.ds(q * pair, pair)
            moves = [(ge, outs[0].at[here]), (gg, outs[1].at[here]), (gu, outs[2].at[here])]
            moves.append((gx, outs[3].at[pl.ds(2 * q, 2)]))
            return [Move(a, b, out_sem.at[i]) for i, (a, b) in enumerate(moves)]

        last = Move(dots, outs[4], out_sem.at[4])

        def opening():
            for copy in load(0):
                copy.start()
            for copy in fetch(0):
                copy.start()
            for copy in heavy:
                copy.start()

        def choose(q):
            for copy in load(q):
                copy.wait()
            fetch(q)[0].wait()
            if q + 1 < pairs:
                for copy in load(q + 1):
                    copy.start()
            if q:
                leave(q - 1)[0].wait()
            for i in range(2):
                row = 2 * q + i
                pick = pick_of(ranks, row, capacity)
                pick_low = pick.astype(full).astype(low)
                scale = jnp.sum(jnp.where(pick, weights[row : row + 1, :], 0.0), axis=1, keepdims=True)
                rows = pl.ds(i * capacity, capacity)
                sums[...] = jnp.zeros_like(sums)

                def tile(cols, i=i, pick_low=pick_low, scale=scale, rows=rows):
                    value = dot(pick_low, cot[q % 2, i, :, cols])
                    ge[rows, cols] = (value * scale).astype(low)
                    product = value * out[rows, cols].astype(full)
                    total = product[:, :128]
                    for lane in range(128, product.shape[1], 128):
                        total = total + product[:, lane : lane + 128]
                    sums[...] += total

                each_tile(width, 512, tile)
                slot_dot = jnp.sum(sums[...], axis=1, keepdims=True)
                dots[row : row + 1, :] = jnp.sum(jnp.where(pick, slot_dot, 0.0), axis=0, keepdims=True)
            leave(q)[0].start()
            if q + 1 < pairs:
                fetch(q + 1)[0].start()

        def narrow(q):
            for copy in fetch(q)[1:]:
                copy.wait()
            if q == 0:
                for copy in heavy:
                    copy.wait()
            else:
                for copy in leave(q - 1)[1:3]:
                    copy.wait()

            def tile(cols):
                grad = dot_across(ge[...], down_w[cols, :])
                gate, up = pre[0, :, cols], pre[1, :, cols]
                sigmoid = jax.nn.sigmoid(gate)
                gg[:, cols] = (grad * up * sigmoid * (1.0 + gate * (1.0 - sigmoid))).astype(low)
                gu[:, cols] = (grad * gate * sigmoid).astype(low)

            each_tile(hidden, 256, tile)
            for copy in leave(q)[1:3]:
                copy.start()
            if q + 1 < pairs:
                for copy in fetch(q + 1)[1:]:
                    copy.start()

        def widen(q):
            if q:
                leave(q - 1)[3].wait()
            puts = [put_of(ranks_t, 2 * q + i, capacity) for i in range(2)]

            def tile(cols):
                value = dot_across(gg[...], gate_w[cols, :]) + dot_across(gu[...], up_w[cols, :])
                value = value.astype(low)
                for i in range(2):
                    part = dot(puts[i], value[i * capacity : (i + 1) * capacity])
                    gx[i, :, cols] = part.astype(low)

            each_tile(width, 256, tile)
            leave(q)[3].start()

        def closing():
            last.start()
            for copy in leave(pairs - 1):
                copy.wait()
            last.wait()

        listed = [opening]
        for q in range(pairs):
            listed += [functools.partial(f, q) for f in (choose, narrow, widen)]
        return listed + [closing]

    return Beside(
        ins=(cot_early, cot_late, rank_rows, rank_cols, weight_rows, gate_pre, up_pre, expert_out) + tuple(halves),
        in_specs=(ANYWHERE, ANYWHERE, ON_CORE, ON_CORE, ON_CORE) + (ANYWHERE,) * 9,
        outs=[
            jax.ShapeDtypeStruct((slots, width), low),
            jax.ShapeDtypeStruct((slots, hidden), low),
            jax.ShapeDtypeStruct((slots, hidden), low),
            jax.ShapeDtypeStruct((row_count, tokens, width), low),
            jax.ShapeDtypeStruct((row_count, tokens), full),
        ],
        scratch=[
            pltpu.VMEM((width, hidden), low),
            pltpu.VMEM((width, hidden), low),
            pltpu.VMEM((hidden, width), low),
            pltpu.VMEM((2, 2, tokens, width), low),
            pltpu.VMEM((pair, width), low),
            pltpu.VMEM((2, pair, hidden), full),
            pltpu.VMEM((pair, width), low),
            pltpu.VMEM((pair, hidden), low),
            pltpu.VMEM((pair, hidden), low),
            pltpu.VMEM((2, tokens, width), low),
            pltpu.VMEM((row_count, tokens), full),
            pltpu.VMEM((capacity, 128), full),
            pltpu.SemaphoreType.DMA((6,)),
            pltpu.SemaphoreType.DMA((7,)),
            pltpu.SemaphoreType.DMA((5,)),
        ],
        steps=steps,
        lead=0,
        span=0.8,
    )


def outer_beside(rows_in, grad_rows, grad_gate, grad_up, units):
    slots, width = rows_in.shape
    hidden = units.shape[1]
    half = hidden // 2
    block = 256
    low, full = jnp.bfloat16, jnp.float32

    def steps(ins, outs, scratch, arrivals):
        rows_ref, grads_ref, gate_ref, up_ref, units_ref = ins
        left, turned, gate, up, grads, wide_own, wide_far, tall_own, tall_far, load_sem, left_sem, out_sem = scratch
        heavy = [
            Move(a, b, load_sem.at[i])
            for i, (a, b) in enumerate([(gate_ref, gate), (up_ref, up), (grads_ref, grads)])
        ]
        jobs = [(rows_ref, t) for t in range(width // block)] + [
            (units_ref, t) for t in range(hidden // block)
        ]

        def load(n):
            ref, t = jobs[n]
            return Move(
                ref.at[:, pl.ds(t * block, block)], left.at[n % 2], left_sem.at[n % 2]
            )

        def turn(n):
            load(n).wait()
            if n + 1 < len(jobs):
                load(n + 1).start()

            @pl.loop(0, slots // block)
            def _(k):
                here = pl.ds(pl.multiple_of(k * block, block), block)
                turned[:, here] = left[n % 2, here, :].astype(full).T.astype(low)

        def leave_wide(which, t):
            here = pl.ds(t * block, block)
            return [
                Move(wide_own.at[which], outs[2 * which].at[here], out_sem.at[2 * which]),
                Move(wide_far.at[which], outs[2 * which + 1].at[here], out_sem.at[2 * which + 1]),
            ]

        def leave_tall(t):
            far = t * block >= half
            here = pl.ds(t * block - (half if far else 0), block)
            return Move(
                tall_far if far else tall_own, outs[5 if far else 4].at[here], out_sem.at[5 if far else 4]
            )

        def wide(which, t):
            right = (gate, up)[which]
            if t == 0:
                heavy[which].wait()
            else:
                for copy in leave_wide(which, t - 1):
                    copy.wait()

            def own(cols):
                wide_own[which, :, cols] = dot(turned[...], right[:, cols])

            each_tile(half, 256, own)

            @pl.loop(0, half // 256)
            def _(k):
                cols = pl.ds(pl.multiple_of(k * 256, 256), 256)
                there = pl.ds(pl.multiple_of(half + k * 256, 256), 256)
                wide_far[which, :, cols] = dot(turned[...], right[:, there]).astype(low)

            for copy in leave_wide(which, t):
                copy.start()

        def tall(t):
            far = t * block >= half
            if t == 0:
                heavy[2].wait()
            if t * block not in (0, half):
                leave_tall(t - 1).wait()

            def tile(cols):
                value = dot(turned[...], grads[:, cols])
                if far:
                    tall_far[:, cols] = value.astype(low)
                else:
                    tall_own[:, cols] = value

            each_tile(width, 256, tile)
            leave_tall(t).start()

        def opening():
            load(0).start()
            for copy in heavy:
                copy.start()

        def closing():
            for which in range(2):
                for copy in leave_wide(which, width // block - 1):
                    copy.wait()
            leave_tall(half // block - 1).wait()
            leave_tall(hidden // block - 1).wait()

        listed = [opening]
        for n, (ref, t) in enumerate(jobs):
            listed.append(functools.partial(turn, n))
            if n < width // block:
                listed += [functools.partial(wide, which, t) for which in range(2)]
            else:
                listed.append(functools.partial(tall, t))
        return listed + [closing]

    return Beside(
        ins=(rows_in, grad_rows, grad_gate, grad_up, units),
        in_specs=(ANYWHERE,) * 5,
        outs=[
            jax.ShapeDtypeStruct((width, half), full),
            jax.ShapeDtypeStruct((width, half), low),
            jax.ShapeDtypeStruct((width, half), full),
            jax.ShapeDtypeStruct((width, half), low),
            jax.ShapeDtypeStruct((half, width), full),
            jax.ShapeDtypeStruct((half, width), low),
        ],
        scratch=[
            pltpu.VMEM((2, slots, block), low),
            pltpu.VMEM((block, slots), low),
            pltpu.VMEM((slots, hidden), low),
            pltpu.VMEM((slots, hidden), low),
            pltpu.VMEM((slots, width), low),
            pltpu.VMEM((2, block, half), full),
            pltpu.VMEM((2, block, half), low),
            pltpu.VMEM((block, width), full),
            pltpu.VMEM((block, width), low),
            pltpu.SemaphoreType.DMA((3,)),
            pltpu.SemaphoreType.DMA((2,)),
            pltpu.SemaphoreType.DMA((6,)),
        ],
        steps=steps,
        lead=0,
        span=0.6,
    )


def turn_half(values):
    return pltpu.roll(values, values.shape[1] // 2, 1)


def attend_beside(tokens, weight_rows, gain_column, live_row, cosine, sine):
    row_count, width = tokens.shape
    low, full = jnp.bfloat16, jnp.float32
    block, group, strip = 256, 2, 32
    tiles, per_part = 3 * width // block, width // block
    score_scale = HEAD ** (-0.5)

    def steps(ins, outs, scratch, arrivals):
        tokens_ref, live, cos, sin = ins
        normed, proj, panel, queries, keys, values, mixed, probs, scale, panel_sem, out_sem, probs_sem = scratch[:12]
        small, gains, small_sem = scratch[12:]
        weight = arrivals[0]
        small_copy = Move(arrivals[1], small, small_sem)

        def load(t):
            return Move(weight.at[:, :, pl.ds(t * block, block)], panel.at[t % 3], panel_sem.at[t % 3])

        leaves = [
            Move(ref, outs[i], out_sem.at[i])
            for i, ref in enumerate((normed, proj.at[:, pl.ds(0, 2 * width)], queries, keys, values, mixed))
        ]

        def leave_probs(n):
            return Move(probs.at[n % 2], outs[6].at[pl.ds(n * group, group)], probs_sem.at[n % 2])

        def opening():
            small_copy.start()
            load(0).start()
            load(1).start()
            small_copy.wait()
            blocks = 128 // small.shape[1]
            for k in range(width // 128):
                columns = small[k * blocks : (k + 1) * blocks].astype(full).reshape(128, 128)
                gains[:, k * 128 : (k + 1) * 128] = columns.T[gain_column : gain_column + 8]

            @pl.loop(0, row_count // strip)
            def _(k):
                here = pl.ds(pl.multiple_of(k * strip, strip), strip)
                value = tokens_ref[here, :].astype(full)
                value = value * lax.rsqrt(jnp.mean(value * value, axis=1, keepdims=True) + NORM_EPS)
                normed[here, :] = (value * gains[0:1, :]).astype(low)

            leaves[0].start()

        def project(t):
            load(t).wait()
            if t + 2 < tiles:
                load(t + 2).start()
            proj[:, t * block : (t + 1) * block] = dot(normed[...], panel[t % 3].reshape(width, block))

        def measure(part):
            @pl.loop(0, row_count // strip)
            def _(k):
                here = pl.ds(pl.multiple_of(k * strip, strip), strip)
                value = proj[here, part * width : (part + 1) * width]
                inverse = lax.rsqrt(jnp.mean(value * value, axis=1, keepdims=True) + NORM_EPS)
                scale[part, here, :] = jnp.broadcast_to(inverse, (strip, HEAD))

        def attend(n):
            if n == 0:
                leaves[1].start()
            if n >= 2:
                leave_probs(n - 2).wait()
            query_slot = lax.broadcasted_iota(jnp.int32, (row_count, row_count), 0)
            key_slot = lax.broadcasted_iota(jnp.int32, (row_count, row_count), 1)
            allowed = (key_slot <= query_slot) & (live[...] > 0.5)

            @pl.loop(0, group)
            def _(i):
                head = n * group + i
                cols = pl.ds(pl.multiple_of(head * HEAD, HEAD), HEAD)

                def place(part, gain):
                    there = pl.ds(pl.multiple_of(part * width + head * HEAD, HEAD), HEAD)
                    value = proj[:, there] * scale[part] * gains[gain : gain + 1, cols]
                    return (value * cos[...] + turn_half(value) * sin[...]).astype(low)

                query, key = place(0, 1), place(1, 2)
                value = proj[:, pl.ds(pl.multiple_of(2 * width + head * HEAD, HEAD), HEAD)].astype(low)
                queries[:, cols], keys[:, cols], values[:, cols] = query, key, value
                score = jnp.where(allowed, dot_across(query, key) * score_scale, -1e30)
                expo = jnp.exp(score - jnp.max(score, axis=1, keepdims=True))
                prob = expo / jnp.sum(expo, axis=1, keepdims=True)
                probs[n % 2, i] = prob
                mixed[:, cols] = dot(prob.astype(low), value).astype(low)

            leave_probs(n).start()

        def closing():
            for move in leaves[2:]:
                move.start()
            for move in leaves:
                move.wait()
            for n in range(HEADS // group - 2, HEADS // group):
                leave_probs(n).wait()

        listed = [opening] + [functools.partial(project, t) for t in range(tiles)]
        listed += [functools.partial(measure, 0), functools.partial(measure, 1)]
        return listed + [functools.partial(attend, n) for n in range(HEADS // group)] + [closing]

    shape = (row_count, width)
    return Beside(
        ins=(tokens, live_row, cosine, sine),
        in_specs=(ON_CORE,) * 4,
        outs=[
            jax.ShapeDtypeStruct(shape, low),
            jax.ShapeDtypeStruct((row_count, 2 * width), full),
            jax.ShapeDtypeStruct(shape, low),
            jax.ShapeDtypeStruct(shape, low),
            jax.ShapeDtypeStruct(shape, low),
            jax.ShapeDtypeStruct(shape, low),
            jax.ShapeDtypeStruct((HEADS, row_count, row_count), full),
        ],
        scratch=[
            pltpu.VMEM(shape, low),
            pltpu.VMEM((row_count, 3 * width), full),
            pltpu.VMEM((3, width // weight_rows, weight_rows, block), low),
            pltpu.VMEM(shape, low),
            pltpu.VMEM(shape, low),
            pltpu.VMEM(shape, low),
            pltpu.VMEM(shape, low),
            pltpu.VMEM((2, group, row_count, row_count), full),
            pltpu.VMEM((2, row_count, HEAD), full),
            pltpu.SemaphoreType.DMA((3,)),
            pltpu.SemaphoreType.DMA((6,)),
            pltpu.SemaphoreType.DMA((2,)),
            pltpu.VMEM((width // weight_rows, weight_rows, 128), low),
            pltpu.VMEM((8, width), full),
            pltpu.SemaphoreType.DMA,
        ],
        steps=steps,
        lead=0,
        span=0.6,
    )


def attend_back_beside(grad_attn, out_weight, queries, keys, values, probs, parts, gain_rows, cosine, sine):
    row_count, width = grad_attn.shape
    low, full = jnp.bfloat16, jnp.float32
    block, group, strip = 256, 2, 32
    score_scale = HEAD ** (-0.5)
    across_rows = (((0,), (0,)), ((), ()))

    def steps(ins, outs, scratch, arrivals):
        grad_ref, weight, query_ref, key_ref, value_ref, probs_in, parts_ref, gains, cos, sin = ins
        grad_mixed, grads, panel, prob_ref, projected, sums, panel_sem, probs_sem, out_sem = scratch
        tiles = width // block

        def load(t):
            return Move(weight.at[pl.ds(t * block, block)], panel.at[t % 3], panel_sem.at[t % 3])

        def load_probs(n):
            return Move(probs_in.at[pl.ds(n * group, group)], prob_ref.at[n % 2], probs_sem.at[n % 2])

        leaves = [Move(projected, outs[0], out_sem.at[0]), Move(sums, outs[1], out_sem.at[1])]

        def opening():
            load(0).start()
            load(1).start()
            load_probs(0).start()

        def unmix(t):
            load(t).wait()
            if t + 2 < tiles:
                load(t + 2).start()
            grad_mixed[:, t * block : (t + 1) * block] = dot_across(grad_ref[...], panel[t % 3]).astype(low)

        def attend(n):
            load_probs(n).wait()
            if n + 1 < HEADS // group:
                load_probs(n + 1).start()

            @pl.loop(0, group)
            def _(i):
                head = n * group + i
                cols = pl.ds(pl.multiple_of(head * HEAD, HEAD), HEAD)
                prob, grad = prob_ref[n % 2, i], grad_mixed[:, cols]
                grad_value = lax.dot_general(prob.astype(low), grad, across_rows, preferred_element_type=full)
                there = pl.ds(pl.multiple_of(2 * width + head * HEAD, HEAD), HEAD)
                projected[:, there] = grad_value.astype(low)
                grad_prob = dot_across(grad, value_ref[:, cols])
                centre = jnp.sum(prob * grad_prob, axis=1, keepdims=True)
                grad_score = (prob * (grad_prob - centre)).astype(low)
                grad_query = dot(grad_score, key_ref[:, cols]) * score_scale
                grad_key = lax.dot_general(grad_score, query_ref[:, cols], across_rows, preferred_element_type=full)
                for part, value in enumerate((grad_query, grad_key * score_scale)):
                    grads[part, :, cols] = value * cos[...] - turn_half(value) * sin[...]

        def settle(part):
            sums[part] = jnp.zeros((8, width), full)

            @pl.loop(0, row_count // strip)
            def _(k):
                here = pl.ds(pl.multiple_of(k * strip, strip), strip)
                value = parts_ref[here, part * width : (part + 1) * width]
                inverse = lax.rsqrt(jnp.mean(value * value, axis=1, keepdims=True) + NORM_EPS)
                unit = value * inverse
                grad = grads[part, here, :]
                product = grad * unit
                total = product[0:8]
                for first in range(8, strip, 8):
                    total = total + product[first : first + 8]
                sums[part] += total
                grad = grad * gains[part + 1 : part + 2, :]
                grad = inverse * (grad - unit * jnp.mean(grad * unit, axis=1, keepdims=True))
                projected[here, part * width : (part + 1) * width] = grad.astype(low)

        def closing():
            for move in leaves:
                move.start()
            for move in leaves:
                move.wait()

        listed = [opening] + [functools.partial(unmix, t) for t in range(tiles)]
        listed += [functools.partial(attend, n) for n in range(HEADS // group)]
        return listed + [functools.partial(settle, part) for part in range(2)] + [closing]

    shape = (row_count, width)
    return Beside(
        ins=(grad_attn, out_weight, queries, keys, values, probs, parts, gain_rows, cosine, sine),
        in_specs=(ON_CORE, ANYWHERE, ON_CORE, ON_CORE, ON_CORE, ANYWHERE, ON_CORE, ON_CORE, ON_CORE, ON_CORE),
        outs=[
            jax.ShapeDtypeStruct((row_count, 3 * width), low),
            jax.ShapeDtypeStruct((2, 8, width), full),
        ],
        scratch=[
            pltpu.VMEM(shape, low),
            pltpu.VMEM((2,) + shape, full),
            pltpu.VMEM((3, block, width), low),
            pltpu.VMEM((2, group, row_count, row_count), full),
            pltpu.VMEM((row_count, 3 * width), low),
            pltpu.VMEM((2, 8, width), full),
            pltpu.SemaphoreType.DMA((3,)),
            pltpu.SemaphoreType.DMA((2,)),
            pltpu.SemaphoreType.DMA((2,)),
        ],
        steps=steps,
    )


def alone(beside):
    def kernel(*refs):
        a, b = len(beside.ins), len(beside.ins) + len(beside.outs)
        for step in beside.steps(refs[:a], refs[a:b], refs[b:], ()):
            step()

    return pl.pallas_call(
        kernel,
        out_shape=beside.outs,
        in_specs=list(beside.in_specs),
        out_specs=[ANYWHERE] * len(beside.outs),
        scratch_shapes=list(beside.scratch),
        compiler_params=pltpu.CompilerParams(vmem_limit_bytes=48 << 20),
    )(*beside.ins)


DEEP = 4


def total_beside(pairs):
    low, full = jnp.bfloat16, jnp.float32
    jobs, shapes = [], []
    for n, (own, _) in enumerate(pairs):
        rows = own.shape[0] // 8
        shape = (rows, own.shape[1])
        if shape not in shapes:
            shapes.append(shape)
        jobs += [(n, k, shapes.index(shape)) for k in range(8)]

    def steps(ins, outs, scratch, arrivals):
        count = len(shapes)
        owns, fars, sums = scratch[:count], scratch[count : 2 * count], scratch[2 * count : 3 * count]
        in_sem, out_sem = scratch[3 * count :]

        def load(m):
            n, k, s = jobs[m]
            here = pl.ds(k * shapes[s][0], shapes[s][0])
            return [
                Move(ins[2 * n].at[here], owns[s].at[m % DEEP], in_sem.at[m % DEEP, 0]),
                Move(ins[2 * n + 1].at[here], fars[s].at[m % DEEP], in_sem.at[m % DEEP, 1]),
            ]

        def leave(m):
            n, k, s = jobs[m]
            here = pl.ds(k * shapes[s][0], shapes[s][0])
            return Move(sums[s].at[m % DEEP], outs[n].at[here], out_sem.at[m % DEEP])

        def opening():
            for m in range(DEEP - 1):
                for move in load(m):
                    move.start()

        def add(m):
            for move in load(m):
                move.wait()
            if m + DEEP - 1 < len(jobs):
                for move in load(m + DEEP - 1):
                    move.start()
            if m >= DEEP:
                leave(m - DEEP).wait()
            s = jobs[m][2]
            sums[s][m % DEEP] = owns[s][m % DEEP] + fars[s][m % DEEP].astype(full)
            leave(m).start()

        def closing():
            for m in range(len(jobs) - DEEP, len(jobs)):
                leave(m).wait()

        return [opening] + [functools.partial(add, m) for m in range(len(jobs))] + [closing]

    return Beside(
        ins=[x for pair in pairs for x in pair],
        in_specs=(ANYWHERE,) * (2 * len(pairs)),
        outs=[jax.ShapeDtypeStruct(own.shape, full) for own, _ in pairs],
        scratch=[pltpu.VMEM((DEEP,) + shape, full) for shape in shapes]
        + [pltpu.VMEM((DEEP,) + shape, low) for shape in shapes]
        + [pltpu.VMEM((DEEP,) + shape, full) for shape in shapes]
        + [pltpu.SemaphoreType.DMA((DEEP, 2)), pltpu.SemaphoreType.DMA((DEEP,))],
        steps=steps,
    )


def together(first, second):
    cuts = [(len(getattr(first, kind)), len(getattr(second, kind))) for kind in ("ins", "outs", "scratch")]

    def steps(ins, outs, scratch, arrivals):
        groups = [(refs[:a], refs[a:]) for refs, (a, _) in zip((ins, outs, scratch), cuts)]
        left = first.steps(*(group[0] for group in groups), arrivals)
        right = second.steps(*(group[1] for group in groups), arrivals)
        listed, done = [], 0
        for n, step in enumerate(left):
            listed.append(step)
            until = (n + 1) * len(right) // len(left)
            listed += right[done:until]
            done = until
        return listed

    return Beside(
        ins=list(first.ins) + list(second.ins),
        in_specs=list(first.in_specs) + list(second.in_specs),
        outs=list(first.outs) + list(second.outs),
        scratch=list(first.scratch) + list(second.scratch),
        steps=steps,
    )


WEIGHTS_LAG = 0.9
ROWS_LAG = 0.95


def gathered_body(
    dims,
    tokens,
    w_qkv,
    w_out,
    w_router,
    gains,
    w_gate,
    w_up,
    w_down,
    lengths,
    routes,
    send_counts,
    cotangent,
):
    row_count = tokens.shape[1]
    top_count = routes.shape[2]
    expert_count = w_router.shape[1]
    owners = math.prod(dims)
    weight_rows = w_qkv.shape[0]
    capacity = row_count * top_count // expert_count
    slots_all = row_count * 2 * owners
    balance_factor = float(expert_count) / (float(top_count) * float(slots_all) * float(slots_all))
    low = jnp.bfloat16
    full = jnp.float32
    chips = Grid(dims)
    devices = Grid(dims, cores=True)
    z, y, x = 0, 1, 2
    row_orders = [(x, z, y), (y, z, x), (z, x, y), (z, y, x)]
    row_shares = [5 * row_count // 16, 5 * row_count // 16, 3 * row_count // 16, 3 * row_count // 16]
    quarter = [weight_rows // 4] * 4
    wide_orders = [tuple(d + 1 for d in order) + (0,) for order in row_orders]
    late_shares = [row_count // 4, row_count // 4, row_count // 8, row_count // 8]
    narrow_orders = [order[:-1] for order in wide_orders]
    expert = lax.axis_index("expert")
    core = lax.axis_index("dp")
    swap = [(0, 1), (1, 0)]

    small = jnp.concatenate(
        [w_router, gains.T, jnp.zeros((weight_rows, 128 - expert_count - 4), low)], axis=1
    )
    gate_own, up_own, down_own = w_gate[0], w_up[0], w_down[0]
    gate_far, up_far, down_far = (lax.ppermute(w, "dp", swap) for w in (gate_own, up_own, down_own))

    positions = jnp.arange(row_count, dtype=jnp.int32)
    live_slots = positions < lengths[0]
    live_float = live_slots.astype(full)[:, None]
    expert_ids = jnp.arange(expert_count, dtype=jnp.int32)
    named = jnp.any(routes[0][:, :, None] == expert_ids, axis=1) & live_slots[:, None]
    before = (positions[None, :] < positions[:, None]).astype(low)
    rank = jnp.dot(before, named.astype(low), preferred_element_type=full)
    limit = jnp.minimum(send_counts[0], capacity).astype(full)
    kept = named & (rank < limit[None, :])
    kept_rank = jnp.where(kept, rank, -1.0)

    cosine, sine = (table[:, 0] for table in rope_tables(row_count, HEAD))
    sine = jnp.concatenate([-sine[:, : HEAD // 2], sine[:, HEAD // 2 :]], axis=1)
    early = row_count // 4
    first_parts = cut(0, quarter, wide_orders) + cut(1, [weight_rows], wide_orders[2:3])
    later_parts = cut(2, quarter, wide_orders) + cut(3, [early // 4] * 4, narrow_orders)
    qkv_all, small_all, out_all, cot_early, normed, qk_parts, queries, keys_low, values_low, mixed_low, probs = gather(
        [w_qkv, small, w_out, cotangent[0, :early]],
        devices,
        first_parts + later_parts,
        1,
        attend_beside(tokens[0], weight_rows, expert_count, live_slots[None, :].astype(full), cosine, sine),
        (0,) * len(first_parts) + (WEIGHTS_LAG,) * len(later_parts),
    )
    small_all = small_all.reshape(D, 128)
    router_weight = small_all[:, :expert_count]
    gain_float = small_all[:, expert_count : expert_count + 4].T.astype(full)
    qkv_weight = qkv_all.reshape(D, 3 * D)
    out_weight = out_all.reshape(D, D)
    inputs = tokens[0].astype(full)
    _, attn_norm_back = jax.vjp(norm_scale, inputs, gain_float[0])
    hidden_state = inputs + jnp.dot(mixed_low, out_weight, preferred_element_type=full)
    ffn_in, ffn_norm_back = jax.vjp(norm_scale, hidden_state, gain_float[3])
    ffn_low = ffn_in.astype(low)
    logits = jnp.dot(ffn_low, router_weight, preferred_element_type=full)
    router_probs = jax.nn.softmax(logits, axis=-1)
    prob_local = jnp.sum(router_probs * live_float, axis=0)
    sums = jnp.concatenate([send_counts[0].astype(full), prob_local])
    aside = jnp.concatenate(
        [
            jnp.where(kept, router_probs, 0.0).T,
            kept_rank.T,
            jnp.pad(sums[None, :], ((0, 7), (0, row_count - 2 * expert_count))),
        ],
        axis=0,
    )

    halves = (gate_own, gate_far, up_own, up_far, down_own, down_far)
    first_parts = cut(0, row_shares, row_orders) + cut(1, [aside.shape[0]], row_orders[2:3])
    later_parts = cut(2, late_shares, row_orders)
    _, aside_rows, cot_late, rows_in, gate_pre, up_pre, units, expert_out, mixture_part = gather(
        [ffn_low, aside, cotangent[0, early:]],
        chips,
        first_parts + later_parts,
        2,
        forward_beside((owners, row_count, D), (owners,) + aside.shape, halves, capacity),
        (0,) * len(first_parts) + (ROWS_LAG,) * len(later_parts),
    )
    sums_core = jnp.sum(aside_rows[:, 2 * expert_count, : 2 * expert_count], axis=0)
    sums_all = sums_core + lax.ppermute(sums_core, "dp", swap)
    count_total, prob_total = sums_all[:expert_count], sums_all[expert_count:]
    balance = jnp.sum(count_total * prob_total) * balance_factor
    weight_of = lax.dynamic_index_in_dim(aside_rows, expert, 1, keepdims=False)
    rank_of = lax.dynamic_index_in_dim(aside_rows, expert_count + expert, 1, keepdims=False)
    mixture, grad_rows, grad_gate, grad_up, back_part, dot_route = scatter(
        [mixture_part],
        chips,
        cut(0, row_shares, row_orders),
        5,
        backward_beside(
            cot_early, cot_late, rank_of, rank_of.T, weight_of, gate_pre, up_pre, expert_out, halves, capacity
        ),
    )
    route_part = jnp.where((expert_ids == expert)[None, :, None], dot_route[:, None, :], 0.0)
    grad_ffn, grad_route, *halves_grads = scatter(
        [back_part, route_part],
        chips,
        cut(0, row_shares, row_orders) + cut(1, [expert_count], row_orders[2:3]),
        4,
        outer_beside(rows_in, grad_rows, grad_gate, grad_up, units),
    )
    far_grads = [lax.ppermute(far, "dp", swap) for far in halves_grads[1::2]]
    result = (live_float * (hidden_state + mixture)).astype(low)[None]

    balance_coef = BALANCE_WEIGHT * balance_factor
    grad_probs = grad_route.T + balance_coef * count_total[None, :] * live_float
    grad_logits = router_probs * (
        grad_probs - jnp.sum(router_probs * grad_probs, axis=-1, keepdims=True)
    )
    grad_logits_low = grad_logits.astype(low)
    grad_ffn = grad_ffn + jnp.einsum("te,de->td", grad_logits_low, router_weight, preferred_element_type=full)
    grad_router_w = jnp.einsum("td,te->de", ffn_low, grad_logits_low, preferred_element_type=full)

    grad_layer = cotangent[0].astype(full) * live_float
    grad_hidden_part, grad_gain_ffn = ffn_norm_back(grad_ffn)
    grad_hidden_state = grad_layer + grad_hidden_part
    grad_attn_low = grad_hidden_state.astype(low)
    grad_projected, head_sums, *expert_grads = alone(
        together(
            attend_back_beside(
                grad_attn_low, out_weight, queries, keys_low, values_low, probs, qk_parts, gain_float, cosine, sine
            ),
            total_beside(list(zip(halves_grads[::2], far_grads))),
        )
    )
    grad_gain_query, grad_gain_key = jnp.sum(head_sums, axis=1)
    grad_normed = jnp.einsum("te,de->td", grad_projected, qkv_weight, preferred_element_type=full)
    grad_input_part, grad_gain_attn = attn_norm_back(grad_normed)
    grad_inputs = grad_hidden_state + grad_input_part
    grad_gain_rows = jnp.stack([grad_gain_attn, grad_gain_query, grad_gain_key, grad_gain_ffn])

    def outer(left, right):
        return jnp.einsum("sa,sb->ab", left, right, preferred_element_type=full)

    small_grads = jnp.concatenate(
        [grad_router_w, grad_gain_rows.T, jnp.zeros((D, 128 - expert_count - 4), full)], axis=1
    )
    shares = [
        g.reshape(devices.size, weight_rows, g.shape[1])
        for g in (outer(normed, grad_projected).astype(low), outer(mixed_low, grad_attn_low).astype(low), small_grads)
    ]
    grad_qkv, grad_out, grad_small = scatter(
        shares,
        devices,
        cut(0, quarter, wide_orders)
        + cut(1, [weight_rows // 2] * 2, wide_orders[:2])
        + cut(2, [weight_rows], wide_orders[2:3]),
        6,
    )
    return (
        result,
        grad_inputs[None],
        grad_qkv,
        grad_out,
        grad_small[:, :expert_count],
        grad_small[:, expert_count : expert_count + 4].T,
        *(g[None] for g in expert_grads),
        balance,
    )


def solution(mesh):
    dims = {4: (1, 2, 2), 8: (2, 2, 2), 16: (4, 2, 2)}.get(mesh.shape["expert"])
    plan = routed_body if dims is None or mesh.shape["dp"] != 2 else functools.partial(gathered_body, dims)
    placed = (
        P(("dp", "expert"), None, None),
        P(("dp", "expert"), None),
        P(("dp", "expert"), None),
        P(("dp", "expert"), None),
        P(None, ("dp", "expert")),
        P("expert", None, "dp"),
        P("expert", None, "dp"),
        P("expert", "dp", None),
        P(("dp", "expert")),
        P(("dp", "expert"), None, None),
        P(("dp", "expert"), None),
        P(("dp", "expert"), None, None),
    )
    return jax.shard_map(
        plan,
        mesh=mesh,
        in_specs=placed,
        out_specs=(
            P(("dp", "expert"), None, None),
            P(("dp", "expert"), None, None),
            P(("dp", "expert"), None),
            P(("dp", "expert"), None),
            P(("dp", "expert"), None),
            P(None, ("dp", "expert")),
            P("expert", None, "dp"),
            P("expert", None, "dp"),
            P("expert", "dp", None),
            P(),
        ),
        check_vma=False,
    )
```
